32 devices in a mesh: groups: 2 (over x), expert: 8 (over z, y), dp: 2 (over core).
Axes of the slice: x: 2, y: 2, z: 4, core: 2. Of those that a mesh axis runs over, the one named last changes fastest.
Arguments:
- tokens: bfloat16 [1024, 3584], P(('groups', 'expert', 'dp')), parts along dimension 0, may hold values from -6 to 6
- cotangent: bfloat16 [1024, 3584], P(('groups', 'expert', 'dp')), parts along dimension 0, may hold values from -60 to 60
- expert_choice_index: int32 [1024, 8], P(('groups', 'expert', 'dp')), parts along dimension 0, may hold values from 0 to 15, all different within a row; in each aligned block of 32 rows (0 to 31, 32 to 63, ...) at most 16 rows name the same one
- capacity: int32 [32], P(('groups', 'expert', 'dp')), parts along dimension 0, may hold values from 128 to 384, as said below
- router_matrix: bfloat16 [3584, 16], replicated, may hold values from -0.09375 to 0.09375
- gate_matrix: bfloat16 [16, 3584, 1024], P(('expert', 'dp')), may hold values from -0.09375 to 0.09375
- up_matrix: bfloat16 [16, 3584, 1024], P(('expert', 'dp')), may hold values from -0.09375 to 0.09375
- down_matrix: bfloat16 [16, 1024, 3584], P(('expert', 'dp')), may hold values from -0.1875 to 0.1875
- up_adapter_first: bfloat16 [16, 3584, 64], P(('expert', 'dp')), may hold values from -0.09375 to 0.09375
- up_adapter_second: bfloat16 [16, 64, 1024], P(('expert', 'dp')), may hold values from -0.75 to 0.75
- down_adapter_first: bfloat16 [16, 1024, 64], P(('expert', 'dp')), may hold values from -0.1875 to 0.1875
- down_adapter_second: bfloat16 [16, 64, 3584], P(('expert', 'dp')), may hold values from -0.75 to 0.75
Outputs:
- mixed: bfloat16 [1024, 3584], P(('groups', 'expert', 'dp')), parts along dimension 0
- input_grad: bfloat16 [1024, 3584], P(('groups', 'expert', 'dp')), parts along dimension 0
- router_grad: float32 [7168, 16], P('groups'), parts along dimension 0
- grad_up_a: bfloat16 [32, 3584, 64], P(('groups', 'expert', 'dp')), parts along dimension 0
- grad_up_b: bfloat16 [32, 64, 1024], P(('groups', 'expert', 'dp')), parts along dimension 0
- grad_down_a: bfloat16 [32, 1024, 64], P(('groups', 'expert', 'dp')), parts along dimension 0
- grad_down_b: bfloat16 [32, 64, 3584], P(('groups', 'expert', 'dp')), parts along dimension 0
The draws below stay inside these ranges and needn't reach their ends.
There are 2 independent parts, one for each index of `groups`. The reference program is written for one: setup_inputs(seed, part) draws one part's arguments, and reference() takes and returns one part's arrays. A program takes and returns all parts, laid end to end along the dimension named above; an argument that names none is the same for every part. Nothing has to cross between parts.
Inputs may be any that keep to these rules, and one draw needn't show every extreme that they name: `expert_choice_index`: each token names 8 different experts. Among the tokens of one device no expert is named more than 16 times, a bound that some block reaches. Some expert has capacity exactly 384.
All inputs are finite; a program needn't handle non-finite values.
Results may differ from the reference program's by a relative error of at most 0.015.
Values may be sent and summed in bfloat16 or wider, within the bound.
No kernel may reach another device: no remote copies, remote signals or barrier semaphores. Data moves between devices by JAX's collectives and lax.ppermute only.
A program may use at most 128 MiB of HBM per device.

```python
import math
import jax
import jax.numpy as jnp
import numpy as np
from jax import lax

MODEL_WIDTH = 3584
HIDDEN_UNITS = 1024
ADAPTER_RANK = 64
TOPK = 8
TOK_DEV = 32
EXPERT_COUNT = 16
TOKENS = 512
MOST = 16
CAPMIN = 128
CAPMAX = 384


def draw_capacity(key, part):
    key = jax.random.fold_in(key, 11)
    key_values, key_widest = jax.random.split(key)
    values = jax.random.randint(key_values, (EXPERT_COUNT,), CAPMIN, CAPMAX + 1)
    widest = jax.random.randint(key_widest, (), 0, EXPERT_COUNT)
    return jnp.where(jnp.arange(EXPERT_COUNT) == widest, CAPMAX, values).astype(jnp.int32)


def draw_cotangent(key, part):
    key = jax.random.fold_in(key, 23)
    key_entries, key_scale = jax.random.split(key, 2)
    row_ramp = jnp.arange(TOKENS, dtype=jnp.float32) / TOKENS
    entries = jax.random.truncated_normal(key_entries, -4.0, 4.0, (TOKENS, MODEL_WIDTH), jnp.float32)
    ramp_log = math.log(3.0)
    row_scale = jnp.exp(ramp_log * row_ramp + jax.random.uniform(key_scale, (TOKENS,), jnp.float32, 0.0, math.log(4.0)))
    return (entries * row_scale[:, None]).astype(jnp.bfloat16)


def block_scale(own_key, extent, pieces, least, top_value):
    factor_of, own = 1.0, jax.random.fold_in(own_key, 6)
    for position, shards_of in pieces:
        steps = jnp.exp(jax.random.uniform(jax.random.fold_in(own, position), (shards_of,), jnp.float32, least / len(pieces), top_value / len(pieces)))
        factor_of = factor_of * jnp.repeat(steps, extent[position] // shards_of).reshape([-1 if axis == position else 1 for axis in range(len(extent))])
    return factor_of


def shared_out(key, own, number, rows, number_of, top, bound, skew):
    ranking = jax.random.permutation(key, number_of)
    heavy_load, usual = portions_of(number_of, rows * top, bound, skew, True), portions_of(number_of, rows * top, bound, skew, False)
    places = jnp.arange(number_of)

    def named(lengths, rotation):
        used = int((lengths > 0).sum())
        fixed = max(1, used // 4)
        passed = fixed + (places - fixed + rotation * (used - fixed)) % max(1, number_of - fixed)
        return jnp.zeros((number_of,), jnp.int32).at[ranking[jnp.where(places < fixed, places, passed)]].set(jnp.asarray(lengths, jnp.int32))

    lengths = jnp.where(number % 4 == 0, named(heavy_load, number // 4), named(usual, number - number // 4 - 1))
    mixed = jax.random.permutation(jax.random.fold_in(own, 3), number_of)
    donor, receiver = mixed[0:number_of // 2 * 2:2], mixed[1:number_of // 2 * 2:2]
    room = jnp.minimum(lengths[donor] - 1, bound - lengths[receiver]) // 2
    room = jnp.where((donor == ranking[0]) | (receiver == ranking[0]) | (lengths[receiver] == 0), 0, jnp.maximum(room, 0))
    passed = jax.random.randint(jax.random.fold_in(own, 4), (number_of // 2,), 0, 1 << 20) % (room + 1)
    lengths = lengths.at[donor].add(-passed).at[receiver].add(passed)
    members = jnp.searchsorted(jnp.cumsum(lengths), jnp.arange(rows * top), side="right").astype(jnp.int32)
    listing = members.reshape(top, rows).T
    listing = listing[jax.random.permutation(jax.random.fold_in(own, 1), rows)]
    rotation = jax.random.randint(jax.random.fold_in(own, 2), (rows, 1), 0, top)
    return jnp.take_along_axis(listing, (jnp.arange(top)[None, :] + rotation) % top, axis=1)


def portions_of(number_of, total, most, lean, full):
    weights = [(1 << 20) // math.isqrt(standing ** lean) + 1 for standing in range(1, number_of + 1)]
    largest = most if full else min(most, max(-(-total // number_of), total * weights[0] // sum(weights)))
    least = 1 if total - largest >= number_of - 1 else 0
    holding, spare = [largest] + [least] * (number_of - 1), total - largest - least * (number_of - 1)
    while spare > 0:
        candidates = [i for i in range(1, number_of) if holding[i] < largest] or [i for i in range(1, number_of) if holding[i] < most]
        pool, remaining = sum([weights[i] for i in candidates]), spare
        for i in candidates:
            extra = min(most - holding[i], max(1, remaining * weights[i] // pool), spare)
            holding[i] = holding[i] + extra
            spare = spare - extra
    return np.array(holding)


def centred(own_key, dims, spread, bound, shards=(), kind=jnp.bfloat16):
    values = jax.random.normal(own_key, dims, jnp.float32) * spread
    if len(shards) > 0:
        values = block_scale(own_key, dims, shards, -0.22, 0.18) * values
    return jnp.clip(values, min=-bound, max=bound).astype(kind)


def setup_inputs(seed: int = 0, part: int = 0) -> dict:
    keys = jax.random.split(jax.random.key(seed), 13)
    own_keys = jax.random.split(jax.random.fold_in(keys[12], part), 13)
    tokens = centred(own_keys[0], (TOKENS, MODEL_WIDTH), 1.0, 6.0, ((0, 16),))
    cotangent = draw_cotangent(jax.random.fold_in(jax.random.fold_in(keys[12], part), 71), part)
    expert_choice_index_keys = jax.random.split(jax.random.fold_in(own_keys[2], 1), TOKENS // TOK_DEV)
    expert_choice_index_turns = jax.random.permutation(jax.random.fold_in(own_keys[2], 3), TOKENS // TOK_DEV)
    expert_choice_index = jax.vmap(lambda own, number: shared_out(jax.random.fold_in(own_keys[2], 2), own, number, TOK_DEV, EXPERT_COUNT, TOPK, MOST, 2))(expert_choice_index_keys, expert_choice_index_turns).reshape((TOKENS, TOPK))
    capacity = draw_capacity(jax.random.fold_in(jax.random.fold_in(keys[12], part), 71), part)
    router_matrix = centred(keys[4], (MODEL_WIDTH, EXPERT_COUNT), MODEL_WIDTH ** -0.5, 0.09375)
    gate_matrix = centred(keys[5], (EXPERT_COUNT, MODEL_WIDTH, HIDDEN_UNITS), MODEL_WIDTH ** -0.5, 0.09375, ((0, 16),))
    up_matrix = centred(keys[6], (EXPERT_COUNT, MODEL_WIDTH, HIDDEN_UNITS), MODEL_WIDTH ** -0.5, 0.09375, ((0, 16),))
    down_matrix = centred(keys[7], (EXPERT_COUNT, HIDDEN_UNITS, MODEL_WIDTH), HIDDEN_UNITS ** -0.5, 0.1875, ((0, 16),))
    up_adapter_first = centred(keys[8], (EXPERT_COUNT, MODEL_WIDTH, ADAPTER_RANK), MODEL_WIDTH ** -0.5, 0.09375, ((0, 16),))
    up_adapter_second = centred(keys[9], (EXPERT_COUNT, ADAPTER_RANK, HIDDEN_UNITS), ADAPTER_RANK ** -0.5, 0.75, ((0, 16),))
    down_adapter_first = centred(keys[10], (EXPERT_COUNT, HIDDEN_UNITS, ADAPTER_RANK), HIDDEN_UNITS ** -0.5, 0.1875, ((0, 16),))
    down_adapter_second = centred(keys[11], (EXPERT_COUNT, ADAPTER_RANK, MODEL_WIDTH), ADAPTER_RANK ** -0.5, 0.75, ((0, 16),))
    return dict(tokens=tokens, cotangent=cotangent, expert_choice_index=expert_choice_index, capacity=capacity, router_matrix=router_matrix, gate_matrix=gate_matrix, up_matrix=up_matrix, down_matrix=down_matrix, up_adapter_first=up_adapter_first, up_adapter_second=up_adapter_second, down_adapter_first=down_adapter_first, down_adapter_second=down_adapter_second)


route_scale = 2.5
adapter_scale = 2.0


def contract_product(left_side, right_side, axes_pair):
    return lax.dot_general(left_side, right_side, ((axes_pair[0], axes_pair[1]), ((), ())), preferred_element_type=jnp.float32)


def silu_parts(pre_act):
    logistic = jax.nn.sigmoid(pre_act)
    return pre_act * logistic, logistic * (1.0 + pre_act * (1.0 - logistic))


def expert_forward(block_of_rows, mask_of_rows, weight_bundle):
    gate_weight_local, up_weight_local, down_weight_local, up_factor_first, up_factor_second, down_factor_first, down_factor_second = weight_bundle
    lowrank_upward = contract_product(block_of_rows, up_factor_first, ((1,), (0,))).astype(jnp.bfloat16)
    pre_gate = contract_product(block_of_rows, gate_weight_local, ((1,), (0,)))
    upward_preactivation = contract_product(block_of_rows, up_weight_local, ((1,), (0,))) + adapter_scale * contract_product(lowrank_upward, up_factor_second, ((1,), (0,)))
    active, gate_slope = silu_parts(pre_gate)
    inner_activation = (active * upward_preactivation).astype(jnp.bfloat16)
    lowrank_downward = contract_product(inner_activation, down_factor_first, ((1,), (0,))).astype(jnp.bfloat16)
    final_output = (mask_of_rows[:, None] * (contract_product(inner_activation, down_weight_local, ((1,), (0,))) + adapter_scale * contract_product(lowrank_downward, down_factor_second, ((1,), (0,))))).astype(jnp.bfloat16)
    return final_output, (block_of_rows, lowrank_upward, upward_preactivation, active, gate_slope, inner_activation, lowrank_downward)


def expert_reverse_pass(stored_state, output_gradient, weight_bundle):
    block_of_rows, lowrank_upward, upward_preactivation, active, gate_slope, inner_activation, lowrank_downward = stored_state
    gate_weight_local, up_weight_local, down_weight_local, up_factor_first, up_factor_second, down_factor_first, down_factor_second = weight_bundle
    backward_lowrank = contract_product(output_gradient, down_factor_second, ((1,), (1,))).astype(jnp.bfloat16)
    inner_gradient = contract_product(output_gradient, down_weight_local, ((1,), (1,))) + adapter_scale * contract_product(backward_lowrank, down_factor_first, ((1,), (1,)))
    gate_gradient = (inner_gradient * upward_preactivation * gate_slope).astype(jnp.bfloat16)
    upward_gradient = (inner_gradient * active).astype(jnp.bfloat16)
    backward_upward = contract_product(upward_gradient, up_factor_second, ((1,), (1,))).astype(jnp.bfloat16)
    backward_row_set = (contract_product(gate_gradient, gate_weight_local, ((1,), (1,))) + contract_product(upward_gradient, up_weight_local, ((1,), (1,))) + adapter_scale * contract_product(backward_upward, up_factor_first, ((1,), (1,)))).astype(jnp.bfloat16)
    adapter_gradient_set = (adapter_scale * contract_product(block_of_rows, backward_upward, ((0,), (0,))),
                  adapter_scale * contract_product(lowrank_upward, upward_gradient, ((0,), (0,))),
                  adapter_scale * contract_product(inner_activation, backward_lowrank, ((0,), (0,))),
                  adapter_scale * contract_product(lowrank_downward, output_gradient, ((0,), (0,))))
    return backward_row_set, adapter_gradient_set


def reference(tokens, cotangent, expert_choice_index, capacity, router_matrix, gate_matrix, up_matrix, down_matrix, up_adapter_first, up_adapter_second, down_adapter_first, down_adapter_second):
    tok_count, feat_width = tokens.shape
    top_count = expert_choice_index.shape[1]
    expert_group = router_matrix.shape[1]
    logits = jnp.dot(tokens, router_matrix, preferred_element_type=jnp.float32)
    affinity = jax.nn.sigmoid(logits)
    hit_float = (expert_choice_index[:, :, None] == jnp.arange(expert_group, dtype=jnp.int32)[None, None, :]).astype(jnp.float32)
    chosen = jnp.sum(hit_float * affinity[:, None, :], axis=2)
    chosen_sum = jnp.sum(chosen, axis=1, keepdims=True)
    gate_vals = route_scale * chosen / chosen_sum
    cot_float = cotangent.astype(jnp.float32)
    scaled = (gate_vals[:, :, None] * cot_float[:, None, :]).astype(jnp.bfloat16)
    token_iota = jnp.arange(tok_count, dtype=jnp.int32)
    slot_iota = jnp.arange(CAPMAX, dtype=jnp.int32)

    def single_expert(totals, input_rows):
        mixture_total, backward_total, product_total = totals
        expert_index = input_rows[0]
        cap_here = input_rows[1]
        weight_bundle = input_rows[2:]
        hit_here = (expert_choice_index == expert_index).astype(jnp.float32)
        member = jnp.sum((expert_choice_index == expert_index).astype(jnp.int32), axis=1)
        slot_rank = jnp.cumsum(member, dtype=jnp.int32) - member
        keep_flag = member * (slot_rank < cap_here).astype(jnp.int32)
        target_spot = jnp.where(keep_flag > 0, slot_rank, CAPMAX).astype(jnp.int32)
        row_order = jnp.zeros((CAPMAX,), jnp.int32).at[target_spot].set(token_iota, mode="drop")
        row_used = (slot_iota < jnp.sum(keep_flag)).astype(jnp.float32)
        block_of_rows = tokens[row_order]
        grad_rows = jnp.sum(scaled[row_order].astype(jnp.float32) * hit_here[row_order][:, :, None], axis=1)
        output_gradient = (grad_rows * row_used[:, None]).astype(jnp.bfloat16)
        final_output, stored_state = expert_forward(block_of_rows, row_used, weight_bundle)
        backward_row_set, adapter_gradient_set = expert_reverse_pass(stored_state, output_gradient, weight_bundle)
        placed = jnp.zeros((tok_count, feat_width), jnp.float32).at[row_order].add(final_output.astype(jnp.float32) * row_used[:, None])
        placed_back = jnp.zeros((tok_count, feat_width), jnp.float32).at[row_order].add(backward_row_set.astype(jnp.float32) * row_used[:, None])
        gate_here = jnp.sum(gate_vals * hit_here, axis=1)
        mixture_total = mixture_total + gate_here[:, None] * placed
        backward_total = backward_total + placed_back
        product_total = product_total + hit_here * jnp.sum(cot_float * placed, axis=1)[:, None]
        return (mixture_total, backward_total, product_total), adapter_gradient_set

    begin_offset = (jnp.zeros((tok_count, feat_width), jnp.float32), jnp.zeros((tok_count, feat_width), jnp.float32), jnp.zeros((tok_count, top_count), jnp.float32))
    input_rows = (jnp.arange(expert_group, dtype=jnp.int32), capacity, gate_matrix, up_matrix, down_matrix, up_adapter_first, up_adapter_second, down_adapter_first, down_adapter_second)
    (mixture_total, backward_total, product_total), adapter_gradient_set = lax.scan(single_expert, begin_offset, input_rows)
    grad_chosen = route_scale * (product_total / chosen_sum - jnp.sum(product_total * chosen, axis=1, keepdims=True) / (chosen_sum * chosen_sum))
    grad_logits = (jnp.sum(hit_float * grad_chosen[:, :, None], axis=1) * affinity * (1.0 - affinity)).astype(jnp.bfloat16)
    input_grad = (backward_total + contract_product(grad_logits, router_matrix, ((1,), (1,)))).astype(jnp.bfloat16)
    router_grad = contract_product(tokens, grad_logits, ((0,), (0,)))
    return (mixture_total.astype(jnp.bfloat16), input_grad, router_grad,
            adapter_gradient_set[0].astype(jnp.bfloat16), adapter_gradient_set[1].astype(jnp.bfloat16),
            adapter_gradient_set[2].astype(jnp.bfloat16), adapter_gradient_set[3].astype(jnp.bfloat16))
```

```python
import jax
import jax.numpy as jnp
from jax import lax
from jax.sharding import PartitionSpec as P

MOST = 16
LANES = 128

route_scale = 2.5
adapter_scale = 2.0


def mm(left, right, axes):
    return lax.dot_general(
        left, right, ((axes[0], axes[1]), ((), ())), preferred_element_type=jnp.float32
    )


def silu_parts(pre_act):
    logistic = jax.nn.sigmoid(pre_act)
    return (pre_act * logistic, logistic * (1.0 + pre_act * (1.0 - logistic)))


def high_low(value):
    high = lax.reduce_precision(value, 8, 7)
    return high.astype(jnp.bfloat16), (value - high).astype(jnp.bfloat16)


def ring_of(count):
    if count == 8:
        order = [0, 2, 4, 6, 7, 5, 3, 1]
    else:
        order = list(range(count))
    ahead = [(order[i], order[(i + 1) % count]) for i in range(count)]
    back = [(b, a) for a, b in ahead]
    return order, ahead, back


def offsets_of(count):
    half = count // 2
    return [0] + [-k for k in range(1, half)] + list(range(1, half)) + [half]


def ring_gather(block, count):
    _, ahead, back = ring_of(count)
    half, rows = count // 2, block.shape[0] // 2
    from_behind, from_front = [block], [block]
    for _ in range(1, half):
        from_behind.append(lax.ppermute(from_behind[-1], "expert", ahead))
        from_front.append(lax.ppermute(from_front[-1], "expert", back))
    top = lax.ppermute(from_behind[-1][:rows], "expert", ahead)
    low = lax.ppermute(from_front[-1][rows:], "expert", back)
    return from_behind + from_front[1:] + [jnp.concatenate([top, low], axis=0)]


def ring_scatter(part_of, count, rows):
    _, ahead, back = ring_of(count)
    half = count // 2
    narrow = lambda v: v.astype(jnp.bfloat16)
    wide = lambda v: v.astype(jnp.float32)
    opposite = narrow(part_of(count - 1))
    forth = lax.ppermute(opposite[:rows], "expert", ahead)
    hither = lax.ppermute(opposite[rows:], "expert", back)
    for k in range(half - 1, 0, -1):
        front, rear = part_of(half - 1 + k), part_of(k)
        if k == half - 1:
            front = jnp.concatenate([front[:rows] + wide(forth), front[rows:]], axis=0)
            rear = jnp.concatenate([rear[:rows], rear[rows:] + wide(hither)], axis=0)
        else:
            front, rear = front + wide(forth), rear + wide(hither)
        forth = lax.ppermute(narrow(front), "expert", ahead)
        hither = lax.ppermute(narrow(rear), "expert", back)
    return part_of(0) + wide(forth) + wide(hither)


def swap_cores(value):
    return lax.ppermute(value, "dp", [(0, 1), (1, 0)])


def make_per_device(count):
    order, _, _ = ring_of(count)
    offsets = offsets_of(count)
    place = [order.index(chip) for chip in range(count)]

    def per_device(
        tokens,
        cotangent,
        expert_choice_index,
        capacity,
        router_matrix,
        gate_matrix,
        up_matrix,
        down_matrix,
        up_adapter_first,
        up_adapter_second,
        down_adapter_first,
        down_adapter_second,
    ):
        tok_count, width = tokens.shape
        experts = router_matrix.shape[1]
        bf16, f32 = jnp.bfloat16, jnp.float32
        chip, core = lax.axis_index("expert"), lax.axis_index("dp")
        position = jnp.asarray(place, jnp.int32)[chip]
        chips = jnp.asarray(order, jnp.int32)[
            (position + jnp.asarray(offsets, jnp.int32) + count) % count
        ]
        mine, other = 2 * chip + core, 2 * chip + 1 - core
        names = jnp.arange(experts, dtype=jnp.int32)
        own_name = (names == mine).astype(f32)
        sibling_name = (names == other).astype(f32)

        hits = jnp.sum(
            (expert_choice_index[:, :, None] == names[None, None, :]).astype(f32), axis=1
        )
        tail = (-(2 * experts)) % LANES
        token_tail = jnp.pad(hits.astype(bf16), ((0, 0), (0, experts + tail)))
        token_load = jnp.concatenate([tokens, token_tail], axis=1)
        logits = jnp.dot(tokens, router_matrix, preferred_element_type=f32)
        affinity = jax.nn.sigmoid(logits)
        chosen = hits * affinity
        chosen_sum = jnp.sum(chosen, axis=1, keepdims=True)
        gates = route_scale * chosen / chosen_sum
        gate_high, gate_low = high_low(gates)
        cot_load = jnp.concatenate(
            [cotangent, gate_high, gate_low, jnp.zeros((tok_count, tail), bf16)], axis=1
        )

        token_blocks = jnp.stack(ring_gather(token_load, count))
        cot_blocks = jnp.stack(ring_gather(cot_load, count))

        block_hits = token_blocks[:, :, width : width + experts].astype(f32)
        member = jnp.stack(
            [
                jnp.sum(block_hits * own_name, axis=2),
                jnp.sum(block_hits * sibling_name, axis=2),
            ],
            axis=1,
        )
        earlier = (
            jnp.arange(tok_count)[:, None] < jnp.arange(tok_count)[None, :]
        ).astype(bf16)
        before = lax.dot_general(
            member.astype(bf16), earlier, (((2,), (0,)), ((), ())), preferred_element_type=f32
        )
        spots = jnp.arange(MOST, dtype=jnp.int32).astype(f32)
        select = (
            jnp.where(before[:, :, None, :] == spots[None, None, :, None], 1.0, 0.0)
            * member[:, :, None, :]
        ).astype(bf16)
        select = select.reshape(count, 2 * MOST, tok_count)

        def to_slots(blocks):
            rows = lax.dot_general(
                select, blocks, (((2,), (1,)), ((0,), (0,))), preferred_element_type=f32
            ).astype(bf16)
            kept = rows[:, :MOST].reshape(count * MOST, -1)
            sent = rows[:, MOST:].reshape(count * MOST, -1)
            return jnp.concatenate([kept, swap_cores(sent)], axis=0)

        token_rows = to_slots(token_blocks)
        cot_rows = to_slots(cot_blocks)

        valid = jnp.sum(
            token_rows[:, width : width + experts].astype(f32) * own_name, axis=1
        ).reshape(2 * count, MOST)
        sources = jnp.concatenate([2 * chips + core, 2 * chips + 1 - core])
        loads = jnp.sum(valid, axis=1)
        ahead_of = jnp.sum(
            jnp.where(sources[None, :] < sources[:, None], loads[None, :], 0.0), axis=1
        )
        rank = ahead_of[:, None] + spots[None, :]
        keep = jnp.where(rank < capacity[0].astype(f32), valid, 0.0).reshape(-1)
        gate_cols = cot_rows[:, width : width + 2 * experts].astype(f32)
        slot_gate = jnp.sum(
            gate_cols * jnp.concatenate([own_name, own_name]), axis=1
        )

        block = token_rows[:, :width]
        cot_block = cot_rows[:, :width].astype(f32)
        gate_w, up_w, down_w = gate_matrix[0], up_matrix[0], down_matrix[0]
        up_a, up_b = up_adapter_first[0], up_adapter_second[0]
        down_a, down_b = down_adapter_first[0], down_adapter_second[0]

        low_up = mm(block, up_a, ((1,), (0,))).astype(bf16)
        pre_gate = mm(block, gate_w, ((1,), (0,)))
        pre_up = mm(block, up_w, ((1,), (0,))) + adapter_scale * mm(low_up, up_b, ((1,), (0,)))
        active, gate_slope = silu_parts(pre_gate)
        inner = (active * pre_up).astype(bf16)
        low_down = mm(inner, down_a, ((1,), (0,))).astype(bf16)
        routed = (
            keep[:, None]
            * (
                mm(inner, down_w, ((1,), (0,)))
                + adapter_scale * mm(low_down, down_b, ((1,), (0,)))
            )
        ).astype(bf16)
        routed_f32 = routed.astype(f32)
        slot_dots = jnp.sum(cot_block * routed_f32, axis=1)
        dot_high, dot_low = high_low(slot_dots)
        weighted = jnp.concatenate(
            [
                (slot_gate[:, None] * routed_f32).astype(bf16),
                dot_high[:, None] * own_name.astype(bf16)[None, :],
                dot_low[:, None] * own_name.astype(bf16)[None, :],
                jnp.zeros((2 * count * MOST, tail), bf16),
            ],
            axis=1,
        )

        def to_tokens(rows):
            kept = rows[: count * MOST].reshape(count, MOST, -1)
            came = swap_cores(rows[count * MOST :]).reshape(count, MOST, -1)
            both = jnp.concatenate([kept, came], axis=1)

            def part_of(i):
                return mm(select[i], both[i], ((0,), (0,)))

            return ring_scatter(part_of, count, tok_count // 2)

        mixed_all = to_tokens(weighted)
        mixed = mixed_all[:, :width].astype(bf16)

        grad_routed = (keep[:, None] * (slot_gate[:, None] * cot_block)).astype(bf16)
        back_low = mm(grad_routed, down_b, ((1,), (1,))).astype(bf16)
        grad_inner = mm(grad_routed, down_w, ((1,), (1,))) + adapter_scale * mm(
            back_low, down_a, ((1,), (1,))
        )
        grad_gate = (grad_inner * pre_up * gate_slope).astype(bf16)
        grad_up = (grad_inner * active).astype(bf16)
        back_up = mm(grad_up, up_b, ((1,), (1,))).astype(bf16)
        back_routed = (
            mm(grad_gate, gate_w, ((1,), (1,)))
            + mm(grad_up, up_w, ((1,), (1,)))
            + adapter_scale * mm(back_up, up_a, ((1,), (1,)))
        ).astype(bf16)
        back_all = to_tokens(back_routed)
        grad_up_a = adapter_scale * mm(block, back_up, ((0,), (0,)))
        grad_up_b = adapter_scale * mm(low_up, grad_up, ((0,), (0,)))
        grad_down_a = adapter_scale * mm(inner, back_low, ((0,), (0,)))
        grad_down_b = adapter_scale * mm(low_down, grad_routed, ((0,), (0,)))

        grad_gates = (
            mixed_all[:, width : width + experts]
            + mixed_all[:, width + experts : width + 2 * experts]
        )
        grad_chosen = route_scale * (
            grad_gates / chosen_sum
            - jnp.sum(grad_gates * chosen, axis=1, keepdims=True) / (chosen_sum * chosen_sum)
        )
        grad_logits = (hits * grad_chosen * affinity * (1.0 - affinity)).astype(bf16)
        input_grad = (back_all + mm(grad_logits, router_matrix, ((1,), (1,)))).astype(bf16)
        gathered, step = grad_logits[None], 1
        while step < count:
            came = lax.ppermute(gathered, "expert", [(i, i ^ step) for i in range(count)])
            gathered = jnp.concatenate([gathered, came], axis=0)
            step *= 2
        pick = ((chips ^ chip)[:, None] == jnp.arange(count, dtype=jnp.int32)[None, :]).astype(bf16)
        ordered = mm(pick, gathered.reshape(count, -1), ((1,), (0,))).astype(bf16)
        router_half = mm(
            ordered.reshape(count * tok_count, experts),
            token_blocks[:, :, :width].reshape(count * tok_count, width),
            ((0,), (0,)),
        )
        router_grad = (router_half + swap_cores(router_half)).T
        return (
            mixed,
            input_grad,
            router_grad,
            grad_up_a.astype(bf16)[None],
            grad_up_b.astype(bf16)[None],
            grad_down_a.astype(bf16)[None],
            grad_down_b.astype(bf16)[None],
        )

    return per_device


def solution(mesh):
    rows = P(("groups", "expert", "dp"), None)
    whole = P(("groups", "expert", "dp"), None, None)
    weight = P(("expert", "dp"), None, None)
    return jax.shard_map(
        make_per_device(mesh.shape["expert"]),
        mesh=mesh,
        in_specs=(rows, rows, rows, P(("groups", "expert", "dp")), P()) + (weight,) * 7,
        out_specs=(rows, rows, P("groups", None), whole, whole, whole, whole),
        check_vma=False,
    )
```

```python
import functools

import jax
import jax.numpy as jnp
import numpy as np
from jax import lax
from jax.experimental import pallas as pl
from jax.experimental.pallas import tpu as pltpu
from jax.sharding import PartitionSpec as P

MOST = 16
LANES = 128
VMEM_LIMIT = 56 * 2**20

route_scale = 2.5
adapter_scale = 2.0

bf16, f32 = jnp.bfloat16, jnp.float32
in_vmem = pl.BlockSpec(memory_space=pltpu.VMEM)
in_smem = pl.BlockSpec(memory_space=pltpu.SMEM)


def mm(left, right, axes=((1,), (0,))):
    return lax.dot_general(
        left, right, ((axes[0], axes[1]), ((), ())), preferred_element_type=jnp.float32
    )


def mm_nt(left, right):
    return mm(left, right, ((1,), (1,)))


def mm_tn(left, right):
    return mm(left, right, ((0,), (0,)))


def call(body, outs, specs, operands, cost, out_specs=None, grid=(), scratch=()):
    flops, moved = cost
    return pl.pallas_call(
        body,
        out_shape=outs,
        grid=grid,
        in_specs=specs,
        out_specs=out_specs if out_specs is not None else [in_vmem] * len(outs),
        scratch_shapes=list(scratch),
        compiler_params=pltpu.CompilerParams(vmem_limit_bytes=VMEM_LIMIT),
        cost_estimate=pl.CostEstimate(flops=flops, bytes_accessed=moved, transcendentals=0),
    )(*operands)


def struct(shape, dtype=bf16):
    return jax.ShapeDtypeStruct(shape, dtype)


def nbytes(arrays):
    return sum(a.size * a.dtype.itemsize for a in arrays)


def token_load_kernel(choice_ref, tokens_ref, load_ref):
    width = tokens_ref.shape[1]
    rows = tokens_ref.shape[0]
    load_ref[:, :width] = tokens_ref[...]
    names = lax.broadcasted_iota(jnp.int32, (rows, LANES), 1)
    hits = jnp.zeros((rows, LANES), f32)
    for k in range(choice_ref.shape[1]):
        hits += jnp.where(choice_ref[:, k : k + 1] == names, 1.0, 0.0)
    load_ref[:, width:] = hits.astype(bf16)


def cot_load_kernel(choice_ref, tokens_ref, router_ref, cot_ref, load_ref, hits_ref, affinity_ref):
    rows, width = tokens_ref.shape
    experts = router_ref.shape[1]
    load_ref[:, :width] = cot_ref[...]
    affinity = jax.nn.sigmoid(mm(tokens_ref[...], router_ref[...]))
    names = lax.broadcasted_iota(jnp.int32, (rows, experts), 1)
    hits = jnp.zeros((rows, experts), f32)
    for k in range(choice_ref.shape[1]):
        hits += jnp.where(choice_ref[:, k : k + 1] == names, 1.0, 0.0)
    chosen = hits * affinity
    gates = route_scale * chosen / jnp.sum(chosen, axis=1, keepdims=True)
    high = gates.astype(bf16)
    low = (gates - high.astype(f32)).astype(bf16)
    load_ref[:, width:] = jnp.zeros((rows, LANES), bf16)
    load_ref[:, width : width + experts] = high
    load_ref[:, width + experts : width + 2 * experts] = low
    hits_ref[...] = hits
    affinity_ref[...] = affinity


def block_values(refs):
    values = [ref[...] for ref in refs[:-2]]
    return values + [jnp.concatenate([refs[-2][...], refs[-1][...]], axis=0)]


def token_slots_kernel(count, info_ref, *refs):
    blocks, (kept_ref, sent_ref, select_ref) = refs[: count + 1], refs[count + 1 :]
    rows, load = blocks[0].shape
    width = load - LANES
    mine = 2 * info_ref[0] + info_ref[1]
    other = 2 * info_ref[0] + 1 - info_ref[1]
    spot = lax.broadcasted_iota(jnp.int32, (2 * MOST, LANES), 0)
    lane = lax.broadcasted_iota(jnp.int32, (2 * MOST, LANES), 1)
    names = jnp.where(lane == jnp.where(spot < MOST, mine, other), 1.0, 0.0).astype(bf16)
    early = lax.broadcasted_iota(jnp.int32, (rows, rows), 0)
    late = lax.broadcasted_iota(jnp.int32, (rows, rows), 1)
    earlier = jnp.where(early < late, 1.0, 0.0).astype(bf16)
    wanted = lax.broadcasted_iota(jnp.int32, (2 * MOST, rows), 0)
    wanted = jnp.where(wanted < MOST, wanted, wanted - MOST).astype(f32)
    for i, value in enumerate(block_values(blocks)):
        member = mm_nt(names, value[:, width:])
        before = mm(member.astype(bf16), earlier)
        select = jnp.where(before == wanted, member, 0.0).astype(bf16)
        select_ref[i] = select
        out = mm(select, value).astype(bf16)
        kept_ref[pl.ds(i * MOST, MOST)] = out[:MOST]
        sent_ref[pl.ds(i * MOST, MOST)] = out[MOST:]


def cot_slots_kernel(count, select_ref, *refs):
    blocks, (kept_ref, sent_ref) = refs[: count + 1], refs[count + 1 :]
    for i, value in enumerate(block_values(blocks)):
        out = mm(select_ref[i], value).astype(bf16)
        kept_ref[pl.ds(i * MOST, MOST)] = out[:MOST]
        sent_ref[pl.ds(i * MOST, MOST)] = out[MOST:]


def forward_kernel(
    count, first, info_ref, table_ref, kept_ref, came_ref, gate_ref, up_ref, down_ref,
    up_a_ref, up_b_ref, down_a_ref, down_b_ref,
    routed_ref, keep_ref, slope_ref, active_ref, low_up_ref, inner_ref, low_down_ref,
    rows_ref,
):
    step = pl.program_id(0)
    half, width = kept_ref.shape[0], rows_ref.shape[1]
    slots = 2 * half
    tile = gate_ref.shape[1]

    @pl.when(step == 0)
    def _():
        rows_ref[:half] = kept_ref[:, :width]
        rows_ref[half:] = came_ref[:, :width]
        low_up_ref[...] = mm(rows_ref[...], up_a_ref[...]).astype(bf16)
        chip, core = info_ref[0], info_ref[1]
        lane = lax.broadcasted_iota(jnp.int32, (slots, LANES), 1)
        tails = jnp.concatenate([kept_ref[:, width:], came_ref[:, width:]], axis=0).astype(f32)
        valid = jnp.sum(jnp.where(lane == 2 * chip + core, tails, 0.0), axis=1, keepdims=True)
        here = lax.broadcasted_iota(jnp.int32, (slots, 1), 0)
        there = lax.broadcasted_iota(jnp.int32, (1, slots), 1)
        source_here = jnp.zeros((slots, 1), jnp.int32)
        source_there = jnp.zeros((1, slots), jnp.int32)
        for i in range(2 * count):
            parity = core if i < count else 1 - core
            source = 2 * table_ref[chip, i % count] + parity
            source_here = jnp.where(here // MOST == i, source, source_here)
            source_there = jnp.where(there // MOST == i, source, source_there)
        ahead = jnp.where(source_there < source_here, 1.0, 0.0).astype(bf16)
        spread = jnp.broadcast_to(valid, (slots, LANES)).astype(bf16)
        rank = mm(ahead, spread) + (here % MOST).astype(f32)
        keep_ref[...] = jnp.where(rank < info_ref[2].astype(f32), valid, 0.0)

    @pl.when(step < first)
    def _():
        rows = rows_ref[...]
        pre_gate = mm(rows, gate_ref[...])
        pre_up = mm(rows, up_ref[...]) + adapter_scale * mm(low_up_ref[...], up_b_ref[...])
        logistic = jax.nn.sigmoid(pre_gate)
        active = pre_gate * logistic
        active_ref[...] = active
        slope_ref[...] = pre_up * (logistic * (1.0 + pre_gate * (1.0 - logistic)))
        inner_ref[:, pl.ds(pl.multiple_of(step * tile, tile), tile)] = (active * pre_up).astype(bf16)

    @pl.when(step == first)
    def _():
        low_down_ref[...] = mm(inner_ref[...], down_a_ref[...]).astype(bf16)

    @pl.when(step >= first)
    def _():
        value = mm(inner_ref[...], down_ref[...]) + adapter_scale * mm(
            low_down_ref[...], down_b_ref[...]
        )
        routed_ref[...] = (keep_ref[:, :1] * value).astype(bf16)


def weigh_kernel(
    info_ref, routed_ref, keep_ref, kept_ref, came_ref, grad_ref, out_kept_ref, out_sent_ref
):
    half, width = kept_ref.shape[0], routed_ref.shape[1]
    experts = info_ref[3]
    mine = 2 * info_ref[0] + info_ref[1]
    lane = lax.broadcasted_iota(jnp.int32, (half, LANES), 1)
    high_lane, low_lane = lane == mine, lane == mine + experts
    chunk = 4 * LANES
    for cot_ref, out_ref, base in ((kept_ref, out_kept_ref, 0), (came_ref, out_sent_ref, half)):
        tail = cot_ref[:, width:].astype(f32)
        gate = jnp.sum(jnp.where(high_lane | low_lane, tail, 0.0), axis=1, keepdims=True)
        grad_gate = keep_ref[pl.ds(base, half), :1] * gate
        total = jnp.zeros((half, LANES), f32)
        for at in range(0, width, chunk):
            cot = cot_ref[:, at : at + chunk].astype(f32)
            routed = routed_ref[pl.ds(base, half), at : at + chunk].astype(f32)
            grad_ref[pl.ds(base, half), at : at + chunk] = (grad_gate * cot).astype(bf16)
            out_ref[:, at : at + chunk] = (gate * routed).astype(bf16)
            product = cot * routed
            for part in range(0, chunk, LANES):
                total += product[:, part : part + LANES]
        dots = jnp.sum(total, axis=1, keepdims=True)
        high = dots.astype(bf16).astype(f32)
        out_ref[:, width:] = jnp.where(
            high_lane, high, jnp.where(low_lane, dots - high, 0.0)
        ).astype(bf16)


def parts_kernel(count, select_ref, kept_ref, came_ref, *outs):
    for i in range(count):
        at = pl.ds(i * MOST, MOST)
        both = jnp.concatenate([kept_ref[at], came_ref[at]], axis=0)
        part = mm_tn(select_ref[i], both).astype(bf16)
        if i < count - 1:
            outs[i][...] = part
        else:
            rows = part.shape[0] // 2
            outs[i][...] = part[:rows]
            outs[i + 1][...] = part[rows:]


def inner_grad_kernel(
    grad_ref, down_ref, down_b_ref, down_a_ref, slope_ref, active_ref, up_b_ref,
    gate_out_ref, up_out_ref, back_low_ref, back_up_ref, total_ref,
):
    step = pl.program_id(0)

    @pl.when(step == 0)
    def _():
        back_low_ref[...] = mm_nt(grad_ref[...], down_b_ref[...]).astype(bf16)
        total_ref[...] = jnp.zeros_like(total_ref)

    inner = mm_nt(grad_ref[...], down_ref[...]) + adapter_scale * mm_nt(
        back_low_ref[...], down_a_ref[...]
    )
    gate_out_ref[...] = (inner * slope_ref[...]).astype(bf16)
    grad_up = (inner * active_ref[...]).astype(bf16)
    up_out_ref[...] = grad_up
    total_ref[...] += mm_nt(grad_up, up_b_ref[...])

    @pl.when(step == pl.num_programs(0) - 1)
    def _():
        back_up_ref[...] = total_ref[...].astype(bf16)


def row_grad_kernel(
    grad_gate_ref, grad_up_ref, back_up_ref, gate_ref, up_ref, up_a_ref, kept_ref, sent_ref
):
    half = kept_ref.shape[0]
    value = (
        mm_nt(grad_gate_ref[...], gate_ref[...])
        + mm_nt(grad_up_ref[...], up_ref[...])
        + adapter_scale * mm_nt(back_up_ref[...], up_a_ref[...])
    ).astype(bf16)
    kept_ref[...] = value[:half]
    sent_ref[...] = value[half:]


def ring_of(count):
    if count == 8:
        order = [0, 2, 4, 6, 7, 5, 3, 1]
    else:
        order = list(range(count))
    ahead = [(order[i], order[(i + 1) % count]) for i in range(count)]
    back = [(b, a) for a, b in ahead]
    return order, ahead, back


def offsets_of(count):
    half = count // 2
    return [0] + [-k for k in range(1, half)] + list(range(1, half)) + [half]


def ring_gather(block, count):
    _, ahead, back = ring_of(count)
    half, rows = count // 2, block.shape[0] // 2
    from_behind, from_front = [block], [block]
    for _ in range(1, half):
        from_behind.append(lax.ppermute(from_behind[-1], "expert", ahead))
        from_front.append(lax.ppermute(from_front[-1], "expert", back))
    top = lax.ppermute(from_behind[-1][:rows], "expert", ahead)
    low = lax.ppermute(from_front[-1][rows:], "expert", back)
    return from_behind + from_front[1:] + [top, low]


def ring_scatter(parts, count):
    _, ahead, back = ring_of(count)
    half = count // 2
    narrow = lambda v: v.astype(bf16)
    wide = lambda v: v.astype(f32)
    rows = parts[-1].shape[0]
    forth = lax.ppermute(parts[-2], "expert", ahead)
    hither = lax.ppermute(parts[-1], "expert", back)
    for k in range(half - 1, 0, -1):
        front, rear = parts[half - 1 + k], parts[k]
        if k == half - 1:
            front = jnp.concatenate([narrow(wide(front[:rows]) + wide(forth)), front[rows:]], axis=0)
            rear = jnp.concatenate([rear[:rows], narrow(wide(rear[rows:]) + wide(hither))], axis=0)
        else:
            front, rear = narrow(wide(front) + wide(forth)), narrow(wide(rear) + wide(hither))
        forth = lax.ppermute(front, "expert", ahead)
        hither = lax.ppermute(rear, "expert", back)
    return wide(parts[0]) + wide(forth) + wide(hither)


def swap_cores(value):
    return lax.ppermute(value, "dp", [(0, 1), (1, 0)])


def make_per_device(count):
    order, _, _ = ring_of(count)
    offsets = offsets_of(count)
    place = [order.index(chip) for chip in range(count)]
    table = np.array(
        [[order[(place[c] + off) % count] for off in offsets] for c in range(count)], np.int32
    )

    def per_device(
        tokens,
        cotangent,
        expert_choice_index,
        capacity,
        router_matrix,
        gate_matrix,
        up_matrix,
        down_matrix,
        up_adapter_first,
        up_adapter_second,
        down_adapter_first,
        down_adapter_second,
    ):
        tok_count, width = tokens.shape
        experts = router_matrix.shape[1]
        load = width + LANES
        half = count * MOST
        slots = 2 * half
        chip, core = lax.axis_index("expert"), lax.axis_index("dp")
        info = jnp.stack([chip, core, capacity[0], jnp.int32(experts)]).astype(jnp.int32)
        gate_w, up_w, down_w = gate_matrix[0], up_matrix[0], down_matrix[0]
        up_a, up_b = up_adapter_first[0], up_adapter_second[0]
        down_a, down_b = down_adapter_first[0], down_adapter_second[0]
        hidden, rank = gate_w.shape[1], up_a.shape[1]

        (token_load,) = call(
            token_load_kernel, [struct((tok_count, load))], [in_vmem] * 2,
            (expert_choice_index, tokens), (0, 2 * nbytes([tokens])),
        )
        cot_load, hits, affinity = call(
            cot_load_kernel,
            [struct((tok_count, load))] + [struct((tok_count, experts), f32)] * 2,
            [in_vmem] * 4,
            (expert_choice_index, tokens, router_matrix, cotangent),
            (0, 8 * nbytes([tokens])),
        )

        token_blocks = ring_gather(token_load, count)
        cot_blocks = ring_gather(cot_load, count)

        kept, sent, select = call(
            functools.partial(token_slots_kernel, count),
            [struct((half, load))] * 2 + [struct((count, 2 * MOST, tok_count))],
            [in_smem] + [in_vmem] * (count + 1),
            (info, *token_blocks),
            (0, 2 * count * nbytes([token_load])),
        )
        came = swap_cores(sent)
        first, tile, wide_tile = 4, hidden // 4, 4 * LANES
        column = lambda j: jnp.minimum(j, first - 1)
        late = lambda j: jnp.maximum(j - first, 0)
        full = lambda shape: pl.BlockSpec(shape, lambda j: (0,) * len(shape))
        routed, keep, slope, active, low_up, inner, low_down = call(
            functools.partial(forward_kernel, count, first),
            [
                struct((slots, width)), struct((slots, LANES), f32),
                struct((slots, hidden), f32), struct((slots, hidden), f32),
                struct((slots, rank)), struct((slots, hidden)), struct((slots, rank)),
            ],
            [
                in_smem, in_smem, full((half, load)), full((half, load)),
                pl.BlockSpec((width, tile), lambda j: (0, column(j))),
                pl.BlockSpec((width, tile), lambda j: (0, column(j))),
                pl.BlockSpec((hidden, wide_tile), lambda j: (0, late(j))),
                full((width, rank)),
                pl.BlockSpec((rank, tile), lambda j: (0, column(j))),
                full((hidden, rank)),
                pl.BlockSpec((rank, wide_tile), lambda j: (0, late(j))),
            ],
            (info, jnp.asarray(table), kept, came, gate_w, up_w, down_w, up_a, up_b, down_a, down_b),
            (6 * slots * width * hidden, 3 * nbytes([gate_w])),
            out_specs=[
                pl.BlockSpec((slots, wide_tile), lambda j: (0, late(j))),
                full((slots, LANES)),
                pl.BlockSpec((slots, tile), lambda j: (0, column(j))),
                pl.BlockSpec((slots, tile), lambda j: (0, column(j))),
                full((slots, rank)), full((slots, hidden)), full((slots, rank)),
            ],
            grid=(first + width // wide_tile,),
            scratch=[pltpu.VMEM((slots, width), bf16)],
        )

        cot_kept, cot_sent = call(
            functools.partial(cot_slots_kernel, count),
            [struct((half, load))] * 2,
            [in_vmem] * (count + 2),
            (select, *cot_blocks),
            (0, 2 * count * nbytes([token_load])),
        )
        cot_came = swap_cores(cot_sent)
        grad_routed, mix_kept, mix_sent = call(
            weigh_kernel,
            [struct((slots, width))] + [struct((half, load))] * 2,
            [in_smem] + [in_vmem] * 4,
            (info, routed, keep, cot_kept, cot_came),
            (0, 4 * nbytes([routed])),
        )

        def to_tokens(kept, sent):
            came, columns = swap_cores(sent), kept.shape[1]
            parts = call(
                functools.partial(parts_kernel, count),
                [struct((tok_count, columns))] * (count - 1)
                + [struct((tok_count // 2, columns))] * 2,
                [in_vmem] * 3,
                (select, kept, came),
                (0, 3 * nbytes([kept, came])),
            )
            return ring_scatter(parts, count)

        mixed_all = to_tokens(mix_kept, mix_sent)
        mixed = mixed_all[:, :width].astype(bf16)

        grad_gate, grad_up, back_low, back_up = call(
            inner_grad_kernel,
            [struct((slots, hidden))] * 2 + [struct((slots, rank))] * 2,
            [
                full((slots, width)),
                pl.BlockSpec((tile, width), lambda j: (j, 0)),
                full((rank, width)),
                pl.BlockSpec((tile, rank), lambda j: (j, 0)),
                pl.BlockSpec((slots, tile), lambda j: (0, j)),
                pl.BlockSpec((slots, tile), lambda j: (0, j)),
                pl.BlockSpec((rank, tile), lambda j: (0, j)),
            ],
            (grad_routed, down_w, down_b, down_a, slope, active, up_b),
            (2 * slots * width * hidden, nbytes([gate_w])),
            out_specs=[pl.BlockSpec((slots, tile), lambda j: (0, j))] * 2
            + [full((slots, rank))] * 2,
            grid=(4,),
            scratch=[pltpu.VMEM((slots, rank), f32)],
        )
        back_kept, back_sent = call(
            row_grad_kernel,
            [struct((half, width))] * 2,
            [
                full((slots, hidden)), full((slots, hidden)), full((slots, rank)),
                pl.BlockSpec((wide_tile, hidden), lambda j: (j, 0)),
                pl.BlockSpec((wide_tile, hidden), lambda j: (j, 0)),
                pl.BlockSpec((wide_tile, rank), lambda j: (j, 0)),
            ],
            (grad_gate, grad_up, back_up, gate_w, up_w, up_a),
            (4 * slots * width * hidden, 2 * nbytes([gate_w])),
            out_specs=[pl.BlockSpec((half, wide_tile), lambda j: (0, j))] * 2,
            grid=(width // wide_tile,),
        )
        back_all = to_tokens(back_kept, back_sent)
        block = jnp.concatenate([kept[:, :width], came[:, :width]], axis=0)
        grad_up_a = adapter_scale * mm_tn(block, back_up)
        grad_up_b = adapter_scale * mm_tn(low_up, grad_up)
        grad_down_a = adapter_scale * mm_tn(inner, back_low)
        grad_down_b = adapter_scale * mm_tn(low_down, grad_routed)

        chosen = hits * affinity
        chosen_sum = jnp.sum(chosen, axis=1, keepdims=True)
        grad_gates = (
            mixed_all[:, width : width + experts]
            + mixed_all[:, width + experts : width + 2 * experts]
        )
        grad_chosen = route_scale * (
            grad_gates / chosen_sum
            - jnp.sum(grad_gates * chosen, axis=1, keepdims=True) / (chosen_sum * chosen_sum)
        )
        grad_logits = (hits * grad_chosen * affinity * (1.0 - affinity)).astype(bf16)
        input_grad = (back_all + mm_nt(grad_logits, router_matrix)).astype(bf16)
        gathered, step = grad_logits[None], 1
        while step < count:
            arrived = lax.ppermute(gathered, "expert", [(i, i ^ step) for i in range(count)])
            gathered = jnp.concatenate([gathered, arrived], axis=0)
            step *= 2
        chips = jnp.sum(
            jnp.where(jnp.arange(count)[:, None] == chip, jnp.asarray(table), 0), axis=0
        )
        pick = ((chips ^ chip)[:, None] == jnp.arange(count, dtype=jnp.int32)[None, :]).astype(bf16)
        ordered = mm(pick, gathered.reshape(count, -1)).astype(bf16)
        router_half = mm_tn(
            ordered.reshape(count * tok_count, experts),
            jnp.concatenate(token_blocks, axis=0)[:, :width],
        )
        router_grad = (router_half + swap_cores(router_half)).T
        return (
            mixed,
            input_grad,
            router_grad,
            grad_up_a.astype(bf16)[None],
            grad_up_b.astype(bf16)[None],
            grad_down_a.astype(bf16)[None],
            grad_down_b.astype(bf16)[None],
        )

    return per_device


def solution(mesh):
    rows = P(("groups", "expert", "dp"), None)
    whole = P(("groups", "expert", "dp"), None, None)
    weight = P(("expert", "dp"), None, None)
    return jax.shard_map(
        make_per_device(mesh.shape["expert"]),
        mesh=mesh,
        in_specs=(rows, rows, rows, P(("groups", "expert", "dp")), P()) + (weight,) * 7,
        out_specs=(rows, rows, P("groups", None), whole, whole, whole, whole),
        check_vma=False,
    )
```

```python
import functools

import jax
import jax.numpy as jnp
import numpy as np
from jax import lax
from jax.experimental import pallas as pl
from jax.experimental.pallas import tpu as pltpu
from jax.sharding import PartitionSpec as P

MOST = 16
LANES = 128

route_scale = 2.5
adapter_scale = 2.0

bf16, f32 = jnp.bfloat16, jnp.float32
in_vmem = pl.BlockSpec(memory_space=pltpu.VMEM)
in_hbm = pl.BlockSpec(memory_space=pl.ANY)
plain = pl.BlockSpec()
in_smem = pl.BlockSpec(memory_space=pltpu.SMEM)


def mm(left, right, axes=((1,), (0,))):
    return lax.dot_general(
        left, right, ((axes[0], axes[1]), ((), ())), preferred_element_type=jnp.float32
    )


def mm_nt(left, right):
    return mm(left, right, ((1,), (1,)))


def mm_tn(left, right):
    return mm(left, right, ((0,), (0,)))


def call(body, outs, specs, operands, cost, scratch=(), mib=16, out_specs=None):
    flops, moved = cost
    return pl.pallas_call(
        body,
        out_shape=outs,
        in_specs=specs,
        out_specs=out_specs if out_specs is not None else [in_vmem] * len(outs),
        scratch_shapes=list(scratch),
        compiler_params=pltpu.CompilerParams(vmem_limit_bytes=mib * 2**20),
        cost_estimate=pl.CostEstimate(flops=flops, bytes_accessed=moved, transcendentals=0),
    )(*operands)


def struct(shape, dtype=bf16):
    return jax.ShapeDtypeStruct(shape, dtype)


def nbytes(arrays):
    return sum(a.size * a.dtype.itemsize for a in arrays)


def pieces(total, size):
    return [(at, min(size, total - at)) for at in range(0, total, size)]


def start_all(copies):
    for copy in copies:
        copy.start()


def hits_of(choice_ref, columns):
    rows = choice_ref.shape[0]
    names = lax.broadcasted_iota(jnp.int32, (rows, columns), 1)
    hits = jnp.zeros((rows, columns), f32)
    for k in range(choice_ref.shape[1]):
        hits += jnp.where(choice_ref[:, k : k + 1] == names, 1.0, 0.0)
    return hits


def token_load_kernel(choice_ref, tokens_ref, load_ref):
    width = tokens_ref.shape[1]
    load_ref[:, :width] = tokens_ref[...]
    load_ref[:, width:] = hits_of(choice_ref, LANES).astype(bf16)


def cot_load_kernel(choice_ref, tokens_ref, router_ref, cot_ref, load_ref, hits_ref, affinity_ref):
    rows, width = tokens_ref.shape
    experts = router_ref.shape[1]
    load_ref[:, :width] = cot_ref[...]
    affinity = jax.nn.sigmoid(mm(tokens_ref[...], router_ref[...]))
    hits = hits_of(choice_ref, experts)
    chosen = hits * affinity
    gates = route_scale * chosen / jnp.sum(chosen, axis=1, keepdims=True)
    high = gates.astype(bf16)
    low = (gates - high.astype(f32)).astype(bf16)
    load_ref[:, width:] = jnp.zeros((rows, LANES), bf16)
    load_ref[:, width : width + experts] = high
    load_ref[:, width + experts : width + 2 * experts] = low
    hits_ref[...] = hits
    affinity_ref[...] = affinity


def assemble(refs, all_ref):
    at = 0
    for ref in refs:
        all_ref[pl.ds(at, ref.shape[0])] = ref[...]
        at += ref.shape[0]


def expert_names(info_ref, slots, shift):
    mine = 2 * info_ref[0] + info_ref[1]
    other = 2 * info_ref[0] + 1 - info_ref[1]
    slot = lax.broadcasted_iota(jnp.int32, (slots, LANES), 0)
    lane = lax.broadcasted_iota(jnp.int32, (slots, LANES), 1)
    return jnp.where(lane == jnp.where(slot < slots // 2, mine, other) + shift, 1.0, 0.0).astype(bf16)


def token_slots_kernel(info_ref, *refs):
    blocks, (kept_ref, sent_ref, select_ref, all_ref) = refs[:-4], refs[-4:]
    rows, load = blocks[0].shape
    toks, slots = all_ref.shape[0], select_ref.shape[0]
    half = slots // 2
    assemble(blocks, all_ref)
    names = expert_names(info_ref, slots, 0)
    slot = lax.broadcasted_iota(jnp.int32, (slots, toks), 0)
    tok = lax.broadcasted_iota(jnp.int32, (slots, toks), 1)
    slot = jnp.where(slot < half, slot, slot - half)
    member = mm_nt(names, all_ref[:, load - LANES :])
    member = jnp.where(slot // MOST == tok // rows, member, 0.0)
    early = lax.broadcasted_iota(jnp.int32, (toks, toks), 0)
    late = lax.broadcasted_iota(jnp.int32, (toks, toks), 1)
    before = mm(member.astype(bf16), jnp.where(early < late, 1.0, 0.0).astype(bf16))
    select = jnp.where(before == (slot % MOST).astype(f32), member, 0.0).astype(bf16)
    select_ref[...] = select
    for at, size in pieces(load, 4 * LANES):
        out = mm(select, all_ref[:, at : at + size]).astype(bf16)
        kept_ref[:, at : at + size] = out[:half]
        sent_ref[:, at : at + size] = out[half:]


def cot_slots_kernel(info_ref, select_ref, *refs):
    blocks, (kept_ref, sent_ref, high_ref, low_ref, all_ref) = refs[:-5], refs[-5:]
    load = blocks[0].shape[1]
    slots, half, width = select_ref.shape[0], kept_ref.shape[0], kept_ref.shape[1]
    assemble(blocks, all_ref)
    gates = all_ref[:, width:]
    select = select_ref[...].astype(f32)
    high = (select * mm_nt(expert_names(info_ref, slots, 0), gates)).astype(bf16)
    low = (select * mm_nt(expert_names(info_ref, slots, info_ref[3]), gates)).astype(bf16)
    high_ref[...] = high
    low_ref[...] = low
    for at, size in pieces(width, 4 * LANES):
        cot = all_ref[:, at : at + size]
        out = (mm(high, cot) + mm(low, cot)).astype(bf16)
        kept_ref[:, at : at + size] = out[:half]
        sent_ref[:, at : at + size] = out[half:]


def inner_kernel(
    count, tiles, info_ref, table_ref, kept_ref, came_ref, gate_hbm, up_hbm, up_a_ref, up_b_ref,
    inner_ref, slope_ref, active_ref, low_up_ref, keep_ref,
    rows_ref, gate_ref, up_ref, sems,
):
    half, width = kept_ref.shape[0], rows_ref.shape[1]
    slots, tile = 2 * half, gate_ref.shape[1] // tiles
    copies = []
    for j in range(tiles):
        cols = pl.ds(j * tile, tile)
        copies.append(
            [
                pltpu.make_async_copy(gate_hbm.at[:, cols], gate_ref.at[:, cols], sems.at[2 * j]),
                pltpu.make_async_copy(up_hbm.at[:, cols], up_ref.at[:, cols], sems.at[2 * j + 1]),
            ]
        )
        start_all(copies[-1])
    rows_ref[:half] = kept_ref[:, :width]
    rows_ref[half:] = came_ref[:, :width]
    low_up_ref[...] = mm(rows_ref[...], up_a_ref[...]).astype(bf16)
    chip, core = info_ref[0], info_ref[1]
    lane = lax.broadcasted_iota(jnp.int32, (slots, LANES), 1)
    tails = jnp.concatenate([kept_ref[:, width:], came_ref[:, width:]], axis=0).astype(f32)
    valid = jnp.sum(jnp.where(lane == 2 * chip + core, tails, 0.0), axis=1, keepdims=True)
    here = lax.broadcasted_iota(jnp.int32, (slots, 1), 0)
    there = lax.broadcasted_iota(jnp.int32, (1, slots), 1)
    source_here = jnp.zeros((slots, 1), jnp.int32)
    source_there = jnp.zeros((1, slots), jnp.int32)
    for i in range(2 * count):
        source = 2 * table_ref[chip, i % count] + (core if i < count else 1 - core)
        source_here = jnp.where(here // MOST == i, source, source_here)
        source_there = jnp.where(there // MOST == i, source, source_there)
    ahead = jnp.where(source_there < source_here, 1.0, 0.0).astype(bf16)
    spread = jnp.broadcast_to(valid, (slots, LANES)).astype(bf16)
    rank = mm(ahead, spread) + (here % MOST).astype(f32)
    keep_ref[...] = jnp.where(rank < info_ref[2].astype(f32), valid, 0.0)
    for j in range(tiles):
        cols = slice(j * tile, (j + 1) * tile)
        copies[j][0].wait()
        pre_gate = mm(rows_ref[...], gate_ref[:, cols])
        copies[j][1].wait()
        pre_up = mm(rows_ref[...], up_ref[:, cols]) + adapter_scale * mm(
            low_up_ref[...], up_b_ref[:, cols]
        )
        logistic = jax.nn.sigmoid(pre_gate)
        active = pre_gate * logistic
        active_ref[:, cols] = active
        slope_ref[:, cols] = pre_up * (logistic * (1.0 + pre_gate * (1.0 - logistic)))
        inner_ref[:, cols] = (active * pre_up).astype(bf16)


def routed_kernel(
    tiles, inner_ref, keep_ref, down_hbm, down_a_ref, down_b_ref,
    kept_ref, sent_ref, low_down_ref, down_ref, sems,
):
    half, tile = kept_ref.shape[0], down_ref.shape[1] // tiles
    copies = []
    for j in range(tiles):
        cols = pl.ds(j * tile, tile)
        copies.append(pltpu.make_async_copy(down_hbm.at[:, cols], down_ref.at[:, cols], sems.at[j]))
    start_all(copies)
    low_down_ref[...] = mm(inner_ref[...], down_a_ref[...]).astype(bf16)
    keep = keep_ref[:, :1]
    for j in range(tiles):
        cols = slice(j * tile, (j + 1) * tile)
        copies[j].wait()
        value = mm(inner_ref[...], down_ref[:, cols]) + adapter_scale * mm(
            low_down_ref[...], down_b_ref[:, cols]
        )
        value = (keep * value).astype(bf16)
        kept_ref[:, cols] = value[:half]
        sent_ref[:, cols] = value[half:]


def write_parts(outs, at, size, part):
    row = 0
    for ref in outs:
        ref[:, at : at + size] = part[row : row + ref.shape[0]]
        row += ref.shape[0]


def mix_parts_kernel(
    blocks, info_ref, select_ref, high_ref, low_ref, kept_ref, came_ref, *refs
):
    cots, outs, (all_ref, routed_ref) = refs[:blocks], refs[blocks : 2 * blocks], refs[2 * blocks :]
    width, half, slots = kept_ref.shape[1], kept_ref.shape[0], select_ref.shape[0]
    assemble([ref.at[:, :width] for ref in cots], all_ref)
    routed_ref[:half] = kept_ref[...]
    routed_ref[half:] = came_ref[...]
    high = high_ref[...].astype(f32).T.astype(bf16)
    low = low_ref[...].astype(f32).T.astype(bf16)
    select = select_ref[...].astype(f32).T
    for at, size in pieces(width, 4 * LANES):
        rows = routed_ref[:, at : at + size]
        write_parts(outs, at, size, (mm(high, rows) + mm(low, rows)).astype(bf16))
    dots = select * mm_nt(all_ref[...], routed_ref[...])
    first = dots.astype(bf16)
    second = (dots - first.astype(f32)).astype(bf16)
    tail = mm(first, expert_names(info_ref, slots, 0)) + mm(
        second, expert_names(info_ref, slots, info_ref[3])
    )
    write_parts(outs, width, LANES, tail.astype(bf16))


def back_parts_kernel(select_ref, kept_ref, came_ref, *refs):
    outs, (rows_ref,) = refs[:-1], refs[-1:]
    width, half = kept_ref.shape[1], kept_ref.shape[0]
    rows_ref[:half] = kept_ref[...]
    rows_ref[half:] = came_ref[...]
    select = select_ref[...].astype(f32).T.astype(bf16)
    for at, size in pieces(width, 4 * LANES):
        write_parts(outs, at, size, mm(select, rows_ref[:, at : at + size]).astype(bf16))


def inner_grad_kernel(
    tiles, kept_ref, came_ref, keep_ref, down_hbm, down_b_ref, down_a_ref, slope_ref, active_ref,
    up_b_ref,
    grad_ref, gate_out_ref, up_out_ref, back_low_ref, back_up_ref, down_ref, sems,
):
    half, tile = kept_ref.shape[0], down_ref.shape[0] // tiles
    copies = []
    for j in range(tiles):
        rows = pl.ds(j * tile, tile)
        copies.append(pltpu.make_async_copy(down_hbm.at[rows], down_ref.at[rows], sems.at[j]))
    start_all(copies)
    keep = keep_ref[:, :1].astype(bf16)
    grad_ref[:half] = kept_ref[...] * keep[:half]
    grad_ref[half:] = came_ref[...] * keep[half:]
    back_low_ref[...] = mm_nt(grad_ref[...], down_b_ref[...]).astype(bf16)
    for j in range(tiles):
        cols = slice(j * tile, (j + 1) * tile)
        copies[j].wait()
        inner = mm_nt(grad_ref[...], down_ref[cols]) + adapter_scale * mm_nt(
            back_low_ref[...], down_a_ref[cols]
        )
        gate_out_ref[:, cols] = (inner * slope_ref[:, cols]).astype(bf16)
        up_out_ref[:, cols] = (inner * active_ref[:, cols]).astype(bf16)
    back_up_ref[...] = mm_nt(up_out_ref[...], up_b_ref[...]).astype(bf16)


def row_grad_kernel(
    tiles, grad_gate_ref, grad_up_ref, back_up_ref, gate_hbm, up_hbm, up_a_ref,
    kept_ref, sent_ref, gate_ref, up_ref, sems,
):
    half, tile = kept_ref.shape[0], gate_ref.shape[0] // tiles
    copies = []
    for j in range(tiles):
        rows = pl.ds(j * tile, tile)
        copies.append(
            [
                pltpu.make_async_copy(gate_hbm.at[rows], gate_ref.at[rows], sems.at[2 * j]),
                pltpu.make_async_copy(up_hbm.at[rows], up_ref.at[rows], sems.at[2 * j + 1]),
            ]
        )
        start_all(copies[-1])
    for j in range(tiles):
        cols = slice(j * tile, (j + 1) * tile)
        for copy in copies[j]:
            copy.wait()
        value = (
            mm_nt(grad_gate_ref[...], gate_ref[cols])
            + mm_nt(grad_up_ref[...], up_ref[cols])
            + adapter_scale * mm_nt(back_up_ref[...], up_a_ref[cols])
        ).astype(bf16)
        kept_ref[:, cols] = value[:half]
        sent_ref[:, cols] = value[half:]


def adapter_kernel(
    kept_ref, came_ref, back_up_ref, low_up_ref, grad_up_ref, inner_ref, back_low_ref,
    low_down_ref, grad_ref, up_a_ref, up_b_ref, down_a_ref, down_b_ref,
):
    width, half = grad_ref.shape[1], kept_ref.shape[0]
    scaled = lambda value: (adapter_scale * value).astype(bf16)
    back_up = back_up_ref[...]
    for at, size in pieces(width, 4 * LANES):
        cols = slice(at, at + size)
        up_a_ref[cols] = scaled(
            mm_tn(kept_ref[:, cols], back_up[:half]) + mm_tn(came_ref[:, cols], back_up[half:])
        )
        down_b_ref[:, cols] = scaled(mm_tn(low_down_ref[...], grad_ref[:, cols]))
    up_b_ref[...] = scaled(mm_tn(low_up_ref[...], grad_up_ref[...]))
    down_a_ref[...] = scaled(mm_tn(inner_ref[...], back_low_ref[...]))


def hop_kernel(front_ref, forth_ref, rear_ref, hither_ref, front_out_ref, rear_out_ref):
    rows, came = front_ref.shape[0], forth_ref.shape[0]
    plus = lambda a, b: (a[...].astype(f32) + b[...].astype(f32)).astype(bf16)
    if came < rows:
        front_out_ref[came:] = front_ref[came:]
        rear_out_ref[: rows - came] = rear_ref[: rows - came]
    front_out_ref[:came] = plus(front_ref.at[:came], forth_ref)
    rear_out_ref[rows - came :] = plus(rear_ref.at[rows - came :], hither_ref)


def mixed_kernel(
    own_ref, forth_ref, hither_ref, hits_ref, affinity_ref, router_ref,
    mixed_ref, logits_ref, term_ref,
):
    width, experts = mixed_ref.shape[1], hits_ref.shape[1]
    total = lambda cols: (
        own_ref[:, cols].astype(f32) + forth_ref[:, cols].astype(f32) + hither_ref[:, cols].astype(f32)
    )
    mixed_ref[...] = total(slice(0, width)).astype(bf16)
    tail = total(slice(width, width + LANES))
    grad_gates = tail[:, :experts] + tail[:, experts : 2 * experts]
    hits, affinity = hits_ref[...], affinity_ref[...]
    chosen = hits * affinity
    chosen_sum = jnp.sum(chosen, axis=1, keepdims=True)
    grad_chosen = route_scale * (
        grad_gates / chosen_sum
        - jnp.sum(grad_gates * chosen, axis=1, keepdims=True) / (chosen_sum * chosen_sum)
    )
    logits = (hits * grad_chosen * affinity * (1.0 - affinity)).astype(bf16)
    logits_ref[...] = logits
    term_ref[...] = mm_nt(logits, router_ref[...])


def input_grad_kernel(own_ref, forth_ref, hither_ref, term_ref, out_ref):
    out_ref[...] = (
        own_ref[...].astype(f32)
        + forth_ref[...].astype(f32)
        + hither_ref[...].astype(f32)
        + term_ref[...]
    ).astype(bf16)


def router_grad_kernel(count, info_ref, table_ref, logits_ref, *refs):
    blocks, (out_ref, all_ref) = refs[:-2], refs[-2:]
    width = out_ref.shape[1]
    assemble([ref.at[:, :width] for ref in blocks], all_ref)
    chip = info_ref[0]
    logits = jnp.concatenate(
        [logits_ref[table_ref[chip, i] ^ chip] for i in range(count)], axis=0
    )
    out_ref[...] = mm_tn(logits, all_ref[...])


def ring_of(count):
    if count == 8:
        order = [0, 2, 4, 6, 7, 5, 3, 1]
    else:
        order = list(range(count))
    ahead = [(order[i], order[(i + 1) % count]) for i in range(count)]
    back = [(b, a) for a, b in ahead]
    return order, ahead, back


def offsets_of(count):
    half = count // 2
    return [0] + [-k for k in range(1, half)] + list(range(1, half)) + [half]


def ring_gather(block, count):
    _, ahead, back = ring_of(count)
    half, rows = count // 2, block.shape[0] // 2
    from_behind, from_front = [block], [block]
    for _ in range(1, half):
        from_behind.append(lax.ppermute(from_behind[-1], "expert", ahead))
        from_front.append(lax.ppermute(from_front[-1], "expert", back))
    top = lax.ppermute(from_behind[-1][:rows], "expert", ahead)
    low = lax.ppermute(from_front[-1][rows:], "expert", back)
    return from_behind + from_front[1:] + [top, low]


def ring_scatter(parts, count):
    _, ahead, back = ring_of(count)
    half = count // 2
    forth = lax.ppermute(parts[-2], "expert", ahead)
    hither = lax.ppermute(parts[-1], "expert", back)
    for k in range(half - 1, 0, -1):
        front, rear = parts[half - 1 + k], parts[k]
        front, rear = call(
            hop_kernel, [struct(front.shape)] * 2, [in_vmem] * 4,
            (front, forth, rear, hither), (0, 3 * nbytes([front, rear])),
        )
        forth = lax.ppermute(front, "expert", ahead)
        hither = lax.ppermute(rear, "expert", back)
    return forth, hither


def swap_cores(value):
    return lax.ppermute(value, "dp", [(0, 1), (1, 0)])


def make_per_device(count):
    order, _, _ = ring_of(count)
    offsets = offsets_of(count)
    place = [order.index(chip) for chip in range(count)]
    table = np.array(
        [[order[(place[c] + off) % count] for off in offsets] for c in range(count)], np.int32
    )

    def per_device(
        tokens,
        cotangent,
        expert_choice_index,
        capacity,
        router_matrix,
        gate_matrix,
        up_matrix,
        down_matrix,
        up_adapter_first,
        up_adapter_second,
        down_adapter_first,
        down_adapter_second,
    ):
        tok_count, width = tokens.shape
        experts = router_matrix.shape[1]
        load = width + LANES
        half = count * MOST
        slots = 2 * half
        chip, core = lax.axis_index("expert"), lax.axis_index("dp")
        info = jnp.stack([chip, core, capacity[0], jnp.int32(experts)]).astype(jnp.int32)
        gate_w, up_w, down_w = gate_matrix[0], up_matrix[0], down_matrix[0]
        up_a, up_b = up_adapter_first[0], up_adapter_second[0]
        down_a, down_b = down_adapter_first[0], down_adapter_second[0]
        hidden, rank = gate_w.shape[1], up_a.shape[1]

        toks = count * tok_count
        tiles = 4
        rows_of = [tok_count] * (count - 1) + [tok_count // 2] * 2
        table_arr = jnp.asarray(table)

        (token_load,) = call(
            token_load_kernel, [struct((tok_count, load))], [plain] * 2,
            (expert_choice_index, tokens), (0, 2 * nbytes([tokens])),
        )
        cot_load, hits, affinity = call(
            cot_load_kernel,
            [struct((tok_count, load))] + [struct((tok_count, experts), f32)] * 2,
            [plain] * 4,
            (expert_choice_index, tokens, router_matrix, cotangent),
            (0, 8 * nbytes([tokens])),
        )

        token_blocks = ring_gather(token_load, count)
        cot_blocks = ring_gather(cot_load, count)

        kept, sent, select = call(
            token_slots_kernel,
            [struct((half, load))] * 2 + [struct((slots, toks))],
            [in_smem] + [in_vmem] * (count + 1),
            (info, *token_blocks),
            (2 * slots * toks * load, 2 * count * nbytes([token_load])),
            scratch=[pltpu.VMEM((toks, load), bf16)],
        )
        came = swap_cores(sent)
        inner, slope, active, low_up, keep = call(
            functools.partial(inner_kernel, count, tiles),
            [
                struct((slots, hidden)), struct((slots, hidden), f32), struct((slots, hidden), f32),
                struct((slots, rank)), struct((slots, LANES), f32),
            ],
            [in_smem, in_smem, in_vmem, in_vmem, in_hbm, in_hbm, plain, plain],
            (info, table_arr, kept, came, gate_w, up_w, up_a, up_b),
            (4 * slots * width * hidden, 2 * nbytes([gate_w])),
            scratch=[
                pltpu.VMEM((slots, width), bf16), pltpu.VMEM((width, hidden), bf16),
                pltpu.VMEM((width, hidden), bf16), pltpu.SemaphoreType.DMA((2 * tiles,)),
            ],
            mib=32,
        )
        routed_kept, routed_sent, low_down = call(
            functools.partial(routed_kernel, tiles),
            [struct((half, width))] * 2 + [struct((slots, rank))],
            [in_vmem, in_vmem, in_hbm, plain, plain],
            (inner, keep, down_w, down_a, down_b),
            (2 * slots * width * hidden, nbytes([gate_w])),
            scratch=[pltpu.VMEM((hidden, width), bf16), pltpu.SemaphoreType.DMA((tiles,))],
            mib=24,
        )
        routed_came = swap_cores(routed_sent)

        cot_kept, cot_sent, high, low = call(
            cot_slots_kernel,
            [struct((half, width))] * 2 + [struct((slots, toks))] * 2,
            [in_smem] + [in_vmem] * (count + 2),
            (info, select, *cot_blocks),
            (4 * slots * toks * load, 2 * count * nbytes([token_load])),
            scratch=[pltpu.VMEM((toks, load), bf16)],
        )
        cot_came = swap_cores(cot_sent)
        mix_parts = call(
            functools.partial(mix_parts_kernel, count + 1),
            [struct((rows, load)) for rows in rows_of],
            [in_smem] + [in_vmem] * (count + 6),
            (info, select, high, low, routed_kept, routed_came, *cot_blocks),
            (6 * slots * toks * load, 3 * count * nbytes([token_load])),
            scratch=[pltpu.VMEM((toks, width), bf16), pltpu.VMEM((slots, width), bf16)],
        )
        mix_forth, mix_hither = ring_scatter(mix_parts, count)

        grad_routed, grad_gate, grad_up, back_low, back_up = call(
            functools.partial(inner_grad_kernel, tiles),
            [struct((slots, width))] + [struct((slots, hidden))] * 2 + [struct((slots, rank))] * 2,
            [in_vmem] * 3 + [in_hbm, plain, plain, in_vmem, in_vmem, plain],
            (cot_kept, cot_came, keep, down_w, down_b, down_a, slope, active, up_b),
            (2 * slots * width * hidden, nbytes([gate_w])),
            scratch=[pltpu.VMEM((hidden, width), bf16), pltpu.SemaphoreType.DMA((tiles,))],
            mib=24,
        )
        back_kept, back_sent = call(
            functools.partial(row_grad_kernel, tiles),
            [struct((half, width))] * 2,
            [in_vmem] * 3 + [in_hbm, in_hbm, plain],
            (grad_gate, grad_up, back_up, gate_w, up_w, up_a),
            (4 * slots * width * hidden, 2 * nbytes([gate_w])),
            scratch=[
                pltpu.VMEM((width, hidden), bf16), pltpu.VMEM((width, hidden), bf16),
                pltpu.SemaphoreType.DMA((2 * tiles,)),
            ],
            mib=32,
        )
        back_came = swap_cores(back_sent)
        back_parts = call(
            back_parts_kernel,
            [struct((rows, width)) for rows in rows_of],
            [in_vmem] * 3,
            (select, back_kept, back_came),
            (2 * slots * toks * load, 2 * count * nbytes([token_load])),
            scratch=[pltpu.VMEM((slots, width), bf16)],
        )
        back_forth, back_hither = ring_scatter(back_parts, count)
        adapters = call(
            adapter_kernel,
            [
                struct((width, rank)), struct((rank, hidden)),
                struct((hidden, rank)), struct((rank, width)),
            ],
            [in_vmem] * 9,
            (kept, came, back_up, low_up, grad_up, inner, back_low, low_down, grad_routed),
            (8 * slots * width * rank, 4 * nbytes([grad_routed])),
            out_specs=[plain] * 4,
        )

        mixed, grad_logits, router_term = call(
            mixed_kernel,
            [
                struct((tok_count, width)), struct((tok_count, experts)),
                struct((tok_count, width), f32),
            ],
            [in_vmem] * 5 + [plain],
            (mix_parts[0], mix_forth, mix_hither, hits, affinity, router_matrix),
            (0, 4 * nbytes([mix_forth])),
            out_specs=[plain, in_vmem, in_vmem],
        )
        gathered, step = grad_logits[None], 1
        while step < count:
            arrived = lax.ppermute(gathered, "expert", [(i, i ^ step) for i in range(count)])
            gathered = jnp.concatenate([gathered, arrived], axis=0)
            step *= 2
        (router_half,) = call(
            functools.partial(router_grad_kernel, count),
            [struct((experts, width), f32)],
            [in_smem, in_smem] + [in_vmem] * (count + 2),
            (info, table_arr, gathered, *token_blocks),
            (0, count * nbytes([token_load])),
            scratch=[pltpu.VMEM((toks, width), bf16)],
        )
        router_grad = (router_half + swap_cores(router_half)).T
        (input_grad,) = call(
            input_grad_kernel,
            [struct((tok_count, width))],
            [in_vmem] * 4,
            (back_parts[0], back_forth, back_hither, router_term),
            (0, 4 * nbytes([back_forth])),
            out_specs=[plain],
        )
        return (mixed, input_grad, router_grad) + tuple(value[None] for value in adapters)

    return per_device


def solution(mesh):
    rows = P(("groups", "expert", "dp"), None)
    whole = P(("groups", "expert", "dp"), None, None)
    weight = P(("expert", "dp"), None, None)
    return jax.shard_map(
        make_per_device(mesh.shape["expert"]),
        mesh=mesh,
        in_specs=(rows, rows, rows, P(("groups", "expert", "dp")), P()) + (weight,) * 7,
        out_specs=(rows, rows, P("groups", None), whole, whole, whole, whole),
        check_vma=False,
    )
```

```python
import functools

import jax
import jax.numpy as jnp
import numpy as np
from jax import lax
from jax.experimental import pallas as pl
from jax.experimental.pallas import tpu as pltpu
from jax.sharding import PartitionSpec as P

MOST = 16
LANES = 128
COST_SHARE = 10**6

route_scale = 2.5
adapter_scale = 2.0

bf16, f32 = jnp.bfloat16, jnp.float32
in_vmem = pl.BlockSpec(memory_space=pltpu.VMEM)
in_hbm = pl.BlockSpec(memory_space=pltpu.HBM)
in_smem = pl.BlockSpec(memory_space=pltpu.SMEM)


def mm(left, right, axes=((1,), (0,))):
    return lax.dot_general(
        left, right, ((axes[0], axes[1]), ((), ())), preferred_element_type=jnp.float32
    )


def mm_nt(left, right):
    return mm(left, right, ((1,), (1,)))


def mm_tn(left, right):
    return mm(left, right, ((0,), (0,)))


def call(body, outs, specs, operands, cost, scratch=(), mib=8, out_specs=None):
    flops, moved = cost
    return pl.pallas_call(
        body,
        out_shape=outs,
        in_specs=specs,
        out_specs=out_specs if out_specs is not None else [in_vmem] * len(outs),
        scratch_shapes=list(scratch),
        compiler_params=pltpu.CompilerParams(vmem_limit_bytes=mib * 2**20),
        cost_estimate=pl.CostEstimate(
            flops=flops // COST_SHARE, bytes_accessed=moved // COST_SHARE, transcendentals=0
        ),
    )(*operands)


def struct(shape, dtype=bf16):
    return jax.ShapeDtypeStruct(shape, dtype)


def nbytes(arrays):
    return sum(a.size * a.dtype.itemsize for a in arrays)


def pieces(total, size):
    return [(at, min(size, total - at)) for at in range(0, total, size)]


def start_all(copies):
    for copy in copies:
        copy.start()


def token_load_kernel(
    choice_hbm, tokens_hbm, router_hbm, load_ref, choice_ref, router_ref, sems
):
    width, experts = tokens_hbm.shape[1], router_ref.shape[0]
    copies = [
        pltpu.make_async_copy(choice_hbm, choice_ref, sems.at[0]),
        pltpu.make_async_copy(tokens_hbm, load_ref.at[:, pl.ds(0, width)], sems.at[1]),
        pltpu.make_async_copy(router_hbm, router_ref, sems.at[2]),
    ]
    start_all(copies)
    copies[0].wait()
    expert = lax.broadcasted_iota(jnp.int32, (LANES, choice_ref.shape[1]), 0)
    hits = jnp.zeros(expert.shape, f32)
    for k in range(choice_ref.shape[0]):
        hits += jnp.where(choice_ref[k : k + 1] == expert, 1.0, 0.0)
    load_ref[:, width:] = hits.T.astype(bf16)
    copies[1].wait()
    copies[2].wait()
    affinity = jax.nn.sigmoid(mm_nt(load_ref[:, :width], router_ref[...]))
    high = affinity.astype(bf16)
    load_ref[:, width + experts : width + 2 * experts] = high
    load_ref[:, width + 2 * experts : width + 3 * experts] = (affinity - high.astype(f32)).astype(bf16)


def fetch_kernel(count, *refs):
    sources, outs, sems = refs[:count], refs[count : 2 * count], refs[-1]
    copies = [
        pltpu.make_async_copy(source, out, sems.at[i])
        for i, (source, out) in enumerate(zip(sources, outs))
    ]
    start_all(copies)
    for copy in copies:
        copy.wait()


def assemble(refs, all_ref):
    at = 0
    for ref in refs:
        all_ref[pl.ds(at, ref.shape[0])] = ref[...]
        at += ref.shape[0]


def expert_names(info_ref, slots):
    mine = 2 * info_ref[0] + info_ref[1]
    other = 2 * info_ref[0] + 1 - info_ref[1]
    slot = lax.broadcasted_iota(jnp.int32, (slots, LANES), 0)
    lane = lax.broadcasted_iota(jnp.int32, (slots, LANES), 1)
    return jnp.where(lane == jnp.where(slot < slots // 2, mine, other), 1.0, 0.0).astype(bf16)


def token_slots_kernel(experts, info_ref, *refs):
    blocks, (kept_ref, sent_ref, select_ref, high_ref, low_ref, all_ref) = refs[:-6], refs[-6:]
    rows, load = blocks[0].shape
    toks, slots = all_ref.shape[0], select_ref.shape[0]
    half, width = slots // 2, load - LANES
    assemble(blocks, all_ref)
    tails = all_ref[:, width:]
    names = expert_names(info_ref, slots)
    slot = lax.broadcasted_iota(jnp.int32, (slots, toks), 0)
    tok = lax.broadcasted_iota(jnp.int32, (slots, toks), 1)
    slot = jnp.where(slot < half, slot, slot - half)
    member = jnp.where(slot // MOST == tok // rows, mm_nt(names, tails), 0.0)
    early = lax.broadcasted_iota(jnp.int32, (toks, toks), 0)
    late = lax.broadcasted_iota(jnp.int32, (toks, toks), 1)
    before = mm(member.astype(bf16), jnp.where(early < late, 1.0, 0.0).astype(bf16))
    select = jnp.where(before == (slot % MOST).astype(f32), member, 0.0)
    select_ref[...] = select.astype(bf16)
    for at, size in pieces(load, 4 * LANES):
        out = mm(select_ref[...], all_ref[:, at : at + size]).astype(bf16)
        kept_ref[:, at : at + size] = out[:half]
        sent_ref[:, at : at + size] = out[half:]
    lane = lax.broadcasted_iota(jnp.int32, (LANES, LANES), 0)
    expert = lax.broadcasted_iota(jnp.int32, (LANES, LANES), 1)
    parts = (lane == expert + experts) | (lane == expert + 2 * experts)
    affinity = mm(tails, jnp.where(parts & (expert < experts), 1.0, 0.0).astype(bf16))
    mine = lax.broadcasted_iota(jnp.int32, (toks, LANES), 1) < experts
    chosen = jnp.where(mine, tails.astype(f32) * affinity, 0.0)
    gates = route_scale * chosen / jnp.sum(chosen, axis=1, keepdims=True)
    high = gates.astype(bf16)
    low = (gates - high.astype(f32)).astype(bf16)
    high_ref[...] = (select * mm_nt(names, high)).astype(bf16)
    low_ref[...] = (select * mm_nt(names, low)).astype(bf16)


def cot_slots_kernel(high_ref, low_ref, *refs):
    blocks, (kept_ref, sent_ref, all_ref) = refs[:-3], refs[-3:]
    half, width = kept_ref.shape
    assemble(blocks, all_ref)
    for at, size in pieces(width, 4 * LANES):
        cot = all_ref[:, at : at + size]
        out = (mm(high_ref[...], cot) + mm(low_ref[...], cot)).astype(bf16)
        kept_ref[:, at : at + size] = out[:half]
        sent_ref[:, at : at + size] = out[half:]


def inner_kernel(
    count, tiles, info_ref, kept_ref, came_ref, gate_ref, up_a_ref, up_b_ref, up_hbm,
    inner_ref, slope_ref, active_ref, low_up_ref, keep_ref, rows_ref, up_ref, sems,
):
    half, width = kept_ref.shape[0], rows_ref.shape[1]
    slots, tile = 2 * half, gate_ref.shape[1] // tiles
    copy = pltpu.make_async_copy(up_hbm, up_ref, sems.at[0])
    copy.start()
    rows_ref[:half] = kept_ref[:, :width]
    rows_ref[half:] = came_ref[:, :width]
    low_up_ref[...] = mm_nt(rows_ref[...], up_a_ref[...]).astype(bf16)
    chip, core = info_ref[0], info_ref[1]
    lane = lax.broadcasted_iota(jnp.int32, (slots, LANES), 1)
    tails = jnp.concatenate([kept_ref[:, width:], came_ref[:, width:]], axis=0).astype(f32)
    valid = jnp.sum(jnp.where(lane == 2 * chip + core, tails, 0.0), axis=1, keepdims=True)
    here = lax.broadcasted_iota(jnp.int32, (slots, 1), 0)
    there = lax.broadcasted_iota(jnp.int32, (1, slots), 1)
    source_here = jnp.zeros((slots, 1), jnp.int32)
    source_there = jnp.zeros((1, slots), jnp.int32)
    for i in range(2 * count):
        source = 2 * info_ref[4 + i % count] + (core if i < count else 1 - core)
        source_here = jnp.where(here // MOST == i, source, source_here)
        source_there = jnp.where(there // MOST == i, source, source_there)
    ahead = jnp.where(source_there < source_here, 1.0, 0.0).astype(bf16)
    spread = jnp.broadcast_to(valid, (slots, LANES)).astype(bf16)
    rank = mm(ahead, spread) + (here % MOST).astype(f32)
    keep_ref[...] = jnp.where(rank < info_ref[2].astype(f32), valid, 0.0)
    for j in range(tiles):
        cols = slice(j * tile, (j + 1) * tile)
        pre_gate = mm(rows_ref[...], gate_ref[:, cols])
        logistic = jax.nn.sigmoid(pre_gate)
        active_ref[:, cols] = pre_gate * logistic
        slope_ref[:, cols] = logistic * (1.0 + pre_gate * (1.0 - logistic))
    copy.wait()
    for j in range(tiles):
        cols = slice(j * tile, (j + 1) * tile)
        pre_up = mm(rows_ref[...], up_ref[:, cols]) + adapter_scale * mm(
            low_up_ref[...], up_b_ref[:, cols]
        )
        slope_ref[:, cols] = slope_ref[:, cols] * pre_up
        inner_ref[:, cols] = (active_ref[:, cols] * pre_up).astype(bf16)


def routed_kernel(
    tiles, inner_ref, keep_ref, down_ref, down_a_ref, down_b_ref, kept_ref, sent_ref, low_down_ref
):
    half, tile = kept_ref.shape[0], down_ref.shape[1] // tiles
    low_down_ref[...] = mm_nt(inner_ref[...], down_a_ref[...]).astype(bf16)
    keep = keep_ref[:, :1]
    for j in range(tiles):
        cols = slice(j * tile, (j + 1) * tile)
        value = mm(inner_ref[...], down_ref[:, cols]) + adapter_scale * mm(
            low_down_ref[...], down_b_ref[:, cols]
        )
        value = (keep * value).astype(bf16)
        kept_ref[:, cols] = value[:half]
        sent_ref[:, cols] = value[half:]


def write_parts(outs, at, size, part):
    row = 0
    for ref in outs:
        ref[:, at : at + size] = part[row : row + ref.shape[0]]
        row += ref.shape[0]


def mix_parts_kernel(high_ref, low_ref, kept_ref, came_ref, *refs):
    outs, (rows_ref,) = refs[:-1], refs[-1:]
    half, width = kept_ref.shape
    rows_ref[:half] = kept_ref[...]
    rows_ref[half:] = came_ref[...]
    high = high_ref[...].astype(f32).T.astype(bf16)
    low = low_ref[...].astype(f32).T.astype(bf16)
    for at, size in pieces(width, 4 * LANES):
        rows = rows_ref[:, at : at + size]
        write_parts(outs, at, size, (mm(high, rows) + mm(low, rows)).astype(bf16))


def token_places(count, info_ref, toks):
    rows = toks // count
    here = lax.broadcasted_iota(jnp.int32, (toks, toks), 0)
    place = jnp.zeros((toks, toks), jnp.int32)
    for i in range(count):
        place = jnp.where(here // rows == i, rows * (info_ref[4 + i] - i) + here, place)
    return jnp.where(place == lax.broadcasted_iota(jnp.int32, (toks, toks), 1), 1.0, 0.0).astype(bf16)


def gate_grad_kernel(count, info_ref, select_ref, kept_ref, came_ref, all_ref, out_ref, rows_ref):
    half = kept_ref.shape[0]
    rows_ref[:half] = kept_ref[...]
    rows_ref[half:] = came_ref[...]
    dots = select_ref[...].astype(f32) * mm_nt(rows_ref[...], all_ref[...])
    own = jnp.sum(dots[:half], axis=0, keepdims=True)
    other = jnp.sum(dots[half:], axis=0, keepdims=True)
    first = info_ref[1] == 0
    row = lax.broadcasted_iota(jnp.int32, out_ref.shape[1:], 0)
    out = jnp.zeros(out_ref.shape[1:], f32)
    for i, value in enumerate((jnp.where(first, own, other), jnp.where(first, other, own))):
        high = value.astype(bf16).astype(f32)
        out = jnp.where(row == 2 * i, high, jnp.where(row == 2 * i + 1, value - high, out))
    out_ref[0] = mm(out.astype(bf16), token_places(count, info_ref, out.shape[1])).astype(bf16)


def back_parts_kernel(select_ref, kept_ref, came_ref, *refs):
    outs, (rows_ref,) = refs[:-1], refs[-1:]
    width, half = kept_ref.shape[1], kept_ref.shape[0]
    rows_ref[:half] = kept_ref[...]
    rows_ref[half:] = came_ref[...]
    select = select_ref[...].astype(f32).T.astype(bf16)
    for at, size in pieces(width, 4 * LANES):
        write_parts(outs, at, size, mm(select, rows_ref[:, at : at + size]).astype(bf16))


def inner_grad_kernel(
    tiles, kept_ref, came_ref, keep_ref, down_ref, down_b_ref, down_a_ref, slope_ref, active_ref,
    up_b_ref, grad_ref, gate_out_ref, up_out_ref, back_low_ref, back_up_ref,
):
    half, tile = kept_ref.shape[0], down_ref.shape[0] // tiles
    keep = keep_ref[:, :1].astype(bf16)
    grad_ref[:half] = kept_ref[...] * keep[:half]
    grad_ref[half:] = came_ref[...] * keep[half:]
    back_low_ref[...] = mm_nt(grad_ref[...], down_b_ref[...]).astype(bf16)
    for j in range(tiles):
        cols = slice(j * tile, (j + 1) * tile)
        inner = mm_nt(grad_ref[...], down_ref[cols]) + adapter_scale * mm(
            back_low_ref[...], down_a_ref[:, cols]
        )
        gate_out_ref[:, cols] = (inner * slope_ref[:, cols]).astype(bf16)
        up_out_ref[:, cols] = (inner * active_ref[:, cols]).astype(bf16)
    back_up_ref[...] = mm_nt(up_out_ref[...], up_b_ref[...]).astype(bf16)


def row_grad_kernel(
    tiles, grad_gate_ref, grad_up_ref, back_up_ref, gate_ref, up_ref, up_a_ref, kept_ref, sent_ref
):
    half, tile = kept_ref.shape[0], gate_ref.shape[0] // tiles
    for j in range(tiles):
        cols = slice(j * tile, (j + 1) * tile)
        value = (
            mm_nt(grad_gate_ref[...], gate_ref[cols])
            + mm_nt(grad_up_ref[...], up_ref[cols])
            + adapter_scale * mm(back_up_ref[...], up_a_ref[:, cols])
        ).astype(bf16)
        kept_ref[:, cols] = value[:half]
        sent_ref[:, cols] = value[half:]


def adapter_kernel(
    kept_ref, came_ref, back_up_ref, low_up_ref, grad_up_ref, inner_ref, back_low_ref,
    low_down_ref, grad_ref, up_a_ref, up_b_ref, down_a_ref, down_b_ref,
):
    width, half = grad_ref.shape[1], kept_ref.shape[0]
    scaled = lambda value: (adapter_scale * value).astype(bf16)
    back_up = back_up_ref[...]
    for at, size in pieces(width, 4 * LANES):
        cols = slice(at, at + size)
        up_a_ref[:, cols] = scaled(
            mm_tn(back_up[:half], kept_ref[:, cols]) + mm_tn(back_up[half:], came_ref[:, cols])
        )
        down_b_ref[:, cols] = scaled(mm_tn(low_down_ref[...], grad_ref[:, cols]))
    up_b_ref[...] = scaled(mm_tn(low_up_ref[...], grad_up_ref[...]))
    down_a_ref[...] = scaled(mm_tn(back_low_ref[...], inner_ref[...]))


def hop_kernel(*refs):
    for i in range(len(refs) // 3):
        own, came, out = refs[2 * i], refs[2 * i + 1], refs[2 * len(refs) // 3 + i]
        out[...] = (own[...].astype(f32) + came[...].astype(f32)).astype(bf16)


def mixed_kernel(own_ref, forth_ref, hither_ref, out_ref):
    out_ref[...] = (
        own_ref[...].astype(f32) + forth_ref[...].astype(f32) + hither_ref[...].astype(f32)
    ).astype(bf16)


def input_grad_kernel(own_ref, forth_ref, hither_ref, term_ref, out_ref):
    out_ref[...] = (
        own_ref[...].astype(f32)
        + forth_ref[...].astype(f32)
        + hither_ref[...].astype(f32)
        + term_ref[...]
    ).astype(bf16)


def router_grad_kernel(count, info_ref, dots_ref, router_ref, all_ref, out_ref, term_ref):
    experts, width = out_ref.shape
    rows, toks = term_ref.shape[0], all_ref.shape[0]
    tails = all_ref[:, width:].astype(f32).T
    hits = tails[:experts]
    affinity = tails[experts : 2 * experts] + tails[2 * experts : 3 * experts]
    expert = lax.broadcasted_iota(jnp.int32, (experts, toks), 0)
    grad_gates = jnp.zeros((experts, toks), f32)
    gathered = jnp.concatenate([dots_ref[i] for i in range(count)], axis=0)
    gathered = mm_nt(gathered, token_places(count, info_ref, toks))
    for i in range(count):
        name = 2 * (info_ref[0] ^ i)
        dots = gathered[i * dots_ref.shape[1] : (i + 1) * dots_ref.shape[1]]
        grad_gates = jnp.where(expert == name, dots[0:1] + dots[1:2], grad_gates)
        grad_gates = jnp.where(expert == name + 1, dots[2:3] + dots[3:4], grad_gates)
    chosen = hits * affinity
    chosen_sum = jnp.sum(chosen, axis=0, keepdims=True)
    grad_chosen = route_scale * (
        grad_gates / chosen_sum
        - jnp.sum(grad_gates * chosen, axis=0, keepdims=True) / (chosen_sum * chosen_sum)
    )
    logits = (hits * grad_chosen * affinity * (1.0 - affinity)).astype(bf16)
    out_ref[...] = mm(logits, all_ref[:, :width])
    term_ref[...] = mm_tn(logits[:, :rows], router_ref[...])


def ring_of(count):
    if count == 8:
        order = [0, 2, 4, 6, 7, 5, 3, 1]
    else:
        order = list(range(count))
    ahead = [(order[i], order[(i + 1) % count]) for i in range(count)]
    back = [(b, a) for a, b in ahead]
    return order, ahead, back


def offsets_of(count):
    half = count // 2
    return [0] + [-k for k in range(1, half)] + list(range(1, half)) + [half]


def tie(*values):
    return lax.optimization_barrier(values)


class Ring:
    def __init__(self, count, far_ahead):
        _, ahead, back = ring_of(count)
        self.half = count // 2
        self.far, self.near = (ahead, back) if far_ahead else (back, ahead)
        self.far_ahead = far_ahead

    def gather_hop(self, far, near):
        far.append(lax.ppermute(far[-1], "expert", self.far))
        if len(near) < self.half:
            near.append(lax.ppermute(near[-1], "expert", self.near))

    def gathered(self, far, near):
        behind, front = (far, near) if self.far_ahead else (near, far)
        return behind[: self.half] + front[1 : self.half] + [far[self.half]]

    def scatter_starts(self, parts):
        half = self.half
        to_front = [parts[half - 1 + k] for k in range(half - 1, 0, -1)]
        to_rear = [parts[k] for k in range(half - 1, 0, -1)]
        far, near = (to_front, to_rear) if self.far_ahead else (to_rear, to_front)
        return [parts[-1]] + far, near

    def scatter_hop(self, outs, came, step):
        (far_out, near_out), (far, near) = outs, came
        if step == 0:
            far_part, near_part = far_out[0], near_out[0]
        else:
            operands = [far_out[step], far]
            if step < self.half - 1:
                operands += [near_out[step], near]
            added = call(
                hop_kernel,
                [struct(far.shape)] * (len(operands) // 2),
                [in_vmem] * len(operands),
                operands,
                (0, 3 * nbytes(operands) // 2),
            )
            far_part, near_part = added[0], added[-1]
        far = lax.ppermute(far_part, "expert", self.far)
        if step < self.half - 1:
            near = lax.ppermute(near_part, "expert", self.near)
        return far, near


def double(gathered, step):
    size = lax.axis_size("expert")
    came = lax.ppermute(gathered, "expert", [(i, i ^ step) for i in range(size)])
    return jnp.concatenate([gathered, came], axis=0)


def swap_cores(value):
    return lax.ppermute(value, "dp", [(0, 1), (1, 0)])


def make_per_device(count):
    order, _, _ = ring_of(count)
    offsets = offsets_of(count)
    place = [order.index(chip) for chip in range(count)]
    table = np.array(
        [[order[(place[c] + off) % count] for off in offsets] for c in range(count)], np.int32
    )

    def per_device(
        tokens,
        cotangent,
        expert_choice_index,
        capacity,
        router_matrix,
        gate_matrix,
        up_matrix,
        down_matrix,
        up_adapter_first,
        up_adapter_second,
        down_adapter_first,
        down_adapter_second,
    ):
        tok_count, width = tokens.shape
        experts = router_matrix.shape[1]
        load = width + LANES
        half = count * MOST
        slots = 2 * half
        chip, core = lax.axis_index("expert"), lax.axis_index("dp")
        chips = jnp.sum(
            jnp.where(jnp.arange(count)[:, None] == chip, jnp.asarray(table), 0), axis=0
        )
        info = jnp.concatenate([jnp.stack([chip, core, capacity[0]]), chips[:1], chips])
        info = info.astype(jnp.int32)
        gate_w, up_w, down_w = gate_matrix[0], up_matrix[0], down_matrix[0]
        up_a, up_b = up_adapter_first[0], up_adapter_second[0]
        down_a, down_b = down_adapter_first[0], down_adapter_second[0]
        hidden, rank = gate_w.shape[1], up_a.shape[1]

        toks = count * tok_count
        tiles = 4
        up_a, down_a, router = up_a.T, down_a.T, router_matrix.T
        choice = expert_choice_index.T
        ring_token, ring_cot = Ring(count, True), Ring(count, False)
        hops = count // 2

        stay = lambda *arrays: [pltpu.with_memory_space_constraint(a, pltpu.HBM) for a in arrays]

        (token_load,) = call(
            token_load_kernel, [struct((tok_count, load))], [in_hbm] * 3,
            stay(choice, tokens, router), (0, 2 * nbytes([tokens])),
            scratch=[
                pltpu.VMEM(choice.shape, jnp.int32), pltpu.VMEM(router.shape, bf16),
                pltpu.SemaphoreType.DMA((3,)),
            ],
        )

        tok_far, tok_near = [token_load], [token_load]
        ring_token.gather_hop(tok_far, tok_near)
        cot_load, tok_far[1] = tie(cotangent, tok_far[1])
        cot_far, cot_near = [cot_load], [cot_load]
        ring_token.gather_hop(tok_far, tok_near)
        ring_cot.gather_hop(cot_far, cot_near)
        for hop in range(2, hops):
            ring_token.gather_hop(tok_far, tok_near)
            if hop == hops - 2:
                tok_far[-1], cot_far[1], cot_near[1] = tie(tok_far[-1], cot_far[1], cot_near[1])
            if hop < hops - 1:
                ring_cot.gather_hop(cot_far, cot_near)
        token_blocks = ring_token.gathered(tok_far, tok_near)

        kept, sent, select, high, low, token_all = call(
            functools.partial(token_slots_kernel, experts),
            [struct((half, load))] * 2 + [struct((slots, toks))] * 3 + [struct((toks, load))],
            [in_smem] + [in_vmem] * count,
            (info, *token_blocks),
            (2 * slots * toks * load, 2 * count * nbytes([token_load])),
        )
        sent, cot_far[-1], cot_near[-1] = tie(sent, cot_far[-1], cot_near[-1])
        came = swap_cores(sent)
        kept, gate_late = tie(kept, gate_w)
        gate_v, up_a_v, up_b_v = call(
            functools.partial(fetch_kernel, 3),
            [pltpu.VMEM(a.shape, bf16) for a in (gate_w, up_a, up_b)],
            [in_hbm] * 3,
            stay(gate_late, up_a, up_b),
            (0, nbytes([gate_w])),
            scratch=[pltpu.SemaphoreType.DMA((3,))],
            mib=1,
        )
        ring_cot.gather_hop(cot_far, cot_near)
        inner, slope, active, low_up, keep = call(
            functools.partial(inner_kernel, count, tiles),
            [
                struct((slots, hidden)), struct((slots, hidden), f32), struct((slots, hidden), f32),
                struct((slots, rank)), struct((slots, LANES), f32),
            ],
            [in_smem] + [in_vmem] * 5 + [in_hbm],
            (info, kept, came, gate_v, up_a_v, up_b_v, *stay(up_w)),
            (4 * slots * width * hidden, 2 * nbytes([gate_w])),
            scratch=[
                pltpu.VMEM((slots, width), bf16), pltpu.VMEM(up_w.shape, bf16),
                pltpu.SemaphoreType.DMA((1,)),
            ],
            mib=16,
        )
        inner, cot_far[-1], cot_near[-1] = tie(inner, cot_far[-1], cot_near[-1])
        while len(cot_far) <= hops:
            ring_cot.gather_hop(cot_far, cot_near)
        routed_kept, routed_sent, low_down = call(
            functools.partial(routed_kernel, tiles),
            [struct((half, width))] * 2 + [struct((slots, rank))],
            [in_vmem] * 5,
            (inner, keep, down_w, down_a, down_b),
            (2 * slots * width * hidden, nbytes([gate_w])),
        )
        routed_sent, cot_far[-1] = tie(routed_sent, cot_far[-1])
        routed_came = swap_cores(routed_sent)

        mix_parts = call(
            mix_parts_kernel,
            [struct((tok_count, width))] * count,
            [in_vmem] * 4,
            (high, low, routed_kept, routed_came),
            (4 * slots * toks * load, 3 * count * nbytes([token_load])),
            scratch=[pltpu.VMEM((slots, width), bf16)],
        )
        cot_blocks = ring_cot.gathered(cot_far, cot_near)
        mix_parts = list(mix_parts)
        mix_outs = ring_token.scatter_starts(mix_parts)
        mix_came = [ring_token.scatter_hop(mix_outs, (None, None), 0)]

        cot_kept, cot_sent, cot_all = call(
            cot_slots_kernel,
            [struct((half, width))] * 2 + [struct((toks, width))],
            [in_vmem] * (count + 2),
            (high, low, *cot_blocks),
            (4 * slots * toks * load, 2 * count * nbytes([token_load])),
        )
        cot_came = swap_cores(cot_sent)
        (dots,) = call(
            functools.partial(gate_grad_kernel, count),
            [struct((1, 2 * 8, toks))],
            [in_smem] + [in_vmem] * 4,
            (info, select, routed_kept, routed_came, cot_all),
            (2 * slots * toks * load, 2 * count * nbytes([token_load])),
            scratch=[pltpu.VMEM((slots, width), bf16)],
        )
        cot_came, dots = tie(cot_came, dots)
        grad_routed, grad_gate, grad_up, back_low, back_up = call(
            functools.partial(inner_grad_kernel, tiles),
            [struct((slots, width))] + [struct((slots, hidden))] * 2 + [struct((slots, rank))] * 2,
            [in_vmem] * 9,
            (cot_kept, cot_came, keep, down_w, down_b, down_a, slope, active, up_b_v),
            (2 * slots * width * hidden, nbytes([gate_w])),
        )
        dots = double(dots, 1)
        grad_up, dots, *mix_came[0] = tie(grad_up, dots, *mix_came[0])
        mix_came.append(ring_token.scatter_hop(mix_outs, mix_came[-1], 1))
        back_kept, back_sent = call(
            functools.partial(row_grad_kernel, tiles),
            [struct((half, width))] * 2,
            [in_vmem] * 6,
            (grad_gate, grad_up, back_up, gate_v, up_w, up_a_v),
            (4 * slots * width * hidden, 2 * nbytes([gate_w])),
        )
        dots = double(dots, 2)
        back_sent, dots, *mix_came[1] = tie(back_sent, dots, *mix_came[1])
        back_came = swap_cores(back_sent)
        back_parts = call(
            back_parts_kernel,
            [struct((tok_count, width))] * count,
            [in_vmem] * 3,
            (select, back_kept, back_came),
            (2 * slots * toks * load, 2 * count * nbytes([token_load])),
            scratch=[pltpu.VMEM((slots, width), bf16)],
        )
        back_parts = list(back_parts)
        back_outs = ring_cot.scatter_starts(back_parts)
        back_came = [ring_cot.scatter_hop(back_outs, (None, None), 0)]
        step = 4
        while step < count:
            dots = double(dots, step)
            step *= 2
        back_up_late = back_up
        for hop in range(1, hops):
            if hop + 1 < hops:
                mix_came.append(ring_token.scatter_hop(mix_outs, mix_came[-1], hop + 1))
            tied = tie(*back_came[-1], *mix_came[-1], back_up_late)
            back_came[-1], mix_came[-1], back_up_late = tied[:2], tied[2:4], tied[4]
            if hop > 1:
                back_came[-1], dots = tie(back_came[-1], dots)
            back_came.append(ring_cot.scatter_hop(back_outs, back_came[-1], hop))
        adapters = call(
            adapter_kernel,
            [
                struct((rank, width)), struct((rank, hidden)),
                struct((rank, hidden)), struct((rank, width)),
            ],
            [in_vmem] * 9,
            (kept, came, back_up_late, low_up, grad_up, inner, back_low, low_down,
             grad_routed),
            (8 * slots * width * rank, 4 * nbytes([grad_routed])),
            out_specs=[pl.BlockSpec()] * 4,
        )
        adapters = (adapters[0].T, adapters[1], adapters[2].T, adapters[3])

        (mixed,) = call(
            mixed_kernel,
            [struct((tok_count, width))],
            [in_vmem] * 3,
            (mix_parts[0], *mix_came[-1]),
            (0, 4 * nbytes([token_load])),
            out_specs=[pl.BlockSpec()],
        )
        router_half, router_term = call(
            functools.partial(router_grad_kernel, count),
            [struct((experts, width), f32), struct((tok_count, width), f32)],
            [in_smem] + [in_vmem] * 3,
            (info, dots, router, token_all),
            (0, count * nbytes([token_load])),
        )
        router_grad = (router_half + swap_cores(router_half)).T
        (input_grad,) = call(
            input_grad_kernel,
            [struct((tok_count, width))],
            [in_vmem] * 4,
            (back_parts[0], *back_came[-1], router_term),
            (0, 4 * nbytes([token_load])),
            out_specs=[pl.BlockSpec()],
        )
        return (mixed, input_grad, router_grad) + tuple(value[None] for value in adapters)

    return per_device


def solution(mesh):
    rows = P(("groups", "expert", "dp"), None)
    whole = P(("groups", "expert", "dp"), None, None)
    weight = P(("expert", "dp"), None, None)
    return jax.shard_map(
        make_per_device(mesh.shape["expert"]),
        mesh=mesh,
        in_specs=(rows, rows, rows, P(("groups", "expert", "dp")), P()) + (weight,) * 7,
        out_specs=(rows, rows, P("groups", None), whole, whole, whole, whole),
        check_vma=False,
    )
```

```python
import functools

import jax
import jax.numpy as jnp
import numpy as np
from jax import lax
from jax.experimental import pallas as pl
from jax.experimental.pallas import tpu as pltpu
from jax.sharding import PartitionSpec as P

MOST = 16
LANES = 128
COST_SHARE = 10**6

route_scale = 2.5
adapter_scale = 2.0

bf16, f32 = jnp.bfloat16, jnp.float32
in_vmem = pl.BlockSpec(memory_space=pltpu.VMEM)
in_hbm = pl.BlockSpec(memory_space=pltpu.HBM)
in_smem = pl.BlockSpec(memory_space=pltpu.SMEM)


def mm(left, right, axes=((1,), (0,))):
    return lax.dot_general(
        left, right, ((axes[0], axes[1]), ((), ())), preferred_element_type=jnp.float32
    )


def mm_nt(left, right):
    return mm(left, right, ((1,), (1,)))


def mm_tn(left, right):
    return mm(left, right, ((0,), (0,)))


def call(body, outs, specs, operands, cost, scratch=(), mib=8, out_specs=None):
    flops, moved = cost
    return pl.pallas_call(
        body,
        out_shape=outs,
        in_specs=specs,
        out_specs=out_specs if out_specs is not None else [in_vmem] * len(outs),
        scratch_shapes=list(scratch),
        compiler_params=pltpu.CompilerParams(vmem_limit_bytes=mib * 2**20),
        cost_estimate=pl.CostEstimate(
            flops=flops // COST_SHARE, bytes_accessed=moved // COST_SHARE, transcendentals=0
        ),
    )(*operands)


def struct(shape, dtype=bf16):
    return jax.ShapeDtypeStruct(shape, dtype)


def nbytes(arrays):
    return sum(a.size * a.dtype.itemsize for a in arrays)


def pieces(total, size):
    return [(at, min(size, total - at)) for at in range(0, total, size)]


def start_all(copies):
    for copy in copies:
        copy.start()


def token_load_kernel(
    choice_hbm, tokens_hbm, router_hbm, load_ref, choice_ref, router_ref, sems
):
    width, experts = tokens_hbm.shape[1], router_ref.shape[0]
    copies = [
        pltpu.make_async_copy(choice_hbm, choice_ref, sems.at[0]),
        pltpu.make_async_copy(tokens_hbm, load_ref.at[:, pl.ds(0, width)], sems.at[1]),
        pltpu.make_async_copy(router_hbm, router_ref, sems.at[2]),
    ]
    start_all(copies)
    copies[0].wait()
    expert = lax.broadcasted_iota(jnp.int32, (LANES, choice_ref.shape[1]), 0)
    hits = jnp.zeros(expert.shape, f32)
    for k in range(choice_ref.shape[0]):
        hits += jnp.where(choice_ref[k : k + 1] == expert, 1.0, 0.0)
    load_ref[:, width:] = hits.T.astype(bf16)
    copies[1].wait()
    copies[2].wait()
    affinity = jax.nn.sigmoid(mm_nt(load_ref[:, :width], router_ref[...]))
    high = affinity.astype(bf16)
    load_ref[:, width + experts : width + 2 * experts] = high
    load_ref[:, width + 2 * experts : width + 3 * experts] = (affinity - high.astype(f32)).astype(bf16)


def fetch_kernel(count, *refs):
    sources, outs, sems = refs[:count], refs[count : 2 * count], refs[-1]
    copies = [
        pltpu.make_async_copy(source, out, sems.at[i])
        for i, (source, out) in enumerate(zip(sources, outs))
    ]
    start_all(copies)
    for copy in copies:
        copy.wait()


def assemble(refs, all_ref):
    at = 0
    for ref in refs:
        all_ref[pl.ds(at, ref.shape[0])] = ref[...]
        at += ref.shape[0]


def expert_names(info_ref, slots):
    mine = 2 * info_ref[0] + info_ref[1]
    other = 2 * info_ref[0] + 1 - info_ref[1]
    slot = lax.broadcasted_iota(jnp.int32, (slots, LANES), 0)
    lane = lax.broadcasted_iota(jnp.int32, (slots, LANES), 1)
    return jnp.where(lane == jnp.where(slot < slots // 2, mine, other), 1.0, 0.0).astype(bf16)


def token_slots_kernel(experts, info_ref, *refs):
    blocks, (kept_ref, sent_ref, select_ref, high_ref, low_ref, all_ref) = refs[2:-6], refs[-6:]
    rows, load = blocks[0].shape
    toks, slots = all_ref.shape[0], select_ref.shape[0]
    half, width = slots // 2, load - LANES
    assemble(blocks, all_ref)
    tails = all_ref[:, width:]
    names = expert_names(info_ref, slots)
    slot = lax.broadcasted_iota(jnp.int32, (slots, toks), 0)
    tok = lax.broadcasted_iota(jnp.int32, (slots, toks), 1)
    slot = jnp.where(slot < half, slot, slot - half)
    member = jnp.where(slot // MOST == tok // rows, mm_nt(names, tails), 0.0)
    early = lax.broadcasted_iota(jnp.int32, (toks, toks), 0)
    late = lax.broadcasted_iota(jnp.int32, (toks, toks), 1)
    before = mm(member.astype(bf16), jnp.where(early < late, 1.0, 0.0).astype(bf16))
    select = jnp.where(before == (slot % MOST).astype(f32), member, 0.0)
    select_ref[...] = select.astype(bf16)
    for at, size in pieces(load, 4 * LANES):
        out = mm(select_ref[...], all_ref[:, at : at + size]).astype(bf16)
        kept_ref[:, at : at + size] = out[:half]
        sent_ref[:, at : at + size] = out[half:]
    lane = lax.broadcasted_iota(jnp.int32, (LANES, LANES), 0)
    expert = lax.broadcasted_iota(jnp.int32, (LANES, LANES), 1)
    parts = (lane == expert + experts) | (lane == expert + 2 * experts)
    affinity = mm(tails, jnp.where(parts & (expert < experts), 1.0, 0.0).astype(bf16))
    mine = lax.broadcasted_iota(jnp.int32, (toks, LANES), 1) < experts
    chosen = jnp.where(mine, tails.astype(f32) * affinity, 0.0)
    gates = route_scale * chosen / jnp.sum(chosen, axis=1, keepdims=True)
    high = gates.astype(bf16)
    low = (gates - high.astype(f32)).astype(bf16)
    high_ref[...] = (select * mm_nt(names, high)).astype(bf16)
    low_ref[...] = (select * mm_nt(names, low)).astype(bf16)


def cot_slots_kernel(high_ref, low_ref, *refs):
    blocks, (kept_ref, sent_ref, all_ref) = refs[:-3], refs[-3:]
    half, width = kept_ref.shape
    assemble(blocks, all_ref)
    for at, size in pieces(width, 4 * LANES):
        cot = all_ref[:, at : at + size]
        out = (mm(high_ref[...], cot) + mm(low_ref[...], cot)).astype(bf16)
        kept_ref[:, at : at + size] = out[:half]
        sent_ref[:, at : at + size] = out[half:]


def inner_kernel(
    count, tiles, info_ref, kept_ref, came_ref, gate_ref, up_a_ref, up_b_ref, up_ref,
    inner_ref, slope_ref, active_ref, low_up_ref, keep_ref, rows_ref,
):
    half, width = kept_ref.shape[0], rows_ref.shape[1]
    slots, tile = 2 * half, gate_ref.shape[1] // tiles
    rows_ref[:half] = kept_ref[:, :width]
    rows_ref[half:] = came_ref[:, :width]
    low_up_ref[...] = mm_nt(rows_ref[...], up_a_ref[...]).astype(bf16)
    chip, core = info_ref[0], info_ref[1]
    lane = lax.broadcasted_iota(jnp.int32, (slots, LANES), 1)
    tails = jnp.concatenate([kept_ref[:, width:], came_ref[:, width:]], axis=0).astype(f32)
    valid = jnp.sum(jnp.where(lane == 2 * chip + core, tails, 0.0), axis=1, keepdims=True)
    here = lax.broadcasted_iota(jnp.int32, (slots, 1), 0)
    there = lax.broadcasted_iota(jnp.int32, (1, slots), 1)
    source_here = jnp.zeros((slots, 1), jnp.int32)
    source_there = jnp.zeros((1, slots), jnp.int32)
    for i in range(2 * count):
        source = 2 * info_ref[4 + i % count] + (core if i < count else 1 - core)
        source_here = jnp.where(here // MOST == i, source, source_here)
        source_there = jnp.where(there // MOST == i, source, source_there)
    ahead = jnp.where(source_there < source_here, 1.0, 0.0).astype(bf16)
    spread = jnp.broadcast_to(valid, (slots, LANES)).astype(bf16)
    rank = mm(ahead, spread) + (here % MOST).astype(f32)
    keep_ref[...] = jnp.where(rank < info_ref[2].astype(f32), valid, 0.0)
    for j in range(tiles):
        cols = slice(j * tile, (j + 1) * tile)
        pre_gate = mm(rows_ref[...], gate_ref[:, cols])
        pre_up = mm(rows_ref[...], up_ref[:, cols]) + adapter_scale * mm(
            low_up_ref[...], up_b_ref[:, cols]
        )
        logistic = jax.nn.sigmoid(pre_gate)
        active = pre_gate * logistic
        active_ref[:, cols] = active
        slope_ref[:, cols] = pre_up * (logistic * (1.0 + pre_gate * (1.0 - logistic)))
        inner_ref[:, cols] = (active * pre_up).astype(bf16)


def routed_kernel(
    tiles, inner_ref, keep_ref, down_ref, down_a_ref, down_b_ref, kept_ref, sent_ref, low_down_ref
):
    half, tile = kept_ref.shape[0], down_ref.shape[1] // tiles
    low_down_ref[...] = mm_nt(inner_ref[...], down_a_ref[...]).astype(bf16)
    keep = keep_ref[:, :1]
    for j in range(tiles):
        cols = slice(j * tile, (j + 1) * tile)
        value = mm(inner_ref[...], down_ref[:, cols]) + adapter_scale * mm(
            low_down_ref[...], down_b_ref[:, cols]
        )
        value = (keep * value).astype(bf16)
        kept_ref[:, cols] = value[:half]
        sent_ref[:, cols] = value[half:]


def write_parts(outs, at, size, part):
    row = 0
    for ref in outs:
        ref[:, at : at + size] = part[row : row + ref.shape[0]]
        row += ref.shape[0]


def mix_parts_kernel(high_ref, low_ref, kept_ref, came_ref, *refs):
    outs, (rows_ref,) = refs[:-1], refs[-1:]
    half, width = kept_ref.shape
    rows_ref[:half] = kept_ref[...]
    rows_ref[half:] = came_ref[...]
    high = high_ref[...].astype(f32).T.astype(bf16)
    low = low_ref[...].astype(f32).T.astype(bf16)
    for at, size in pieces(width, 4 * LANES):
        rows = rows_ref[:, at : at + size]
        write_parts(outs, at, size, (mm(high, rows) + mm(low, rows)).astype(bf16))


def token_places(count, info_ref, toks):
    rows = toks // count
    here = lax.broadcasted_iota(jnp.int32, (toks, toks), 0)
    place = jnp.zeros((toks, toks), jnp.int32)
    for i in range(count):
        place = jnp.where(here // rows == i, rows * (info_ref[4 + i] - i) + here, place)
    return jnp.where(place == lax.broadcasted_iota(jnp.int32, (toks, toks), 1), 1.0, 0.0).astype(bf16)


def gate_grad_kernel(count, info_ref, select_ref, kept_ref, came_ref, all_ref, out_ref, rows_ref):
    half = kept_ref.shape[0]
    rows_ref[:half] = kept_ref[...]
    rows_ref[half:] = came_ref[...]
    dots = select_ref[...].astype(f32) * mm_nt(rows_ref[...], all_ref[...])
    own = jnp.sum(dots[:half], axis=0, keepdims=True)
    other = jnp.sum(dots[half:], axis=0, keepdims=True)
    first = info_ref[1] == 0
    row = lax.broadcasted_iota(jnp.int32, out_ref.shape[1:], 0)
    out = jnp.zeros(out_ref.shape[1:], f32)
    for i, value in enumerate((jnp.where(first, own, other), jnp.where(first, other, own))):
        high = value.astype(bf16).astype(f32)
        out = jnp.where(row == 2 * i, high, jnp.where(row == 2 * i + 1, value - high, out))
    out_ref[0] = mm(out.astype(bf16), token_places(count, info_ref, out.shape[1])).astype(bf16)


def back_parts_kernel(select_ref, kept_ref, came_ref, *refs):
    outs, (rows_ref,) = refs[:-1], refs[-1:]
    width, half = kept_ref.shape[1], kept_ref.shape[0]
    rows_ref[:half] = kept_ref[...]
    rows_ref[half:] = came_ref[...]
    select = select_ref[...].astype(f32).T.astype(bf16)
    for at, size in pieces(width, 4 * LANES):
        write_parts(outs, at, size, mm(select, rows_ref[:, at : at + size]).astype(bf16))


def inner_grad_kernel(
    tiles, kept_ref, came_ref, keep_ref, down_ref, down_b_ref, down_a_ref, slope_ref, active_ref,
    up_b_ref, grad_ref, gate_out_ref, up_out_ref, back_low_ref, back_up_ref,
):
    half, tile = kept_ref.shape[0], down_ref.shape[0] // tiles
    keep = keep_ref[:, :1].astype(bf16)
    grad_ref[:half] = kept_ref[...] * keep[:half]
    grad_ref[half:] = came_ref[...] * keep[half:]
    back_low_ref[...] = mm_nt(grad_ref[...], down_b_ref[...]).astype(bf16)
    for j in range(tiles):
        cols = slice(j * tile, (j + 1) * tile)
        inner = mm_nt(grad_ref[...], down_ref[cols]) + adapter_scale * mm(
            back_low_ref[...], down_a_ref[:, cols]
        )
        gate_out_ref[:, cols] = (inner * slope_ref[:, cols]).astype(bf16)
        up_out_ref[:, cols] = (inner * active_ref[:, cols]).astype(bf16)
    back_up_ref[...] = mm_nt(up_out_ref[...], up_b_ref[...]).astype(bf16)


def row_grad_kernel(
    tiles, grad_gate_ref, grad_up_ref, back_up_ref, gate_ref, up_ref, up_a_ref, kept_ref, sent_ref
):
    half, tile = kept_ref.shape[0], gate_ref.shape[0] // tiles
    for j in range(tiles):
        cols = slice(j * tile, (j + 1) * tile)
        value = (
            mm_nt(grad_gate_ref[...], gate_ref[cols])
            + mm_nt(grad_up_ref[...], up_ref[cols])
            + adapter_scale * mm(back_up_ref[...], up_a_ref[:, cols])
        ).astype(bf16)
        kept_ref[:, cols] = value[:half]
        sent_ref[:, cols] = value[half:]


def adapter_kernel(
    kept_ref, came_ref, back_up_ref, low_up_ref, grad_up_ref, inner_ref, back_low_ref,
    low_down_ref, grad_ref, up_a_ref, up_b_ref, down_a_ref, down_b_ref,
):
    width, half = grad_ref.shape[1], kept_ref.shape[0]
    scaled = lambda value: (adapter_scale * value).astype(bf16)
    back_up = back_up_ref[...]
    for at, size in pieces(width, 4 * LANES):
        cols = slice(at, at + size)
        up_a_ref[:, cols] = scaled(
            mm_tn(back_up[:half], kept_ref[:, cols]) + mm_tn(back_up[half:], came_ref[:, cols])
        )
        down_b_ref[:, cols] = scaled(mm_tn(low_down_ref[...], grad_ref[:, cols]))
    up_b_ref[...] = scaled(mm_tn(low_up_ref[...], grad_up_ref[...]))
    down_a_ref[...] = scaled(mm_tn(back_low_ref[...], inner_ref[...]))


def hop_kernel(front_ref, forth_ref, rear_ref, hither_ref, front_out_ref, rear_out_ref):
    rows, came = front_ref.shape[0], forth_ref.shape[0]
    plus = lambda a, b: (a[...].astype(f32) + b[...].astype(f32)).astype(bf16)
    if came < rows:
        front_out_ref[came:] = front_ref[came:]
        rear_out_ref[: rows - came] = rear_ref[: rows - came]
    front_out_ref[:came] = plus(front_ref.at[:came], forth_ref)
    rear_out_ref[rows - came :] = plus(rear_ref.at[rows - came :], hither_ref)


def mixed_kernel(own_ref, forth_ref, hither_ref, out_ref):
    out_ref[...] = (
        own_ref[...].astype(f32) + forth_ref[...].astype(f32) + hither_ref[...].astype(f32)
    ).astype(bf16)


def input_grad_kernel(own_ref, forth_ref, hither_ref, term_ref, out_ref):
    out_ref[...] = (
        own_ref[...].astype(f32)
        + forth_ref[...].astype(f32)
        + hither_ref[...].astype(f32)
        + term_ref[...]
    ).astype(bf16)


def router_grad_kernel(count, info_ref, dots_ref, router_ref, all_ref, out_ref, term_ref):
    experts, width = out_ref.shape
    rows, toks = term_ref.shape[0], all_ref.shape[0]
    tails = all_ref[:, width:].astype(f32).T
    hits = tails[:experts]
    affinity = tails[experts : 2 * experts] + tails[2 * experts : 3 * experts]
    expert = lax.broadcasted_iota(jnp.int32, (experts, toks), 0)
    grad_gates = jnp.zeros((experts, toks), f32)
    gathered = jnp.concatenate([dots_ref[i] for i in range(count)], axis=0)
    gathered = mm_nt(gathered, token_places(count, info_ref, toks))
    for i in range(count):
        name = 2 * (info_ref[0] ^ i)
        dots = gathered[i * dots_ref.shape[1] : (i + 1) * dots_ref.shape[1]]
        grad_gates = jnp.where(expert == name, dots[0:1] + dots[1:2], grad_gates)
        grad_gates = jnp.where(expert == name + 1, dots[2:3] + dots[3:4], grad_gates)
    chosen = hits * affinity
    chosen_sum = jnp.sum(chosen, axis=0, keepdims=True)
    grad_chosen = route_scale * (
        grad_gates / chosen_sum
        - jnp.sum(grad_gates * chosen, axis=0, keepdims=True) / (chosen_sum * chosen_sum)
    )
    logits = (hits * grad_chosen * affinity * (1.0 - affinity)).astype(bf16)
    out_ref[...] = mm(logits, all_ref[:, :width])
    term_ref[...] = mm_tn(logits[:, :rows], router_ref[...])


def ring_of(count):
    if count == 8:
        order = [0, 2, 4, 6, 7, 5, 3, 1]
    else:
        order = list(range(count))
    ahead = [(order[i], order[(i + 1) % count]) for i in range(count)]
    back = [(b, a) for a, b in ahead]
    return order, ahead, back


def offsets_of(count):
    half = count // 2
    return [0] + [-k for k in range(1, half)] + list(range(1, half)) + [half]


def tie(*values):
    return lax.optimization_barrier(values)


class Ring:
    def __init__(self, count, far_ahead):
        _, ahead, back = ring_of(count)
        self.half = count // 2
        self.far, self.near = (ahead, back) if far_ahead else (back, ahead)
        self.far_ahead = far_ahead

    def gather_hop(self, far, near):
        far.append(lax.ppermute(far[-1], "expert", self.far))
        if len(near) < self.half:
            near.append(lax.ppermute(near[-1], "expert", self.near))

    def gathered(self, far, near):
        behind, front = (far, near) if self.far_ahead else (near, far)
        return behind[: self.half] + front[1 : self.half] + [far[self.half]]


def scatter_hop(parts, count, came, step):
    _, ahead, back = ring_of(count)
    half = count // 2
    if step == 0:
        front, rear = parts[-2], parts[-1]
    else:
        front, rear = parts[count - 1 - step], parts[half - step]
        front, rear = call(
            hop_kernel, [struct(front.shape)] * 2, [in_vmem] * 4,
            (front, came[0], rear, came[1]), (0, 3 * nbytes([front, rear])),
        )
    return lax.ppermute(front, "expert", ahead), lax.ppermute(rear, "expert", back)


def double(gathered, step):
    size = lax.axis_size("expert")
    came = lax.ppermute(gathered, "expert", [(i, i ^ step) for i in range(size)])
    return jnp.concatenate([gathered, came], axis=0)


def swap_cores(value):
    return lax.ppermute(value, "dp", [(0, 1), (1, 0)])


def make_per_device(count):
    order, _, _ = ring_of(count)
    offsets = offsets_of(count)
    place = [order.index(chip) for chip in range(count)]
    table = np.array(
        [[order[(place[c] + off) % count] for off in offsets] for c in range(count)], np.int32
    )

    def per_device(
        tokens,
        cotangent,
        expert_choice_index,
        capacity,
        router_matrix,
        gate_matrix,
        up_matrix,
        down_matrix,
        up_adapter_first,
        up_adapter_second,
        down_adapter_first,
        down_adapter_second,
    ):
        tok_count, width = tokens.shape
        experts = router_matrix.shape[1]
        load = width + LANES
        half = count * MOST
        slots = 2 * half
        chip, core = lax.axis_index("expert"), lax.axis_index("dp")
        chips = jnp.sum(
            jnp.where(jnp.arange(count)[:, None] == chip, jnp.asarray(table), 0), axis=0
        )
        info = jnp.concatenate([jnp.stack([chip, core, capacity[0]]), chips[:1], chips])
        info = info.astype(jnp.int32)
        gate_w, up_w, down_w = gate_matrix[0], up_matrix[0], down_matrix[0]
        up_a, up_b = up_adapter_first[0], up_adapter_second[0]
        down_a, down_b = down_adapter_first[0], down_adapter_second[0]
        hidden, rank = gate_w.shape[1], up_a.shape[1]

        toks = count * tok_count
        tiles = 4
        up_a, down_a, router = up_a.T, down_a.T, router_matrix.T
        choice = expert_choice_index.T
        ring_token, ring_cot = Ring(count, True), Ring(count, False)
        hops = count // 2
        rows_of = [tok_count] * (count - 1) + [tok_count // 2] * 2

        stay = lambda *arrays: [pltpu.with_memory_space_constraint(a, pltpu.HBM) for a in arrays]

        def fetch(*arrays):
            return call(
                functools.partial(fetch_kernel, len(arrays)),
                [pltpu.VMEM(a.shape, bf16) for a in arrays],
                [in_hbm] * len(arrays),
                stay(*arrays),
                (0, nbytes(arrays)),
                scratch=[pltpu.SemaphoreType.DMA((len(arrays),))],
                mib=1,
            )

        (token_load,) = call(
            token_load_kernel, [struct((tok_count, load))], [in_hbm] * 3,
            stay(choice, tokens, router), (0, 2 * nbytes([tokens])),
            scratch=[
                pltpu.VMEM(choice.shape, jnp.int32), pltpu.VMEM(router.shape, bf16),
                pltpu.SemaphoreType.DMA((3,)),
            ],
        )

        tok_far, tok_near = [token_load], [token_load]
        ring_token.gather_hop(tok_far, tok_near)
        cot_far, cot_near = [cotangent], [cotangent]
        ring_token.gather_hop(tok_far, tok_near)
        tok_near[-1], gate_late = tie(tok_near[-1], gate_w)
        ring_cot.gather_hop(cot_far, cot_near)
        gate_v, up_a_v, up_b_v = fetch(gate_late, up_a, up_b)
        for hop in range(2, hops):
            if hop == hops - 1:
                tok_far[-1], up_b_v = tie(tok_far[-1], up_b_v)
            tok_far[-1], cot_far[-1], cot_near[-1] = tie(tok_far[-1], cot_far[-1], cot_near[-1])
            ring_token.gather_hop(tok_far, tok_near)
            ring_cot.gather_hop(cot_far, cot_near)
            if hop == hops - 2:
                tok_near[-1], up_late = tie(tok_near[-1], up_w)
        (up_v,) = fetch(up_late)
        token_blocks = ring_token.gathered(tok_far, tok_near)

        kept, sent, select, high, low, token_all = call(
            functools.partial(token_slots_kernel, experts),
            [struct((half, load))] * 2 + [struct((slots, toks))] * 3 + [struct((toks, load))],
            [in_smem] + [in_vmem] * (count + 2),
            (info, gate_v, up_v, *token_blocks),
            (2 * slots * toks * load, 2 * count * nbytes([token_load])),
        )
        sent, cot_far[-1], cot_near[-1] = tie(sent, cot_far[-1], cot_near[-1])
        came = swap_cores(sent)
        ring_cot.gather_hop(cot_far, cot_near)
        inner, slope, active, low_up, keep = call(
            functools.partial(inner_kernel, count, tiles),
            [
                struct((slots, hidden)), struct((slots, hidden), f32), struct((slots, hidden), f32),
                struct((slots, rank)), struct((slots, LANES), f32),
            ],
            [in_smem] + [in_vmem] * 6,
            (info, kept, came, gate_v, up_a_v, up_b_v, up_v),
            (4 * slots * width * hidden, 2 * nbytes([gate_w])),
            scratch=[pltpu.VMEM((slots, width), bf16)],
        )
        routed_kept, routed_sent, low_down = call(
            functools.partial(routed_kernel, tiles),
            [struct((half, width))] * 2 + [struct((slots, rank))],
            [in_vmem] * 5,
            (inner, keep, down_w, down_a, down_b),
            (2 * slots * width * hidden, nbytes([gate_w])),
        )
        routed_sent, high = tie(routed_sent, high)
        routed_came = swap_cores(routed_sent)
        cot_blocks = ring_cot.gathered(cot_far, cot_near)
        cot_kept, cot_sent, cot_all = call(
            cot_slots_kernel,
            [struct((half, width))] * 2 + [struct((toks, width))],
            [in_vmem] * (count + 2),
            (high, low, *cot_blocks),
            (4 * slots * toks * load, 2 * count * nbytes([token_load])),
        )
        cot_came = swap_cores(cot_sent)
        routed_came, cot_kept = tie(routed_came, cot_kept)

        mix_parts = call(
            mix_parts_kernel,
            [struct((rows, width)) for rows in rows_of],
            [in_vmem] * 4,
            (high, low, routed_kept, routed_came),
            (4 * slots * toks * load, 3 * count * nbytes([token_load])),
            scratch=[pltpu.VMEM((slots, width), bf16)],
        )
        mix_parts = list(mix_parts)
        cot_came, mix_parts[-1] = tie(cot_came, mix_parts[-1])
        mix_came = [scatter_hop(mix_parts, count, None, 0)]

        grad_routed, grad_gate, grad_up, back_low, back_up = call(
            functools.partial(inner_grad_kernel, tiles),
            [struct((slots, width))] + [struct((slots, hidden))] * 2 + [struct((slots, rank))] * 2,
            [in_vmem] * 9,
            (cot_kept, cot_came, keep, down_w, down_b, down_a, slope, active, up_b_v),
            (2 * slots * width * hidden, nbytes([gate_w])),
        )
        grad_up, *mix_came[0] = tie(grad_up, *mix_came[0])
        mix_came.append(scatter_hop(mix_parts, count, mix_came[0], 1))
        back_kept, back_sent = call(
            functools.partial(row_grad_kernel, tiles),
            [struct((half, width))] * 2,
            [in_vmem] * 6,
            (grad_gate, grad_up, back_up, gate_v, up_v, up_a_v),
            (4 * slots * width * hidden, 2 * nbytes([gate_w])),
        )
        back_sent, *mix_came[1] = tie(back_sent, *mix_came[1])
        back_came = swap_cores(back_sent)
        mix_came.append(scatter_hop(mix_parts, count, mix_came[1], 2))
        back_parts = call(
            back_parts_kernel,
            [struct((rows, width)) for rows in rows_of],
            [in_vmem] * 3,
            (select, back_kept, back_came),
            (2 * slots * toks * load, 2 * count * nbytes([token_load])),
            scratch=[pltpu.VMEM((slots, width), bf16)],
        )
        back_parts = list(back_parts)
        routed_came, *mix_came[2] = tie(routed_came, *mix_came[2])
        back_came = [scatter_hop(back_parts, count, None, 0)]
        (dots,) = call(
            functools.partial(gate_grad_kernel, count),
            [struct((1, 2 * 8, toks))],
            [in_smem] + [in_vmem] * 4,
            (info, select, routed_kept, routed_came, cot_all),
            (2 * slots * toks * load, 2 * count * nbytes([token_load])),
            scratch=[pltpu.VMEM((slots, width), bf16)],
        )
        step = 1
        back_up_late = back_up
        for hop in range(1, hops):
            if hop + 2 < hops:
                mix_came.append(scatter_hop(mix_parts, count, mix_came[-1], hop + 2))
            if hop == hops - 1:
                tied = tie(*back_came[-1], back_up_late, dots, *mix_came[-1])
                mix_came[-1] = tied[4:]
            else:
                tied = tie(*back_came[-1], back_up_late, dots)
            back_came[-1], back_up_late, dots = tied[:2], tied[2], tied[3]
            back_came.append(scatter_hop(back_parts, count, back_came[-1], hop))
            if step < count:
                dots = double(dots, step)
                step *= 2
        while step < count:
            dots = double(dots, step)
            step *= 2
        adapters = call(
            adapter_kernel,
            [
                struct((rank, width)), struct((rank, hidden)),
                struct((rank, hidden)), struct((rank, width)),
            ],
            [in_vmem] * 9,
            (kept, came, back_up_late, low_up, grad_up, inner, back_low, low_down,
             grad_routed),
            (8 * slots * width * rank, 4 * nbytes([grad_routed])),
            out_specs=[pl.BlockSpec()] * 4,
        )
        adapters = (adapters[0].T, adapters[1], adapters[2].T, adapters[3])

        (mixed,) = call(
            mixed_kernel,
            [struct((tok_count, width))],
            [in_vmem] * 3,
            (mix_parts[0], *mix_came[-1]),
            (0, 4 * nbytes([token_load])),
            out_specs=[pl.BlockSpec()],
        )
        router_half, router_term = call(
            functools.partial(router_grad_kernel, count),
            [struct((experts, width), f32), struct((tok_count, width), f32)],
            [in_smem] + [in_vmem] * 3,
            (info, dots, router, token_all),
            (0, count * nbytes([token_load])),
        )
        router_grad = (router_half + swap_cores(router_half)).T
        (input_grad,) = call(
            input_grad_kernel,
            [struct((tok_count, width))],
            [in_vmem] * 4,
            (back_parts[0], *back_came[-1], router_term),
            (0, 4 * nbytes([token_load])),
            out_specs=[pl.BlockSpec()],
        )
        return (mixed, input_grad, router_grad) + tuple(value[None] for value in adapters)

    return per_device


def solution(mesh):
    rows = P(("groups", "expert", "dp"), None)
    whole = P(("groups", "expert", "dp"), None, None)
    weight = P(("expert", "dp"), None, None)
    return jax.shard_map(
        make_per_device(mesh.shape["expert"]),
        mesh=mesh,
        in_specs=(rows, rows, rows, P(("groups", "expert", "dp")), P()) + (weight,) * 7,
        out_specs=(rows, rows, P("groups", None), whole, whole, whole, whole),
        check_vma=False,
    )
```

```python
import functools

import jax
import jax.numpy as jnp
import numpy as np
from jax import lax
from jax.experimental import pallas as pl
from jax.experimental.pallas import tpu as pltpu
from jax.sharding import PartitionSpec as P

MOST = 16
LANES = 128
COST_SHARE = 10**6

route_scale = 2.5
adapter_scale = 2.0

bf16, f32 = jnp.bfloat16, jnp.float32
in_vmem = pl.BlockSpec(memory_space=pltpu.VMEM)
in_hbm = pl.BlockSpec(memory_space=pltpu.HBM)
in_smem = pl.BlockSpec(memory_space=pltpu.SMEM)


def mm(left, right, axes=((1,), (0,))):
    return lax.dot_general(
        left, right, ((axes[0], axes[1]), ((), ())), preferred_element_type=jnp.float32
    )


def mm_nt(left, right):
    return mm(left, right, ((1,), (1,)))


def mm_tn(left, right):
    return mm(left, right, ((0,), (0,)))


def call(body, outs, specs, operands, cost, scratch=(), mib=8, out_specs=None):
    flops, moved = cost
    return pl.pallas_call(
        body,
        out_shape=outs,
        in_specs=specs,
        out_specs=out_specs if out_specs is not None else [in_vmem] * len(outs),
        scratch_shapes=list(scratch),
        compiler_params=pltpu.CompilerParams(vmem_limit_bytes=mib * 2**20),
        cost_estimate=pl.CostEstimate(
            flops=flops // COST_SHARE, bytes_accessed=moved // COST_SHARE, transcendentals=0
        ),
    )(*operands)


def struct(shape, dtype=bf16):
    return jax.ShapeDtypeStruct(shape, dtype)


def nbytes(arrays):
    return sum(a.size * a.dtype.itemsize for a in arrays)


def pieces(total, size):
    return [(at, min(size, total - at)) for at in range(0, total, size)]


def start_all(copies):
    for copy in copies:
        copy.start()


def token_load_kernel(
    choice_hbm, tokens_hbm, router_hbm, load_ref, choice_ref, router_ref, sems
):
    width, experts = tokens_hbm.shape[1], router_ref.shape[0]
    copies = [
        pltpu.make_async_copy(choice_hbm, choice_ref, sems.at[0]),
        pltpu.make_async_copy(tokens_hbm, load_ref.at[:, pl.ds(0, width)], sems.at[1]),
        pltpu.make_async_copy(router_hbm, router_ref, sems.at[2]),
    ]
    start_all(copies)
    copies[0].wait()
    expert = lax.broadcasted_iota(jnp.int32, (LANES, choice_ref.shape[1]), 0)
    hits = jnp.zeros(expert.shape, f32)
    for k in range(choice_ref.shape[0]):
        hits += jnp.where(choice_ref[k : k + 1] == expert, 1.0, 0.0)
    load_ref[:, width:] = hits.T.astype(bf16)
    copies[1].wait()
    copies[2].wait()
    affinity = jax.nn.sigmoid(mm_nt(load_ref[:, :width], router_ref[...]))
    high = affinity.astype(bf16)
    load_ref[:, width + experts : width + 2 * experts] = high
    load_ref[:, width + 2 * experts : width + 3 * experts] = (affinity - high.astype(f32)).astype(bf16)


def fetch_kernel(count, *refs):
    sources, outs, sems = refs[:count], refs[count : 2 * count], refs[-1]
    copies = [
        pltpu.make_async_copy(source, out, sems.at[i])
        for i, (source, out) in enumerate(zip(sources, outs))
    ]
    start_all(copies)
    for copy in copies:
        copy.wait()


def assemble(refs, all_ref):
    at = 0
    for ref in refs:
        all_ref[pl.ds(at, ref.shape[0])] = ref[...]
        at += ref.shape[0]


def expert_names(info_ref, slots):
    mine = 2 * info_ref[0] + info_ref[1]
    other = 2 * info_ref[0] + 1 - info_ref[1]
    slot = lax.broadcasted_iota(jnp.int32, (slots, LANES), 0)
    lane = lax.broadcasted_iota(jnp.int32, (slots, LANES), 1)
    return jnp.where(lane == jnp.where(slot < slots // 2, mine, other), 1.0, 0.0).astype(bf16)


def token_slots_kernel(experts, info_ref, *refs):
    blocks, (kept_ref, sent_ref, select_ref, high_ref, low_ref, all_ref) = refs[1:-6], refs[-6:]
    rows, load = blocks[0].shape
    toks, slots = all_ref.shape[0], select_ref.shape[0]
    half, width = slots // 2, load - LANES
    assemble(blocks, all_ref)
    tails = all_ref[:, width:]
    names = expert_names(info_ref, slots)
    slot = lax.broadcasted_iota(jnp.int32, (slots, toks), 0)
    tok = lax.broadcasted_iota(jnp.int32, (slots, toks), 1)
    slot = jnp.where(slot < half, slot, slot - half)
    member = jnp.where(slot // MOST == tok // rows, mm_nt(names, tails), 0.0)
    early = lax.broadcasted_iota(jnp.int32, (toks, toks), 0)
    late = lax.broadcasted_iota(jnp.int32, (toks, toks), 1)
    before = mm(member.astype(bf16), jnp.where(early < late, 1.0, 0.0).astype(bf16))
    select = jnp.where(before == (slot % MOST).astype(f32), member, 0.0)
    select_ref[...] = select.astype(bf16)
    for at, size in pieces(load, 4 * LANES):
        out = mm(select_ref[...], all_ref[:, at : at + size]).astype(bf16)
        kept_ref[:, at : at + size] = out[:half]
        sent_ref[:, at : at + size] = out[half:]
    lane = lax.broadcasted_iota(jnp.int32, (LANES, LANES), 0)
    expert = lax.broadcasted_iota(jnp.int32, (LANES, LANES), 1)
    parts = (lane == expert + experts) | (lane == expert + 2 * experts)
    affinity = mm(tails, jnp.where(parts & (expert < experts), 1.0, 0.0).astype(bf16))
    mine = lax.broadcasted_iota(jnp.int32, (toks, LANES), 1) < experts
    chosen = jnp.where(mine, tails.astype(f32) * affinity, 0.0)
    gates = route_scale * chosen / jnp.sum(chosen, axis=1, keepdims=True)
    high = gates.astype(bf16)
    low = (gates - high.astype(f32)).astype(bf16)
    high_ref[...] = (select * mm_nt(names, high)).astype(bf16)
    low_ref[...] = (select * mm_nt(names, low)).astype(bf16)


def cot_slots_kernel(high_ref, low_ref, *refs):
    blocks, (kept_ref, sent_ref, all_ref) = refs[:-3], refs[-3:]
    half, width = kept_ref.shape
    assemble(blocks, all_ref)
    for at, size in pieces(width, 4 * LANES):
        cot = all_ref[:, at : at + size]
        out = (mm(high_ref[...], cot) + mm(low_ref[...], cot)).astype(bf16)
        kept_ref[:, at : at + size] = out[:half]
        sent_ref[:, at : at + size] = out[half:]


def inner_kernel(
    count, tiles, info_ref, kept_ref, came_ref, gate_ref, up_a_ref, up_b_ref, up_hbm,
    inner_ref, slope_ref, active_ref, low_up_ref, keep_ref, rows_ref, up_ref, sems,
):
    half, width = kept_ref.shape[0], rows_ref.shape[1]
    slots, tile = 2 * half, gate_ref.shape[1] // tiles
    copy = pltpu.make_async_copy(up_hbm, up_ref, sems.at[0])
    copy.start()
    rows_ref[:half] = kept_ref[:, :width]
    rows_ref[half:] = came_ref[:, :width]
    low_up_ref[...] = mm_nt(rows_ref[...], up_a_ref[...]).astype(bf16)
    chip, core = info_ref[0], info_ref[1]
    lane = lax.broadcasted_iota(jnp.int32, (slots, LANES), 1)
    tails = jnp.concatenate([kept_ref[:, width:], came_ref[:, width:]], axis=0).astype(f32)
    valid = jnp.sum(jnp.where(lane == 2 * chip + core, tails, 0.0), axis=1, keepdims=True)
    here = lax.broadcasted_iota(jnp.int32, (slots, 1), 0)
    there = lax.broadcasted_iota(jnp.int32, (1, slots), 1)
    source_here = jnp.zeros((slots, 1), jnp.int32)
    source_there = jnp.zeros((1, slots), jnp.int32)
    for i in range(2 * count):
        source = 2 * info_ref[4 + i % count] + (core if i < count else 1 - core)
        source_here = jnp.where(here // MOST == i, source, source_here)
        source_there = jnp.where(there // MOST == i, source, source_there)
    ahead = jnp.where(source_there < source_here, 1.0, 0.0).astype(bf16)
    spread = jnp.broadcast_to(valid, (slots, LANES)).astype(bf16)
    rank = mm(ahead, spread) + (here % MOST).astype(f32)
    keep_ref[...] = jnp.where(rank < info_ref[2].astype(f32), valid, 0.0)
    for j in range(tiles):
        cols = slice(j * tile, (j + 1) * tile)
        pre_gate = mm(rows_ref[...], gate_ref[:, cols])
        logistic = jax.nn.sigmoid(pre_gate)
        active_ref[:, cols] = pre_gate * logistic
        slope_ref[:, cols] = logistic * (1.0 + pre_gate * (1.0 - logistic))
    copy.wait()
    for j in range(tiles):
        cols = slice(j * tile, (j + 1) * tile)
        pre_up = mm(rows_ref[...], up_ref[:, cols]) + adapter_scale * mm(
            low_up_ref[...], up_b_ref[:, cols]
        )
        slope_ref[:, cols] = slope_ref[:, cols] * pre_up
        inner_ref[:, cols] = (active_ref[:, cols] * pre_up).astype(bf16)


def routed_kernel(
    tiles, inner_ref, keep_ref, down_ref, down_a_ref, down_b_ref, kept_ref, sent_ref, low_down_ref
):
    half, tile = kept_ref.shape[0], down_ref.shape[1] // tiles
    low_down_ref[...] = mm_nt(inner_ref[...], down_a_ref[...]).astype(bf16)
    keep = keep_ref[:, :1]
    for j in range(tiles):
        cols = slice(j * tile, (j + 1) * tile)
        value = mm(inner_ref[...], down_ref[:, cols]) + adapter_scale * mm(
            low_down_ref[...], down_b_ref[:, cols]
        )
        value = (keep * value).astype(bf16)
        kept_ref[:, cols] = value[:half]
        sent_ref[:, cols] = value[half:]


def write_parts(outs, at, size, part):
    row = 0
    for ref in outs:
        ref[:, at : at + size] = part[row : row + ref.shape[0]]
        row += ref.shape[0]


def mix_parts_kernel(high_ref, low_ref, kept_ref, came_ref, *refs):
    outs, (rows_ref,) = refs[:-1], refs[-1:]
    half, width = kept_ref.shape
    rows_ref[:half] = kept_ref[...]
    rows_ref[half:] = came_ref[...]
    high = high_ref[...].astype(f32).T.astype(bf16)
    low = low_ref[...].astype(f32).T.astype(bf16)
    for at, size in pieces(width, 4 * LANES):
        rows = rows_ref[:, at : at + size]
        write_parts(outs, at, size, (mm(high, rows) + mm(low, rows)).astype(bf16))


def token_places(count, info_ref, toks):
    rows = toks // count
    here = lax.broadcasted_iota(jnp.int32, (toks, toks), 0)
    place = jnp.zeros((toks, toks), jnp.int32)
    for i in range(count):
        place = jnp.where(here // rows == i, rows * (info_ref[4 + i] - i) + here, place)
    return jnp.where(place == lax.broadcasted_iota(jnp.int32, (toks, toks), 1), 1.0, 0.0).astype(bf16)


def gate_grad_kernel(count, info_ref, select_ref, kept_ref, came_ref, all_ref, out_ref, rows_ref):
    half = kept_ref.shape[0]
    rows_ref[:half] = kept_ref[...]
    rows_ref[half:] = came_ref[...]
    dots = select_ref[...].astype(f32) * mm_nt(rows_ref[...], all_ref[...])
    own = jnp.sum(dots[:half], axis=0, keepdims=True)
    other = jnp.sum(dots[half:], axis=0, keepdims=True)
    first = info_ref[1] == 0
    row = lax.broadcasted_iota(jnp.int32, out_ref.shape[1:], 0)
    out = jnp.zeros(out_ref.shape[1:], f32)
    for i, value in enumerate((jnp.where(first, own, other), jnp.where(first, other, own))):
        high = value.astype(bf16).astype(f32)
        out = jnp.where(row == 2 * i, high, jnp.where(row == 2 * i + 1, value - high, out))
    out_ref[0] = mm(out.astype(bf16), token_places(count, info_ref, out.shape[1])).astype(bf16)


def back_parts_kernel(select_ref, kept_ref, came_ref, *refs):
    outs, (rows_ref,) = refs[:-1], refs[-1:]
    width, half = kept_ref.shape[1], kept_ref.shape[0]
    rows_ref[:half] = kept_ref[...]
    rows_ref[half:] = came_ref[...]
    select = select_ref[...].astype(f32).T.astype(bf16)
    for at, size in pieces(width, 4 * LANES):
        write_parts(outs, at, size, mm(select, rows_ref[:, at : at + size]).astype(bf16))


def inner_grad_kernel(
    tiles, kept_ref, came_ref, keep_ref, down_ref, down_b_ref, down_a_ref, slope_ref, active_ref,
    up_b_ref, grad_ref, gate_out_ref, up_out_ref, back_low_ref, back_up_ref,
):
    half, tile = kept_ref.shape[0], down_ref.shape[0] // tiles
    keep = keep_ref[:, :1].astype(bf16)
    grad_ref[:half] = kept_ref[...] * keep[:half]
    grad_ref[half:] = came_ref[...] * keep[half:]
    back_low_ref[...] = mm_nt(grad_ref[...], down_b_ref[...]).astype(bf16)
    for j in range(tiles):
        cols = slice(j * tile, (j + 1) * tile)
        inner = mm_nt(grad_ref[...], down_ref[cols]) + adapter_scale * mm(
            back_low_ref[...], down_a_ref[:, cols]
        )
        gate_out_ref[:, cols] = (inner * slope_ref[:, cols]).astype(bf16)
        up_out_ref[:, cols] = (inner * active_ref[:, cols]).astype(bf16)
    back_up_ref[...] = mm_nt(up_out_ref[...], up_b_ref[...]).astype(bf16)


def row_grad_kernel(
    tiles, grad_gate_ref, grad_up_ref, back_up_ref, gate_ref, up_ref, up_a_ref, kept_ref, sent_ref
):
    half, tile = kept_ref.shape[0], gate_ref.shape[0] // tiles
    for j in range(tiles):
        cols = slice(j * tile, (j + 1) * tile)
        value = (
            mm_nt(grad_gate_ref[...], gate_ref[cols])
            + mm_nt(grad_up_ref[...], up_ref[cols])
            + adapter_scale * mm(back_up_ref[...], up_a_ref[:, cols])
        ).astype(bf16)
        kept_ref[:, cols] = value[:half]
        sent_ref[:, cols] = value[half:]


def adapter_kernel(
    kept_ref, came_ref, back_up_ref, low_up_ref, grad_up_ref, inner_ref, back_low_ref,
    low_down_ref, grad_ref, up_a_ref, up_b_ref, down_a_ref, down_b_ref,
):
    width, half = grad_ref.shape[1], kept_ref.shape[0]
    scaled = lambda value: (adapter_scale * value).astype(bf16)
    back_up = back_up_ref[...]
    for at, size in pieces(width, 4 * LANES):
        cols = slice(at, at + size)
        up_a_ref[:, cols] = scaled(
            mm_tn(back_up[:half], kept_ref[:, cols]) + mm_tn(back_up[half:], came_ref[:, cols])
        )
        down_b_ref[:, cols] = scaled(mm_tn(low_down_ref[...], grad_ref[:, cols]))
    up_b_ref[...] = scaled(mm_tn(low_up_ref[...], grad_up_ref[...]))
    down_a_ref[...] = scaled(mm_tn(back_low_ref[...], inner_ref[...]))


def hop_kernel(front_ref, forth_ref, rear_ref, hither_ref, front_out_ref, rear_out_ref):
    rows, came = front_ref.shape[0], forth_ref.shape[0]
    plus = lambda a, b: (a[...].astype(f32) + b[...].astype(f32)).astype(bf16)
    if came < rows:
        front_out_ref[came:] = front_ref[came:]
        rear_out_ref[: rows - came] = rear_ref[: rows - came]
    front_out_ref[:came] = plus(front_ref.at[:came], forth_ref)
    rear_out_ref[rows - came :] = plus(rear_ref.at[rows - came :], hither_ref)


def mixed_kernel(own_ref, forth_ref, hither_ref, out_ref):
    out_ref[...] = (
        own_ref[...].astype(f32) + forth_ref[...].astype(f32) + hither_ref[...].astype(f32)
    ).astype(bf16)


def input_grad_kernel(own_ref, forth_ref, hither_ref, term_ref, out_ref):
    out_ref[...] = (
        own_ref[...].astype(f32)
        + forth_ref[...].astype(f32)
        + hither_ref[...].astype(f32)
        + term_ref[...]
    ).astype(bf16)


def router_grad_kernel(count, info_ref, dots_ref, router_ref, all_ref, out_ref, term_ref):
    experts, width = out_ref.shape
    rows, toks = term_ref.shape[0], all_ref.shape[0]
    tails = all_ref[:, width:].astype(f32).T
    hits = tails[:experts]
    affinity = tails[experts : 2 * experts] + tails[2 * experts : 3 * experts]
    expert = lax.broadcasted_iota(jnp.int32, (experts, toks), 0)
    grad_gates = jnp.zeros((experts, toks), f32)
    gathered = jnp.concatenate([dots_ref[i] for i in range(count)], axis=0)
    gathered = mm_nt(gathered, token_places(count, info_ref, toks))
    for i in range(count):
        name = 2 * (info_ref[0] ^ i)
        dots = gathered[i * dots_ref.shape[1] : (i + 1) * dots_ref.shape[1]]
        grad_gates = jnp.where(expert == name, dots[0:1] + dots[1:2], grad_gates)
        grad_gates = jnp.where(expert == name + 1, dots[2:3] + dots[3:4], grad_gates)
    chosen = hits * affinity
    chosen_sum = jnp.sum(chosen, axis=0, keepdims=True)
    grad_chosen = route_scale * (
        grad_gates / chosen_sum
        - jnp.sum(grad_gates * chosen, axis=0, keepdims=True) / (chosen_sum * chosen_sum)
    )
    logits = (hits * grad_chosen * affinity * (1.0 - affinity)).astype(bf16)
    out_ref[...] = mm(logits, all_ref[:, :width])
    term_ref[...] = mm_tn(logits[:, :rows], router_ref[...])


def ring_of(count):
    if count == 8:
        order = [0, 2, 4, 6, 7, 5, 3, 1]
    else:
        order = list(range(count))
    ahead = [(order[i], order[(i + 1) % count]) for i in range(count)]
    back = [(b, a) for a, b in ahead]
    return order, ahead, back


def offsets_of(count):
    half = count // 2
    return [0] + [-k for k in range(1, half)] + list(range(1, half)) + [half]


def tie(*values):
    return lax.optimization_barrier(values)


class Ring:
    def __init__(self, count, far_ahead):
        _, ahead, back = ring_of(count)
        self.half = count // 2
        self.far, self.near = (ahead, back) if far_ahead else (back, ahead)
        self.far_ahead = far_ahead

    def gather_hop(self, far, near):
        far.append(lax.ppermute(far[-1], "expert", self.far))
        if len(near) < self.half:
            near.append(lax.ppermute(near[-1], "expert", self.near))

    def gathered(self, far, near):
        behind, front = (far, near) if self.far_ahead else (near, far)
        return behind[: self.half] + front[1 : self.half] + [far[self.half]]


def scatter_hop(parts, count, came, step):
    _, ahead, back = ring_of(count)
    half = count // 2
    if step == 0:
        front, rear = parts[-2], parts[-1]
    else:
        front, rear = parts[count - 1 - step], parts[half - step]
        front, rear = call(
            hop_kernel, [struct(front.shape)] * 2, [in_vmem] * 4,
            (front, came[0], rear, came[1]), (0, 3 * nbytes([front, rear])),
        )
    return lax.ppermute(front, "expert", ahead), lax.ppermute(rear, "expert", back)


def double(gathered, step):
    size = lax.axis_size("expert")
    came = lax.ppermute(gathered, "expert", [(i, i ^ step) for i in range(size)])
    return jnp.concatenate([gathered, came], axis=0)


def swap_cores(value):
    return lax.ppermute(value, "dp", [(0, 1), (1, 0)])


def make_per_device(count):
    order, _, _ = ring_of(count)
    offsets = offsets_of(count)
    place = [order.index(chip) for chip in range(count)]
    table = np.array(
        [[order[(place[c] + off) % count] for off in offsets] for c in range(count)], np.int32
    )

    def per_device(
        tokens,
        cotangent,
        expert_choice_index,
        capacity,
        router_matrix,
        gate_matrix,
        up_matrix,
        down_matrix,
        up_adapter_first,
        up_adapter_second,
        down_adapter_first,
        down_adapter_second,
    ):
        tok_count, width = tokens.shape
        experts = router_matrix.shape[1]
        load = width + LANES
        half = count * MOST
        slots = 2 * half
        chip, core = lax.axis_index("expert"), lax.axis_index("dp")
        chips = jnp.sum(
            jnp.where(jnp.arange(count)[:, None] == chip, jnp.asarray(table), 0), axis=0
        )
        info = jnp.concatenate([jnp.stack([chip, core, capacity[0]]), chips[:1], chips])
        info = info.astype(jnp.int32)
        gate_w, up_w, down_w = gate_matrix[0], up_matrix[0], down_matrix[0]
        up_a, up_b = up_adapter_first[0], up_adapter_second[0]
        down_a, down_b = down_adapter_first[0], down_adapter_second[0]
        hidden, rank = gate_w.shape[1], up_a.shape[1]

        toks = count * tok_count
        tiles = 4
        up_a, down_a, router = up_a.T, down_a.T, router_matrix.T
        choice = expert_choice_index.T
        ring_token, ring_cot = Ring(count, True), Ring(count, False)
        hops = count // 2
        rows_of = [tok_count] * (count - 1) + [tok_count // 2] * 2

        stay = lambda *arrays: [pltpu.with_memory_space_constraint(a, pltpu.HBM) for a in arrays]

        def fetch(*arrays):
            return call(
                functools.partial(fetch_kernel, len(arrays)),
                [pltpu.VMEM(a.shape, bf16) for a in arrays],
                [in_hbm] * len(arrays),
                stay(*arrays),
                (0, nbytes(arrays)),
                scratch=[pltpu.SemaphoreType.DMA((len(arrays),))],
                mib=1,
            )

        (token_load,) = call(
            token_load_kernel, [struct((tok_count, load))], [in_hbm] * 3,
            stay(choice, tokens, router), (0, 2 * nbytes([tokens])),
            scratch=[
                pltpu.VMEM(choice.shape, jnp.int32), pltpu.VMEM(router.shape, bf16),
                pltpu.SemaphoreType.DMA((3,)),
            ],
        )

        tok_far, tok_near = [token_load], [token_load]
        ring_token.gather_hop(tok_far, tok_near)
        cot_far, cot_near = [cotangent], [cotangent]
        ring_token.gather_hop(tok_far, tok_near)
        ring_cot.gather_hop(cot_far, cot_near)
        for hop in range(2, hops):
            ring_token.gather_hop(tok_far, tok_near)
            if hop == hops - 2:
                tok_far[-1], cot_far[1], cot_near[1] = tie(tok_far[-1], cot_far[1], cot_near[1])
                tok_near[-1], gate_late = tie(tok_near[-1], gate_w)
            if hop < hops - 1:
                ring_cot.gather_hop(cot_far, cot_near)
        gate_v, up_a_v, up_b_v = fetch(gate_late, up_a, up_b)
        token_blocks = ring_token.gathered(tok_far, tok_near)

        kept, sent, select, high, low, token_all = call(
            functools.partial(token_slots_kernel, experts),
            [struct((half, load))] * 2 + [struct((slots, toks))] * 3 + [struct((toks, load))],
            [in_smem] + [in_vmem] * (count + 1),
            (info, gate_v, *token_blocks),
            (2 * slots * toks * load, 2 * count * nbytes([token_load])),
        )
        sent, cot_far[-1], cot_near[-1] = tie(sent, cot_far[-1], cot_near[-1])
        came = swap_cores(sent)
        ring_cot.gather_hop(cot_far, cot_near)
        inner, slope, active, low_up, keep = call(
            functools.partial(inner_kernel, count, tiles),
            [
                struct((slots, hidden)), struct((slots, hidden), f32), struct((slots, hidden), f32),
                struct((slots, rank)), struct((slots, LANES), f32),
            ],
            [in_smem] + [in_vmem] * 5 + [in_hbm],
            (info, kept, came, gate_v, up_a_v, up_b_v, *stay(up_w)),
            (4 * slots * width * hidden, 2 * nbytes([gate_w])),
            scratch=[
                pltpu.VMEM((slots, width), bf16), pltpu.VMEM(up_w.shape, bf16),
                pltpu.SemaphoreType.DMA((1,)),
            ],
            mib=16,
        )
        inner, cot_far[-1], cot_near[-1] = tie(inner, cot_far[-1], cot_near[-1])
        while len(cot_far) <= hops:
            ring_cot.gather_hop(cot_far, cot_near)
        routed_kept, routed_sent, low_down = call(
            functools.partial(routed_kernel, tiles),
            [struct((half, width))] * 2 + [struct((slots, rank))],
            [in_vmem] * 5,
            (inner, keep, down_w, down_a, down_b),
            (2 * slots * width * hidden, nbytes([gate_w])),
        )
        routed_sent, high, cot_far[-1] = tie(routed_sent, high, cot_far[-1])
        routed_came = swap_cores(routed_sent)
        cot_blocks = ring_cot.gathered(cot_far, cot_near)
        cot_kept, cot_sent, cot_all = call(
            cot_slots_kernel,
            [struct((half, width))] * 2 + [struct((toks, width))],
            [in_vmem] * (count + 2),
            (high, low, *cot_blocks),
            (4 * slots * toks * load, 2 * count * nbytes([token_load])),
        )
        cot_came = swap_cores(cot_sent)
        routed_came, cot_kept = tie(routed_came, cot_kept)

        mix_parts = call(
            mix_parts_kernel,
            [struct((rows, width)) for rows in rows_of],
            [in_vmem] * 4,
            (high, low, routed_kept, routed_came),
            (4 * slots * toks * load, 3 * count * nbytes([token_load])),
            scratch=[pltpu.VMEM((slots, width), bf16)],
        )
        mix_parts = list(mix_parts)
        cot_came, mix_parts[-1] = tie(cot_came, mix_parts[-1])
        mix_came = [scatter_hop(mix_parts, count, None, 0)]

        grad_routed, grad_gate, grad_up, back_low, back_up = call(
            functools.partial(inner_grad_kernel, tiles),
            [struct((slots, width))] + [struct((slots, hidden))] * 2 + [struct((slots, rank))] * 2,
            [in_vmem] * 9,
            (cot_kept, cot_came, keep, down_w, down_b, down_a, slope, active, up_b_v),
            (2 * slots * width * hidden, nbytes([gate_w])),
        )
        grad_up, *mix_came[0] = tie(grad_up, *mix_came[0])
        mix_came.append(scatter_hop(mix_parts, count, mix_came[0], 1))
        back_kept, back_sent = call(
            functools.partial(row_grad_kernel, tiles),
            [struct((half, width))] * 2,
            [in_vmem] * 6,
            (grad_gate, grad_up, back_up, gate_v, up_w, up_a_v),
            (4 * slots * width * hidden, 2 * nbytes([gate_w])),
        )
        back_sent, *mix_came[1] = tie(back_sent, *mix_came[1])
        back_came = swap_cores(back_sent)
        mix_came.append(scatter_hop(mix_parts, count, mix_came[1], 2))
        back_parts = call(
            back_parts_kernel,
            [struct((rows, width)) for rows in rows_of],
            [in_vmem] * 3,
            (select, back_kept, back_came),
            (2 * slots * toks * load, 2 * count * nbytes([token_load])),
            scratch=[pltpu.VMEM((slots, width), bf16)],
        )
        back_parts = list(back_parts)
        routed_came, *mix_came[2] = tie(routed_came, *mix_came[2])
        back_came = [scatter_hop(back_parts, count, None, 0)]
        (dots,) = call(
            functools.partial(gate_grad_kernel, count),
            [struct((1, 2 * 8, toks))],
            [in_smem] + [in_vmem] * 4,
            (info, select, routed_kept, routed_came, cot_all),
            (2 * slots * toks * load, 2 * count * nbytes([token_load])),
            scratch=[pltpu.VMEM((slots, width), bf16)],
        )
        step = 1
        back_up_late = back_up
        for hop in range(1, hops):
            if hop + 2 < hops:
                mix_came.append(scatter_hop(mix_parts, count, mix_came[-1], hop + 2))
            if hop == hops - 1:
                tied = tie(*back_came[-1], back_up_late, dots, *mix_came[-1])
                mix_came[-1] = tied[4:]
            else:
                tied = tie(*back_came[-1], back_up_late, dots)
            back_came[-1], back_up_late, dots = tied[:2], tied[2], tied[3]
            if hop == 1:
                adapters = call(
                    adapter_kernel,
                    [
                        struct((rank, width)), struct((rank, hidden)),
                        struct((rank, hidden)), struct((rank, width)),
                    ],
                    [in_vmem] * 9,
                    (kept, came, back_up_late, low_up, grad_up, inner, back_low, low_down,
                     grad_routed),
                    (8 * slots * width * rank, 4 * nbytes([grad_routed])),
                    out_specs=[pl.BlockSpec()] * 4,
                )
                adapters = list(adapters)
            if hop == 2:
                *back_came[-1], adapters[1] = tie(*back_came[-1], adapters[1])
            back_came.append(scatter_hop(back_parts, count, back_came[-1], hop))
            if step < count:
                dots = double(dots, step)
                step *= 2
        while step < count:
            dots = double(dots, step)
            step *= 2
        adapters = (adapters[0].T, adapters[1], adapters[2].T, adapters[3])

        (mixed,) = call(
            mixed_kernel,
            [struct((tok_count, width))],
            [in_vmem] * 3,
            (mix_parts[0], *mix_came[-1]),
            (0, 4 * nbytes([token_load])),
            out_specs=[pl.BlockSpec()],
        )
        router_half, router_term = call(
            functools.partial(router_grad_kernel, count),
            [struct((experts, width), f32), struct((tok_count, width), f32)],
            [in_smem] + [in_vmem] * 3,
            (info, dots, router, token_all),
            (0, count * nbytes([token_load])),
        )
        router_grad = (router_half + swap_cores(router_half)).T
        (input_grad,) = call(
            input_grad_kernel,
            [struct((tok_count, width))],
            [in_vmem] * 4,
            (back_parts[0], *back_came[-1], router_term),
            (0, 4 * nbytes([token_load])),
            out_specs=[pl.BlockSpec()],
        )
        return (mixed, input_grad, router_grad) + tuple(value[None] for value in adapters)

    return per_device


def solution(mesh):
    rows = P(("groups", "expert", "dp"), None)
    whole = P(("groups", "expert", "dp"), None, None)
    weight = P(("expert", "dp"), None, None)
    return jax.shard_map(
        make_per_device(mesh.shape["expert"]),
        mesh=mesh,
        in_specs=(rows, rows, rows, P(("groups", "expert", "dp")), P()) + (weight,) * 7,
        out_specs=(rows, rows, P("groups", None), whole, whole, whole, whole),
        check_vma=False,
    )
```

```python
import functools

import jax
import jax.numpy as jnp
import numpy as np
from jax import lax
from jax.experimental import pallas as pl
from jax.experimental.pallas import tpu as pltpu
from jax.sharding import PartitionSpec as P

MOST = 16
LANES = 128
COST_SHARE = 10**6

route_scale = 2.5
adapter_scale = 2.0

bf16, f32 = jnp.bfloat16, jnp.float32
in_vmem = pl.BlockSpec(memory_space=pltpu.VMEM)
in_hbm = pl.BlockSpec(memory_space=pltpu.HBM)
in_smem = pl.BlockSpec(memory_space=pltpu.SMEM)


def mm(left, right, axes=((1,), (0,))):
    return lax.dot_general(
        left, right, ((axes[0], axes[1]), ((), ())), preferred_element_type=jnp.float32
    )


def mm_nt(left, right):
    return mm(left, right, ((1,), (1,)))


def mm_tn(left, right):
    return mm(left, right, ((0,), (0,)))


def call(body, outs, specs, operands, cost, scratch=(), mib=8, out_specs=None):
    flops, moved = cost
    return pl.pallas_call(
        body,
        out_shape=outs,
        in_specs=specs,
        out_specs=out_specs if out_specs is not None else [in_vmem] * len(outs),
        scratch_shapes=list(scratch),
        compiler_params=pltpu.CompilerParams(vmem_limit_bytes=mib * 2**20),
        cost_estimate=pl.CostEstimate(
            flops=flops // COST_SHARE, bytes_accessed=moved // COST_SHARE, transcendentals=0
        ),
    )(*operands)


def struct(shape, dtype=bf16):
    return jax.ShapeDtypeStruct(shape, dtype)


def nbytes(arrays):
    return sum(a.size * a.dtype.itemsize for a in arrays)


def pieces(total, size):
    return [(at, min(size, total - at)) for at in range(0, total, size)]


def start_all(copies):
    for copy in copies:
        copy.start()


def token_load_kernel(
    choice_hbm, tokens_hbm, router_hbm, load_ref, choice_ref, router_ref, sems
):
    width, experts = tokens_hbm.shape[1], router_ref.shape[0]
    copies = [
        pltpu.make_async_copy(choice_hbm, choice_ref, sems.at[0]),
        pltpu.make_async_copy(tokens_hbm, load_ref.at[:, pl.ds(0, width)], sems.at[1]),
        pltpu.make_async_copy(router_hbm, router_ref, sems.at[2]),
    ]
    start_all(copies)
    copies[0].wait()
    expert = lax.broadcasted_iota(jnp.int32, (LANES, choice_ref.shape[1]), 0)
    hits = jnp.zeros(expert.shape, f32)
    for k in range(choice_ref.shape[0]):
        hits += jnp.where(choice_ref[k : k + 1] == expert, 1.0, 0.0)
    load_ref[:, width:] = hits.T.astype(bf16)
    copies[1].wait()
    copies[2].wait()
    affinity = jax.nn.sigmoid(mm_nt(load_ref[:, :width], router_ref[...]))
    high = affinity.astype(bf16)
    load_ref[:, width + experts : width + 2 * experts] = high
    load_ref[:, width + 2 * experts : width + 3 * experts] = (affinity - high.astype(f32)).astype(bf16)


def fetch_kernel(count, *refs):
    sources, outs, sems = refs[:count], refs[count : 2 * count], refs[-1]
    copies = [
        pltpu.make_async_copy(source, out, sems.at[i])
        for i, (source, out) in enumerate(zip(sources, outs))
    ]
    start_all(copies)
    for copy in copies:
        copy.wait()


def assemble(refs, all_ref):
    at = 0
    for ref in refs:
        all_ref[pl.ds(at, ref.shape[0])] = ref[...]
        at += ref.shape[0]


def expert_names(info_ref, slots):
    mine = 2 * info_ref[0] + info_ref[1]
    other = 2 * info_ref[0] + 1 - info_ref[1]
    slot = lax.broadcasted_iota(jnp.int32, (slots, LANES), 0)
    lane = lax.broadcasted_iota(jnp.int32, (slots, LANES), 1)
    return jnp.where(lane == jnp.where(slot < slots // 2, mine, other), 1.0, 0.0).astype(bf16)


def token_slots_kernel(experts, info_ref, *refs):
    blocks, (kept_ref, sent_ref, select_ref, high_ref, low_ref, all_ref) = refs[1:-6], refs[-6:]
    rows, load = blocks[0].shape
    toks, slots = all_ref.shape[0], select_ref.shape[0]
    half, width = slots // 2, load - LANES
    assemble(blocks, all_ref)
    tails = all_ref[:, width:]
    names = expert_names(info_ref, slots)
    slot = lax.broadcasted_iota(jnp.int32, (slots, toks), 0)
    tok = lax.broadcasted_iota(jnp.int32, (slots, toks), 1)
    slot = jnp.where(slot < half, slot, slot - half)
    member = jnp.where(slot // MOST == tok // rows, mm_nt(names, tails), 0.0)
    early = lax.broadcasted_iota(jnp.int32, (toks, toks), 0)
    late = lax.broadcasted_iota(jnp.int32, (toks, toks), 1)
    before = mm(member.astype(bf16), jnp.where(early < late, 1.0, 0.0).astype(bf16))
    select = jnp.where(before == (slot % MOST).astype(f32), member, 0.0)
    select_ref[...] = select.astype(bf16)
    for at, size in pieces(load, 4 * LANES):
        out = mm(select_ref[...], all_ref[:, at : at + size]).astype(bf16)
        kept_ref[:, at : at + size] = out[:half]
        sent_ref[:, at : at + size] = out[half:]
    lane = lax.broadcasted_iota(jnp.int32, (LANES, LANES), 0)
    expert = lax.broadcasted_iota(jnp.int32, (LANES, LANES), 1)
    parts = (lane == expert + experts) | (lane == expert + 2 * experts)
    affinity = mm(tails, jnp.where(parts & (expert < experts), 1.0, 0.0).astype(bf16))
    mine = lax.broadcasted_iota(jnp.int32, (toks, LANES), 1) < experts
    chosen = jnp.where(mine, tails.astype(f32) * affinity, 0.0)
    gates = route_scale * chosen / jnp.sum(chosen, axis=1, keepdims=True)
    high = gates.astype(bf16)
    low = (gates - high.astype(f32)).astype(bf16)
    high_ref[...] = (select * mm_nt(names, high)).astype(bf16)
    low_ref[...] = (select * mm_nt(names, low)).astype(bf16)


def cot_slots_kernel(high_ref, low_ref, *refs):
    blocks, (kept_ref, sent_ref, all_ref) = refs[:-3], refs[-3:]
    half, width = kept_ref.shape
    assemble(blocks, all_ref)
    for at, size in pieces(width, 4 * LANES):
        cot = all_ref[:, at : at + size]
        out = (mm(high_ref[...], cot) + mm(low_ref[...], cot)).astype(bf16)
        kept_ref[:, at : at + size] = out[:half]
        sent_ref[:, at : at + size] = out[half:]


def inner_kernel(
    count, tiles, info_ref, kept_ref, came_ref, gate_ref, up_a_ref, up_b_ref, up_hbm,
    inner_ref, slope_ref, active_ref, low_up_ref, keep_ref, rows_ref, up_ref, sems,
):
    half, width = kept_ref.shape[0], rows_ref.shape[1]
    slots, tile = 2 * half, gate_ref.shape[1] // tiles
    copy = pltpu.make_async_copy(up_hbm, up_ref, sems.at[0])
    copy.start()
    rows_ref[:half] = kept_ref[:, :width]
    rows_ref[half:] = came_ref[:, :width]
    low_up_ref[...] = mm_nt(rows_ref[...], up_a_ref[...]).astype(bf16)
    chip, core = info_ref[0], info_ref[1]
    lane = lax.broadcasted_iota(jnp.int32, (slots, LANES), 1)
    tails = jnp.concatenate([kept_ref[:, width:], came_ref[:, width:]], axis=0).astype(f32)
    valid = jnp.sum(jnp.where(lane == 2 * chip + core, tails, 0.0), axis=1, keepdims=True)
    here = lax.broadcasted_iota(jnp.int32, (slots, 1), 0)
    there = lax.broadcasted_iota(jnp.int32, (1, slots), 1)
    source_here = jnp.zeros((slots, 1), jnp.int32)
    source_there = jnp.zeros((1, slots), jnp.int32)
    for i in range(2 * count):
        source = 2 * info_ref[4 + i % count] + (core if i < count else 1 - core)
        source_here = jnp.where(here // MOST == i, source, source_here)
        source_there = jnp.where(there // MOST == i, source, source_there)
    ahead = jnp.where(source_there < source_here, 1.0, 0.0).astype(bf16)
    spread = jnp.broadcast_to(valid, (slots, LANES)).astype(bf16)
    rank = mm(ahead, spread) + (here % MOST).astype(f32)
    keep_ref[...] = jnp.where(rank < info_ref[2].astype(f32), valid, 0.0)
    for j in range(tiles):
        cols = slice(j * tile, (j + 1) * tile)
        pre_gate = mm(rows_ref[...], gate_ref[:, cols])
        logistic = jax.nn.sigmoid(pre_gate)
        active_ref[:, cols] = pre_gate * logistic
        slope_ref[:, cols] = logistic * (1.0 + pre_gate * (1.0 - logistic))
    copy.wait()
    for j in range(tiles):
        cols = slice(j * tile, (j + 1) * tile)
        pre_up = mm(rows_ref[...], up_ref[:, cols]) + adapter_scale * mm(
            low_up_ref[...], up_b_ref[:, cols]
        )
        keep = jnp.concatenate([keep_ref[...]] * (tile // LANES), axis=1)
        active = keep * active_ref[:, cols]
        active_ref[:, cols] = active
        slope_ref[:, cols] = slope_ref[:, cols] * (keep * pre_up)
        inner_ref[:, cols] = (active * pre_up).astype(bf16)


def routed_kernel(
    tiles, inner_ref, down_ref, down_a_ref, down_b_ref, kept_ref, sent_ref, low_down_ref
):
    half, tile = kept_ref.shape[0], down_ref.shape[1] // tiles
    low_down_ref[...] = mm_nt(inner_ref[...], down_a_ref[...]).astype(bf16)
    for j in range(tiles):
        cols = slice(j * tile, (j + 1) * tile)
        value = mm(inner_ref[...], down_ref[:, cols]) + adapter_scale * mm(
            low_down_ref[...], down_b_ref[:, cols]
        )
        value = value.astype(bf16)
        kept_ref[:, cols] = value[:half]
        sent_ref[:, cols] = value[half:]


def write_parts(outs, at, size, part):
    row = 0
    for ref in outs:
        ref[:, at : at + size] = part[row : row + ref.shape[0]]
        row += ref.shape[0]


def mix_parts_kernel(high_ref, low_ref, kept_ref, came_ref, *refs):
    outs, (rows_ref,) = refs[:-1], refs[-1:]
    half, width = kept_ref.shape
    rows_ref[:half] = kept_ref[...]
    rows_ref[half:] = came_ref[...]
    high = high_ref[...].astype(f32).T.astype(bf16)
    low = low_ref[...].astype(f32).T.astype(bf16)
    for at, size in pieces(width, 4 * LANES):
        rows = rows_ref[:, at : at + size]
        write_parts(outs, at, size, (mm(high, rows) + mm(low, rows)).astype(bf16))


def token_places(count, info_ref, toks):
    rows = toks // count
    here = lax.broadcasted_iota(jnp.int32, (toks, toks), 0)
    place = jnp.zeros((toks, toks), jnp.int32)
    for i in range(count):
        place = jnp.where(here // rows == i, rows * (info_ref[4 + i] - i) + here, place)
    return jnp.where(place == lax.broadcasted_iota(jnp.int32, (toks, toks), 1), 1.0, 0.0).astype(bf16)


def gate_grad_kernel(count, info_ref, select_ref, kept_ref, came_ref, all_ref, out_ref, rows_ref):
    half = kept_ref.shape[0]
    rows_ref[:half] = kept_ref[...]
    rows_ref[half:] = came_ref[...]
    dots = select_ref[...].astype(f32) * mm_nt(rows_ref[...], all_ref[...])
    own = jnp.sum(dots[:half], axis=0, keepdims=True)
    other = jnp.sum(dots[half:], axis=0, keepdims=True)
    first = info_ref[1] == 0
    row = lax.broadcasted_iota(jnp.int32, out_ref.shape[1:], 0)
    out = jnp.zeros(out_ref.shape[1:], f32)
    for i, value in enumerate((jnp.where(first, own, other), jnp.where(first, other, own))):
        high = value.astype(bf16).astype(f32)
        out = jnp.where(row == 2 * i, high, jnp.where(row == 2 * i + 1, value - high, out))
    out_ref[0] = mm(out.astype(bf16), token_places(count, info_ref, out.shape[1])).astype(bf16)


def back_parts_kernel(select_ref, kept_ref, came_ref, *refs):
    outs, (rows_ref,) = refs[:-1], refs[-1:]
    width, half = kept_ref.shape[1], kept_ref.shape[0]
    rows_ref[:half] = kept_ref[...]
    rows_ref[half:] = came_ref[...]
    select = select_ref[...].astype(f32).T.astype(bf16)
    for at, size in pieces(width, 4 * LANES):
        write_parts(outs, at, size, mm(select, rows_ref[:, at : at + size]).astype(bf16))


def inner_grad_kernel(
    tiles, kept_ref, came_ref, down_ref, down_b_ref, down_a_ref, slope_ref, active_ref,
    up_b_ref, grad_ref, gate_out_ref, up_out_ref, back_low_ref, back_up_ref,
):
    half, tile = kept_ref.shape[0], down_ref.shape[0] // tiles
    grad_ref[:half] = kept_ref[...]
    grad_ref[half:] = came_ref[...]
    back_low_ref[...] = mm_nt(grad_ref[...], down_b_ref[...]).astype(bf16)
    for j in range(tiles):
        cols = slice(j * tile, (j + 1) * tile)
        inner = mm_nt(grad_ref[...], down_ref[cols]) + adapter_scale * mm(
            back_low_ref[...], down_a_ref[:, cols]
        )
        gate_out_ref[:, cols] = (inner * slope_ref[:, cols]).astype(bf16)
        up_out_ref[:, cols] = (inner * active_ref[:, cols]).astype(bf16)
    back_up_ref[...] = mm_nt(up_out_ref[...], up_b_ref[...]).astype(bf16)


def row_grad_kernel(
    tiles, grad_gate_ref, grad_up_ref, back_up_ref, gate_ref, up_ref, up_a_ref, kept_ref, sent_ref
):
    half, tile = kept_ref.shape[0], gate_ref.shape[0] // tiles
    for j in range(tiles):
        cols = slice(j * tile, (j + 1) * tile)
        value = (
            mm_nt(grad_gate_ref[...], gate_ref[cols])
            + mm_nt(grad_up_ref[...], up_ref[cols])
            + adapter_scale * mm(back_up_ref[...], up_a_ref[:, cols])
        ).astype(bf16)
        kept_ref[:, cols] = value[:half]
        sent_ref[:, cols] = value[half:]


def adapter_kernel(
    kept_ref, came_ref, back_up_ref, low_up_ref, grad_up_ref, inner_ref, back_low_ref,
    low_down_ref, grad_ref, up_a_ref, up_b_ref, down_a_ref, down_b_ref,
):
    width, half = grad_ref.shape[1], kept_ref.shape[0]
    scaled = lambda value: (adapter_scale * value).astype(bf16)
    back_up = back_up_ref[...]
    for at, size in pieces(width, 4 * LANES):
        cols = slice(at, at + size)
        up_a_ref[:, cols] = scaled(
            mm_tn(back_up[:half], kept_ref[:, cols]) + mm_tn(back_up[half:], came_ref[:, cols])
        )
        down_b_ref[:, cols] = scaled(mm_tn(low_down_ref[...], grad_ref[:, cols]))
    up_b_ref[...] = scaled(mm_tn(low_up_ref[...], grad_up_ref[...]))
    down_a_ref[...] = scaled(mm_tn(back_low_ref[...], inner_ref[...]))


def halves_kernel(behind_ref, front_ref, top_ref, low_ref):
    rows = top_ref.shape[0]
    top_ref[...] = behind_ref[:rows]
    low_ref[...] = front_ref[rows:]


def hop_kernel(front_ref, forth_ref, rear_ref, hither_ref, front_out_ref, rear_out_ref):
    rows, came = front_ref.shape[0], forth_ref.shape[0]
    plus = lambda a, b: (a[...].astype(f32) + b[...].astype(f32)).astype(bf16)
    if came < rows:
        front_out_ref[came:] = front_ref[came:]
        rear_out_ref[: rows - came] = rear_ref[: rows - came]
    front_out_ref[:came] = plus(front_ref.at[:came], forth_ref)
    rear_out_ref[rows - came :] = plus(rear_ref.at[rows - came :], hither_ref)


def mixed_kernel(own_ref, forth_ref, hither_ref, out_ref):
    out_ref[...] = (
        own_ref[...].astype(f32) + forth_ref[...].astype(f32) + hither_ref[...].astype(f32)
    ).astype(bf16)


def input_grad_kernel(own_ref, forth_ref, hither_ref, term_ref, out_ref):
    out_ref[...] = (
        own_ref[...].astype(f32)
        + forth_ref[...].astype(f32)
        + hither_ref[...].astype(f32)
        + term_ref[...]
    ).astype(bf16)


def router_grad_kernel(count, info_ref, dots_ref, router_ref, all_ref, out_ref, term_ref):
    experts, width = out_ref.shape
    rows, toks = term_ref.shape[0], all_ref.shape[0]
    tails = all_ref[:, width:].astype(f32).T
    hits = tails[:experts]
    affinity = tails[experts : 2 * experts] + tails[2 * experts : 3 * experts]
    expert = lax.broadcasted_iota(jnp.int32, (experts, toks), 0)
    grad_gates = jnp.zeros((experts, toks), f32)
    gathered = jnp.concatenate([dots_ref[i] for i in range(count)], axis=0)
    gathered = mm_nt(gathered, token_places(count, info_ref, toks))
    for i in range(count):
        name = 2 * (info_ref[0] ^ i)
        dots = gathered[i * dots_ref.shape[1] : (i + 1) * dots_ref.shape[1]]
        grad_gates = jnp.where(expert == name, dots[0:1] + dots[1:2], grad_gates)
        grad_gates = jnp.where(expert == name + 1, dots[2:3] + dots[3:4], grad_gates)
    chosen = hits * affinity
    chosen_sum = jnp.sum(chosen, axis=0, keepdims=True)
    grad_chosen = route_scale * (
        grad_gates / chosen_sum
        - jnp.sum(grad_gates * chosen, axis=0, keepdims=True) / (chosen_sum * chosen_sum)
    )
    logits = (hits * grad_chosen * affinity * (1.0 - affinity)).astype(bf16)
    out_ref[...] = mm(logits, all_ref[:, :width])
    term_ref[...] = mm_tn(logits[:, :rows], router_ref[...])


def ring_of(count):
    if count == 8:
        order = [0, 2, 4, 6, 7, 5, 3, 1]
    else:
        order = list(range(count))
    ahead = [(order[i], order[(i + 1) % count]) for i in range(count)]
    back = [(b, a) for a, b in ahead]
    return order, ahead, back


def offsets_of(count):
    half = count // 2
    return [0] + [-k for k in range(1, half)] + list(range(1, half)) + [half]


def tie(*values):
    return lax.optimization_barrier(values)


class Ring:
    def __init__(self, count, far_ahead):
        _, ahead, back = ring_of(count)
        self.half = count // 2
        self.far, self.near = (ahead, back) if far_ahead else (back, ahead)
        self.far_ahead = far_ahead

    def gather_hop(self, far, near):
        far.append(lax.ppermute(far[-1], "expert", self.far))
        if len(near) < self.half:
            near.append(lax.ppermute(near[-1], "expert", self.near))

    def last_hop(self, far, near):
        ahead, back = (self.far, self.near) if self.far_ahead else (self.near, self.far)
        behind, front = (far, near) if self.far_ahead else (near, far)
        rows, columns = far[-1].shape
        top, low = call(
            halves_kernel, [struct((rows // 2, columns))] * 2, [in_vmem] * 2,
            (behind[-1], front[-1]), (0, nbytes([far[-1]])),
        )
        return lax.ppermute(top, "expert", ahead), lax.ppermute(low, "expert", back)

    def gathered(self, far, near, *opposite):
        behind, front = (far, near) if self.far_ahead else (near, far)
        return behind[: self.half] + front[1 : self.half] + list(opposite or [far[self.half]])


def scatter_hop(parts, count, came, step):
    _, ahead, back = ring_of(count)
    half = count // 2
    if step == 0:
        front, rear = parts[-2], parts[-1]
    else:
        front, rear = parts[count - 1 - step], parts[half - step]
        front, rear = call(
            hop_kernel, [struct(front.shape)] * 2, [in_vmem] * 4,
            (front, came[0], rear, came[1]), (0, 3 * nbytes([front, rear])),
        )
    return lax.ppermute(front, "expert", ahead), lax.ppermute(rear, "expert", back)


def double(gathered, step):
    size = lax.axis_size("expert")
    came = lax.ppermute(gathered, "expert", [(i, i ^ step) for i in range(size)])
    return jnp.concatenate([gathered, came], axis=0)


def swap_cores(value):
    return lax.ppermute(value, "dp", [(0, 1), (1, 0)])


def make_per_device(count):
    order, _, _ = ring_of(count)
    offsets = offsets_of(count)
    place = [order.index(chip) for chip in range(count)]
    table = np.array(
        [[order[(place[c] + off) % count] for off in offsets] for c in range(count)], np.int32
    )

    def per_device(
        tokens,
        cotangent,
        expert_choice_index,
        capacity,
        router_matrix,
        gate_matrix,
        up_matrix,
        down_matrix,
        up_adapter_first,
        up_adapter_second,
        down_adapter_first,
        down_adapter_second,
    ):
        tok_count, width = tokens.shape
        experts = router_matrix.shape[1]
        load = width + LANES
        half = count * MOST
        slots = 2 * half
        chip, core = lax.axis_index("expert"), lax.axis_index("dp")
        chips = jnp.sum(
            jnp.where(jnp.arange(count)[:, None] == chip, jnp.asarray(table), 0), axis=0
        )
        info = jnp.concatenate([jnp.stack([chip, core, capacity[0]]), chips[:1], chips])
        info = info.astype(jnp.int32)
        gate_w, up_w, down_w = gate_matrix[0], up_matrix[0], down_matrix[0]
        up_a, up_b = up_adapter_first[0], up_adapter_second[0]
        down_a, down_b = down_adapter_first[0], down_adapter_second[0]
        hidden, rank = gate_w.shape[1], up_a.shape[1]

        toks = count * tok_count
        tiles = 4
        up_a, down_a, router = up_a.T, down_a.T, router_matrix.T
        choice = expert_choice_index.T
        ring_token, ring_cot = Ring(count, True), Ring(count, False)
        hops = count // 2
        rows_of = [tok_count] * (count - 1) + [tok_count // 2] * 2

        stay = lambda *arrays: [pltpu.with_memory_space_constraint(a, pltpu.HBM) for a in arrays]

        def fetch(*arrays):
            return call(
                functools.partial(fetch_kernel, len(arrays)),
                [pltpu.VMEM(a.shape, bf16) for a in arrays],
                [in_hbm] * len(arrays),
                stay(*arrays),
                (0, nbytes(arrays)),
                scratch=[pltpu.SemaphoreType.DMA((len(arrays),))],
                mib=1,
            )

        (token_load,) = call(
            token_load_kernel, [struct((tok_count, load))], [in_hbm] * 3,
            stay(choice, tokens, router), (0, 2 * nbytes([tokens])),
            scratch=[
                pltpu.VMEM(choice.shape, jnp.int32), pltpu.VMEM(router.shape, bf16),
                pltpu.SemaphoreType.DMA((3,)),
            ],
        )

        tok_far, tok_near = [token_load], [token_load]
        ring_token.gather_hop(tok_far, tok_near)
        cot_far, cot_near = [cotangent], [cotangent]
        tok_near[-1], info = tie(tok_near[-1], info)
        ring_token.gather_hop(tok_far, tok_near)
        ring_cot.gather_hop(cot_far, cot_near)
        for hop in range(2, hops):
            ring_token.gather_hop(tok_far, tok_near)
            if hop == hops - 2:
                tok_far[-1], cot_far[1], cot_near[1] = tie(tok_far[-1], cot_far[1], cot_near[1])
                tok_near[-1], gate_late = tie(tok_near[-1], gate_w)
            if hop < hops - 1:
                ring_cot.gather_hop(cot_far, cot_near)
        gate_v, up_a_v, up_b_v = fetch(gate_late, up_a, up_b)
        token_blocks = ring_token.gathered(tok_far, tok_near)

        kept, sent, select, high, low, token_all = call(
            functools.partial(token_slots_kernel, experts),
            [struct((half, load))] * 2 + [struct((slots, toks))] * 3 + [struct((toks, load))],
            [in_smem] + [in_vmem] * (count + 1),
            (info, gate_v, *token_blocks),
            (2 * slots * toks * load, 2 * count * nbytes([token_load])),
        )
        sent, cot_far[-1], cot_near[-1] = tie(sent, cot_far[-1], cot_near[-1])
        came = swap_cores(sent)
        ring_cot.gather_hop(cot_far, cot_near)
        inner, slope, active, low_up = call(
            functools.partial(inner_kernel, count, tiles),
            [
                struct((slots, hidden)), struct((slots, hidden), f32), struct((slots, hidden), f32),
                struct((slots, rank)),
            ],
            [in_smem] + [in_vmem] * 5 + [in_hbm],
            (info, kept, came, gate_v, up_a_v, up_b_v, *stay(up_w)),
            (4 * slots * width * hidden, 2 * nbytes([gate_w])),
            scratch=[
                pltpu.VMEM((slots, LANES), f32), pltpu.VMEM((slots, width), bf16),
                pltpu.VMEM(up_w.shape, bf16),
                pltpu.SemaphoreType.DMA((1,)),
            ],
            mib=16,
        )
        inner, cot_far[-1], cot_near[-1] = tie(inner, cot_far[-1], cot_near[-1])
        cot_top, cot_low = ring_cot.last_hop(cot_far, cot_near)
        routed_kept, routed_sent, low_down = call(
            functools.partial(routed_kernel, tiles),
            [struct((half, width))] * 2 + [struct((slots, rank))],
            [in_vmem] * 4,
            (inner, down_w, down_a, down_b),
            (2 * slots * width * hidden, nbytes([gate_w])),
        )
        routed_sent, high, cot_top, cot_low = tie(routed_sent, high, cot_top, cot_low)
        routed_came = swap_cores(routed_sent)
        cot_blocks = ring_cot.gathered(cot_far, cot_near, cot_top, cot_low)
        cot_kept, cot_sent, cot_all = call(
            cot_slots_kernel,
            [struct((half, width))] * 2 + [struct((toks, width))],
            [in_vmem] * (count + 3),
            (high, low, *cot_blocks),
            (4 * slots * toks * load, 2 * count * nbytes([token_load])),
        )
        cot_came = swap_cores(cot_sent)
        routed_came, cot_kept = tie(routed_came, cot_kept)

        mix_parts = call(
            mix_parts_kernel,
            [struct((rows, width)) for rows in rows_of],
            [in_vmem] * 4,
            (high, low, routed_kept, routed_came),
            (4 * slots * toks * load, 3 * count * nbytes([token_load])),
            scratch=[pltpu.VMEM((slots, width), bf16)],
        )
        mix_parts = list(mix_parts)
        cot_came, mix_parts[-1] = tie(cot_came, mix_parts[-1])
        mix_came = [scatter_hop(mix_parts, count, None, 0)]

        grad_routed, grad_gate, grad_up, back_low, back_up = call(
            functools.partial(inner_grad_kernel, tiles),
            [struct((slots, width))] + [struct((slots, hidden))] * 2 + [struct((slots, rank))] * 2,
            [in_vmem] * 8,
            (cot_kept, cot_came, down_w, down_b, down_a, slope, active, up_b_v),
            (2 * slots * width * hidden, nbytes([gate_w])),
        )
        grad_up, *mix_came[0] = tie(grad_up, *mix_came[0])
        mix_came.append(scatter_hop(mix_parts, count, mix_came[0], 1))
        back_kept, back_sent = call(
            functools.partial(row_grad_kernel, tiles),
            [struct((half, width))] * 2,
            [in_vmem] * 6,
            (grad_gate, grad_up, back_up, gate_v, up_w, up_a_v),
            (4 * slots * width * hidden, 2 * nbytes([gate_w])),
        )
        back_sent, *mix_came[1] = tie(back_sent, *mix_came[1])
        back_came = swap_cores(back_sent)
        mix_came.append(scatter_hop(mix_parts, count, mix_came[1], 2))
        back_parts = call(
            back_parts_kernel,
            [struct((rows, width)) for rows in rows_of],
            [in_vmem] * 3,
            (select, back_kept, back_came),
            (2 * slots * toks * load, 2 * count * nbytes([token_load])),
            scratch=[pltpu.VMEM((slots, width), bf16)],
        )
        back_parts = list(back_parts)
        routed_came, *mix_came[2] = tie(routed_came, *mix_came[2])
        back_came = [scatter_hop(back_parts, count, None, 0)]
        (dots,) = call(
            functools.partial(gate_grad_kernel, count),
            [struct((1, 2 * 8, toks))],
            [in_smem] + [in_vmem] * 4,
            (info, select, routed_kept, routed_came, cot_all),
            (2 * slots * toks * load, 2 * count * nbytes([token_load])),
            scratch=[pltpu.VMEM((slots, width), bf16)],
        )
        step = 1
        back_up_late = back_up
        for hop in range(1, hops):
            if hop + 2 < hops:
                mix_came.append(scatter_hop(mix_parts, count, mix_came[-1], hop + 2))
            if hop == hops - 1:
                tied = tie(*back_came[-1], back_up_late, dots, *mix_came[-1])
                mix_came[-1] = tied[4:]
            else:
                tied = tie(*back_came[-1], back_up_late, dots)
            back_came[-1], back_up_late, dots = tied[:2], tied[2], tied[3]
            if hop == 1:
                adapters = call(
                    adapter_kernel,
                    [
                        struct((rank, width)), struct((rank, hidden)),
                        struct((rank, hidden)), struct((rank, width)),
                    ],
                    [in_vmem] * 9,
                    (kept, came, back_up_late, low_up, grad_up, inner, back_low, low_down,
                     grad_routed),
                    (8 * slots * width * rank, 4 * nbytes([grad_routed])),
                    out_specs=[pl.BlockSpec()] * 4,
                )
                adapters = list(adapters)
            if hop == 2:
                *back_came[-1], adapters[1] = tie(*back_came[-1], adapters[1])
            back_came.append(scatter_hop(back_parts, count, back_came[-1], hop))
            if step < count:
                dots = double(dots, step)
                step *= 2
        while step < count:
            dots = double(dots, step)
            step *= 2
        adapters = (adapters[0].T, adapters[1], adapters[2].T, adapters[3])

        (mixed,) = call(
            mixed_kernel,
            [struct((tok_count, width))],
            [in_vmem] * 3,
            (mix_parts[0], *mix_came[-1]),
            (0, 4 * nbytes([token_load])),
            out_specs=[pl.BlockSpec()],
        )
        router_half, router_term = call(
            functools.partial(router_grad_kernel, count),
            [struct((experts, width), f32), struct((tok_count, width), f32)],
            [in_smem] + [in_vmem] * 3,
            (info, dots, router, token_all),
            (0, count * nbytes([token_load])),
        )
        router_grad = (router_half + swap_cores(router_half)).T
        (input_grad,) = call(
            input_grad_kernel,
            [struct((tok_count, width))],
            [in_vmem] * 4,
            (back_parts[0], *back_came[-1], router_term),
            (0, 4 * nbytes([token_load])),
            out_specs=[pl.BlockSpec()],
        )
        return (mixed, input_grad, router_grad) + tuple(value[None] for value in adapters)

    return per_device


def solution(mesh):
    rows = P(("groups", "expert", "dp"), None)
    whole = P(("groups", "expert", "dp"), None, None)
    weight = P(("expert", "dp"), None, None)
    return jax.shard_map(
        make_per_device(mesh.shape["expert"]),
        mesh=mesh,
        in_specs=(rows, rows, rows, P(("groups", "expert", "dp")), P()) + (weight,) * 7,
        out_specs=(rows, rows, P("groups", None), whole, whole, whole, whole),
        check_vma=False,
    )
```

```python
import functools

import jax
import jax.numpy as jnp
import numpy as np
from jax import lax
from jax.experimental import pallas as pl
from jax.experimental.pallas import tpu as pltpu
from jax.sharding import PartitionSpec as P

MOST = 16
LANES = 128
COST_SHARE = 10**6

route_scale = 2.5
adapter_scale = 2.0

bf16, f32 = jnp.bfloat16, jnp.float32
in_vmem = pl.BlockSpec(memory_space=pltpu.VMEM)
in_hbm = pl.BlockSpec(memory_space=pltpu.HBM)
in_smem = pl.BlockSpec(memory_space=pltpu.SMEM)


def mm(left, right, axes=((1,), (0,))):
    return lax.dot_general(
        left, right, ((axes[0], axes[1]), ((), ())), preferred_element_type=jnp.float32
    )


def mm_nt(left, right):
    return mm(left, right, ((1,), (1,)))


def mm_tn(left, right):
    return mm(left, right, ((0,), (0,)))


def call(body, outs, specs, operands, cost, scratch=(), mib=8, out_specs=None):
    flops, moved = cost
    return pl.pallas_call(
        body,
        out_shape=outs,
        in_specs=specs,
        out_specs=out_specs if out_specs is not None else [in_vmem] * len(outs),
        scratch_shapes=list(scratch),
        compiler_params=pltpu.CompilerParams(vmem_limit_bytes=mib * 2**20),
        cost_estimate=pl.CostEstimate(
            flops=flops // COST_SHARE, bytes_accessed=moved // COST_SHARE, transcendentals=0
        ),
    )(*operands)


def struct(shape, dtype=bf16):
    return jax.ShapeDtypeStruct(shape, dtype)


def nbytes(arrays):
    return sum(a.size * a.dtype.itemsize for a in arrays)


def pieces(total, size):
    return [(at, min(size, total - at)) for at in range(0, total, size)]


def start_all(copies):
    for copy in copies:
        copy.start()


def token_load_kernel(
    choice_hbm, tokens_hbm, router_hbm, load_ref, choice_ref, router_ref, sems
):
    width, experts = tokens_hbm.shape[1], router_ref.shape[0]
    copies = [
        pltpu.make_async_copy(choice_hbm, choice_ref, sems.at[0]),
        pltpu.make_async_copy(tokens_hbm, load_ref.at[:, pl.ds(0, width)], sems.at[1]),
        pltpu.make_async_copy(router_hbm, router_ref, sems.at[2]),
    ]
    start_all(copies)
    copies[0].wait()
    expert = lax.broadcasted_iota(jnp.int32, (LANES, choice_ref.shape[1]), 0)
    hits = jnp.zeros(expert.shape, f32)
    for k in range(choice_ref.shape[0]):
        hits += jnp.where(choice_ref[k : k + 1] == expert, 1.0, 0.0)
    load_ref[:, width:] = hits.T.astype(bf16)
    copies[1].wait()
    copies[2].wait()
    affinity = jax.nn.sigmoid(mm_nt(load_ref[:, :width], router_ref[...]))
    high = affinity.astype(bf16)
    load_ref[:, width + experts : width + 2 * experts] = high
    load_ref[:, width + 2 * experts : width + 3 * experts] = (affinity - high.astype(f32)).astype(bf16)


def fetch_kernel(count, *refs):
    sources, outs, sems = refs[:count], refs[count : 2 * count], refs[-1]
    copies = [
        pltpu.make_async_copy(source, out, sems.at[i])
        for i, (source, out) in enumerate(zip(sources, outs))
    ]
    start_all(copies)
    for copy in copies:
        copy.wait()


def assemble(refs, all_ref):
    at = 0
    for ref in refs:
        all_ref[pl.ds(at, ref.shape[0])] = ref[...]
        at += ref.shape[0]


def expert_names(info_ref, slots):
    mine = 2 * info_ref[0] + info_ref[1]
    other = 2 * info_ref[0] + 1 - info_ref[1]
    slot = lax.broadcasted_iota(jnp.int32, (slots, LANES), 0)
    lane = lax.broadcasted_iota(jnp.int32, (slots, LANES), 1)
    return jnp.where(lane == jnp.where(slot < slots // 2, mine, other), 1.0, 0.0).astype(bf16)


def token_slots_kernel(experts, info_ref, *refs):
    blocks, (kept_ref, sent_ref, select_ref, high_ref, low_ref, all_ref) = refs[1:-6], refs[-6:]
    rows, load = blocks[0].shape
    toks, slots = all_ref.shape[0], select_ref.shape[0]
    half, width = slots // 2, load - LANES
    assemble(blocks, all_ref)
    tails = all_ref[:, width:]
    names = expert_names(info_ref, slots)
    slot = lax.broadcasted_iota(jnp.int32, (slots, toks), 0)
    tok = lax.broadcasted_iota(jnp.int32, (slots, toks), 1)
    slot = jnp.where(slot < half, slot, slot - half)
    member = jnp.where(slot // MOST == tok // rows, mm_nt(names, tails), 0.0)
    early = lax.broadcasted_iota(jnp.int32, (toks, toks), 0)
    late = lax.broadcasted_iota(jnp.int32, (toks, toks), 1)
    before = mm(member.astype(bf16), jnp.where(early < late, 1.0, 0.0).astype(bf16))
    select = jnp.where(before == (slot % MOST).astype(f32), member, 0.0)
    select_ref[...] = select.astype(bf16)
    for at, size in pieces(load, 4 * LANES):
        out = mm(select_ref[...], all_ref[:, at : at + size]).astype(bf16)
        kept_ref[:, at : at + size] = out[:half]
        sent_ref[:, at : at + size] = out[half:]
    lane = lax.broadcasted_iota(jnp.int32, (LANES, LANES), 0)
    expert = lax.broadcasted_iota(jnp.int32, (LANES, LANES), 1)
    parts = (lane == expert + experts) | (lane == expert + 2 * experts)
    affinity = mm(tails, jnp.where(parts & (expert < experts), 1.0, 0.0).astype(bf16))
    mine = lax.broadcasted_iota(jnp.int32, (toks, LANES), 1) < experts
    chosen = jnp.where(mine, tails.astype(f32) * affinity, 0.0)
    gates = route_scale * chosen / jnp.sum(chosen, axis=1, keepdims=True)
    high = gates.astype(bf16)
    low = (gates - high.astype(f32)).astype(bf16)
    high_ref[...] = (select * mm_nt(names, high)).astype(bf16)
    low_ref[...] = (select * mm_nt(names, low)).astype(bf16)


def cot_slots_kernel(high_ref, low_ref, *refs):
    blocks, (kept_ref, sent_ref, all_ref) = refs[:-3], refs[-3:]
    half, width = kept_ref.shape
    assemble(blocks, all_ref)
    for at, size in pieces(width, 4 * LANES):
        cot = all_ref[:, at : at + size]
        out = (mm(high_ref[...], cot) + mm(low_ref[...], cot)).astype(bf16)
        kept_ref[:, at : at + size] = out[:half]
        sent_ref[:, at : at + size] = out[half:]


def inner_kernel(
    count, tiles, info_ref, kept_ref, came_ref, gate_ref, up_a_ref, up_b_ref, up_hbm,
    inner_ref, slope_ref, active_ref, low_up_ref, keep_ref, rows_ref, up_ref, sems,
):
    half, width = kept_ref.shape[0], rows_ref.shape[1]
    slots, tile = 2 * half, gate_ref.shape[1] // tiles
    copy = pltpu.make_async_copy(up_hbm, up_ref, sems.at[0])
    copy.start()
    rows_ref[:half] = kept_ref[:, :width]
    rows_ref[half:] = came_ref[:, :width]
    low_up_ref[...] = mm_nt(rows_ref[...], up_a_ref[...]).astype(bf16)
    chip, core = info_ref[0], info_ref[1]
    lane = lax.broadcasted_iota(jnp.int32, (slots, LANES), 1)
    tails = jnp.concatenate([kept_ref[:, width:], came_ref[:, width:]], axis=0).astype(f32)
    valid = jnp.sum(jnp.where(lane == 2 * chip + core, tails, 0.0), axis=1, keepdims=True)
    here = lax.broadcasted_iota(jnp.int32, (slots, 1), 0)
    there = lax.broadcasted_iota(jnp.int32, (1, slots), 1)
    source_here = jnp.zeros((slots, 1), jnp.int32)
    source_there = jnp.zeros((1, slots), jnp.int32)
    for i in range(2 * count):
        source = 2 * info_ref[4 + i % count] + (core if i < count else 1 - core)
        source_here = jnp.where(here // MOST == i, source, source_here)
        source_there = jnp.where(there // MOST == i, source, source_there)
    ahead = jnp.where(source_there < source_here, 1.0, 0.0).astype(bf16)
    spread = jnp.broadcast_to(valid, (slots, LANES)).astype(bf16)
    rank = mm(ahead, spread) + (here % MOST).astype(f32)
    keep_ref[...] = jnp.where(rank < info_ref[2].astype(f32), valid, 0.0)
    for j in range(tiles):
        cols = slice(j * tile, (j + 1) * tile)
        pre_gate = mm(rows_ref[...], gate_ref[:, cols])
        logistic = jax.nn.sigmoid(pre_gate)
        active_ref[:, cols] = pre_gate * logistic
        slope_ref[:, cols] = logistic * (1.0 + pre_gate * (1.0 - logistic))
    copy.wait()
    for j in range(tiles):
        cols = slice(j * tile, (j + 1) * tile)
        pre_up = mm(rows_ref[...], up_ref[:, cols]) + adapter_scale * mm(
            low_up_ref[...], up_b_ref[:, cols]
        )
        keep = jnp.concatenate([keep_ref[...]] * (tile // LANES), axis=1)
        active = keep * active_ref[:, cols]
        active_ref[:, cols] = active
        slope_ref[:, cols] = slope_ref[:, cols] * (keep * pre_up)
        inner_ref[:, cols] = (active * pre_up).astype(bf16)


def routed_kernel(
    tiles, inner_ref, down_ref, down_a_ref, down_b_ref, kept_ref, sent_ref, low_down_ref
):
    half, tile = kept_ref.shape[0], down_ref.shape[1] // tiles
    low_down_ref[...] = mm_nt(inner_ref[...], down_a_ref[...]).astype(bf16)
    for j in range(tiles):
        cols = slice(j * tile, (j + 1) * tile)
        value = mm(inner_ref[...], down_ref[:, cols]) + adapter_scale * mm(
            low_down_ref[...], down_b_ref[:, cols]
        )
        value = value.astype(bf16)
        kept_ref[:, cols] = value[:half]
        sent_ref[:, cols] = value[half:]


def write_parts(outs, at, size, part):
    row = 0
    for ref in outs:
        ref[:, at : at + size] = part[row : row + ref.shape[0]]
        row += ref.shape[0]


def mix_parts_kernel(high_ref, low_ref, kept_ref, came_ref, *refs):
    outs, (rows_ref,) = refs[:-1], refs[-1:]
    half, width = kept_ref.shape
    rows_ref[:half] = kept_ref[...]
    rows_ref[half:] = came_ref[...]
    high = high_ref[...].astype(f32).T.astype(bf16)
    low = low_ref[...].astype(f32).T.astype(bf16)
    for at, size in pieces(width, 4 * LANES):
        rows = rows_ref[:, at : at + size]
        write_parts(outs, at, size, (mm(high, rows) + mm(low, rows)).astype(bf16))


def token_places(count, info_ref, toks):
    rows = toks // count
    here = lax.broadcasted_iota(jnp.int32, (toks, toks), 0)
    place = jnp.zeros((toks, toks), jnp.int32)
    for i in range(count):
        place = jnp.where(here // rows == i, rows * (info_ref[4 + i] - i) + here, place)
    return jnp.where(place == lax.broadcasted_iota(jnp.int32, (toks, toks), 1), 1.0, 0.0).astype(bf16)


def gate_grad_kernel(count, info_ref, select_ref, kept_ref, came_ref, all_ref, out_ref, rows_ref):
    half = kept_ref.shape[0]
    rows_ref[:half] = kept_ref[...]
    rows_ref[half:] = came_ref[...]
    dots = select_ref[...].astype(f32) * mm_nt(rows_ref[...], all_ref[...])
    own = jnp.sum(dots[:half], axis=0, keepdims=True)
    other = jnp.sum(dots[half:], axis=0, keepdims=True)
    first = info_ref[1] == 0
    row = lax.broadcasted_iota(jnp.int32, out_ref.shape[1:], 0)
    out = jnp.zeros(out_ref.shape[1:], f32)
    for i, value in enumerate((jnp.where(first, own, other), jnp.where(first, other, own))):
        high = value.astype(bf16).astype(f32)
        out = jnp.where(row == 2 * i, high, jnp.where(row == 2 * i + 1, value - high, out))
    out_ref[0] = mm(out.astype(bf16), token_places(count, info_ref, out.shape[1])).astype(bf16)


def back_parts_kernel(select_ref, kept_ref, came_ref, *refs):
    outs, (rows_ref,) = refs[:-1], refs[-1:]
    width, half = kept_ref.shape[1], kept_ref.shape[0]
    rows_ref[:half] = kept_ref[...]
    rows_ref[half:] = came_ref[...]
    select = select_ref[...].astype(f32).T.astype(bf16)
    for at, size in pieces(width, 4 * LANES):
        write_parts(outs, at, size, mm(select, rows_ref[:, at : at + size]).astype(bf16))


def inner_grad_kernel(
    tiles, kept_ref, came_ref, down_ref, down_b_ref, down_a_ref, slope_ref, active_ref,
    up_b_ref, grad_ref, gate_out_ref, up_out_ref, back_low_ref, back_up_ref,
):
    half, tile = kept_ref.shape[0], down_ref.shape[0] // tiles
    grad_ref[:half] = kept_ref[...]
    grad_ref[half:] = came_ref[...]
    back_low_ref[...] = mm_nt(grad_ref[...], down_b_ref[...]).astype(bf16)
    for j in range(tiles):
        cols = slice(j * tile, (j + 1) * tile)
        inner = mm_nt(grad_ref[...], down_ref[cols]) + adapter_scale * mm(
            back_low_ref[...], down_a_ref[:, cols]
        )
        gate_out_ref[:, cols] = (inner * slope_ref[:, cols]).astype(bf16)
        up_out_ref[:, cols] = (inner * active_ref[:, cols]).astype(bf16)
    back_up_ref[...] = mm_nt(up_out_ref[...], up_b_ref[...]).astype(bf16)


def row_grad_kernel(
    tiles, grad_gate_ref, grad_up_ref, back_up_ref, gate_ref, up_ref, up_a_ref, kept_ref, sent_ref
):
    half, tile = kept_ref.shape[0], gate_ref.shape[0] // tiles
    for j in range(tiles):
        cols = slice(j * tile, (j + 1) * tile)
        value = (
            mm_nt(grad_gate_ref[...], gate_ref[cols])
            + mm_nt(grad_up_ref[...], up_ref[cols])
            + adapter_scale * mm(back_up_ref[...], up_a_ref[:, cols])
        ).astype(bf16)
        kept_ref[:, cols] = value[:half]
        sent_ref[:, cols] = value[half:]


def adapter_kernel(
    kept_ref, came_ref, back_up_ref, low_up_ref, grad_up_ref, inner_ref, back_low_ref,
    low_down_ref, grad_ref, up_a_ref, up_b_ref, down_a_ref, down_b_ref,
):
    width, half = grad_ref.shape[1], kept_ref.shape[0]
    scaled = lambda value: (adapter_scale * value).astype(bf16)
    back_up = back_up_ref[...]
    for at, size in pieces(width, 4 * LANES):
        cols = slice(at, at + size)
        up_a_ref[:, cols] = scaled(
            mm_tn(back_up[:half], kept_ref[:, cols]) + mm_tn(back_up[half:], came_ref[:, cols])
        )
        down_b_ref[:, cols] = scaled(mm_tn(low_down_ref[...], grad_ref[:, cols]))
    up_b_ref[...] = scaled(mm_tn(low_up_ref[...], grad_up_ref[...]))
    down_a_ref[...] = scaled(mm_tn(back_low_ref[...], inner_ref[...]))


def halves_kernel(behind_ref, front_ref, top_ref, low_ref):
    rows = top_ref.shape[0]
    top_ref[...] = behind_ref[:rows]
    low_ref[...] = front_ref[rows:]


def hop_kernel(front_ref, forth_ref, rear_ref, hither_ref, front_out_ref, rear_out_ref):
    rows, came = front_ref.shape[0], forth_ref.shape[0]
    plus = lambda a, b: (a[...].astype(f32) + b[...].astype(f32)).astype(bf16)
    if came < rows:
        front_out_ref[came:] = front_ref[came:]
        rear_out_ref[: rows - came] = rear_ref[: rows - came]
    front_out_ref[:came] = plus(front_ref.at[:came], forth_ref)
    rear_out_ref[rows - came :] = plus(rear_ref.at[rows - came :], hither_ref)


def mixed_kernel(own_ref, forth_ref, hither_ref, out_ref):
    out_ref[...] = (
        own_ref[...].astype(f32) + forth_ref[...].astype(f32) + hither_ref[...].astype(f32)
    ).astype(bf16)


def input_grad_kernel(
    own_ref, forth_ref, hither_ref, term_ref, half_ref, came_ref, out_ref, router_ref
):
    router_ref[...] = half_ref[...] + came_ref[...]
    out_ref[...] = (
        own_ref[...].astype(f32)
        + forth_ref[...].astype(f32)
        + hither_ref[...].astype(f32)
        + term_ref[...]
    ).astype(bf16)


def router_grad_kernel(count, info_ref, dots_ref, router_ref, all_ref, out_ref, term_ref):
    experts, width = out_ref.shape
    rows, toks = term_ref.shape[0], all_ref.shape[0]
    tails = all_ref[:, width:].astype(f32).T
    hits = tails[:experts]
    affinity = tails[experts : 2 * experts] + tails[2 * experts : 3 * experts]
    expert = lax.broadcasted_iota(jnp.int32, (experts, toks), 0)
    grad_gates = jnp.zeros((experts, toks), f32)
    gathered = jnp.concatenate([dots_ref[i] for i in range(count)], axis=0)
    gathered = mm_nt(gathered, token_places(count, info_ref, toks))
    for i in range(count):
        far = sum(count >> (bit + 1) for bit in range(count.bit_length()) if i >> bit & 1)
        name = 2 * (info_ref[0] ^ far)
        dots = gathered[i * dots_ref.shape[1] : (i + 1) * dots_ref.shape[1]]
        grad_gates = jnp.where(expert == name, dots[0:1] + dots[1:2], grad_gates)
        grad_gates = jnp.where(expert == name + 1, dots[2:3] + dots[3:4], grad_gates)
    chosen = hits * affinity
    chosen_sum = jnp.sum(chosen, axis=0, keepdims=True)
    grad_chosen = route_scale * (
        grad_gates / chosen_sum
        - jnp.sum(grad_gates * chosen, axis=0, keepdims=True) / (chosen_sum * chosen_sum)
    )
    logits = (hits * grad_chosen * affinity * (1.0 - affinity)).astype(bf16)
    out_ref[...] = mm(logits, all_ref[:, :width])
    term_ref[...] = mm_tn(logits[:, :rows], router_ref[...])


def ring_of(count):
    if count == 8:
        order = [0, 2, 4, 6, 7, 5, 3, 1]
    else:
        order = list(range(count))
    ahead = [(order[i], order[(i + 1) % count]) for i in range(count)]
    back = [(b, a) for a, b in ahead]
    return order, ahead, back


def offsets_of(count):
    half = count // 2
    return [0] + [-k for k in range(1, half)] + list(range(1, half)) + [half]


def tie(*values):
    return lax.optimization_barrier(values)


class Ring:
    def __init__(self, count, far_ahead):
        _, ahead, back = ring_of(count)
        self.half = count // 2
        self.far, self.near = (ahead, back) if far_ahead else (back, ahead)
        self.far_ahead = far_ahead

    def gather_hop(self, far, near):
        far.append(lax.ppermute(far[-1], "expert", self.far))
        if len(near) < self.half:
            near.append(lax.ppermute(near[-1], "expert", self.near))

    def last_hop(self, far, near):
        ahead, back = (self.far, self.near) if self.far_ahead else (self.near, self.far)
        behind, front = (far, near) if self.far_ahead else (near, far)
        rows, columns = far[-1].shape
        top, low = call(
            halves_kernel, [struct((rows // 2, columns))] * 2, [in_vmem] * 2,
            (behind[-1], front[-1]), (0, nbytes([far[-1]])),
        )
        return lax.ppermute(top, "expert", ahead), lax.ppermute(low, "expert", back)

    def gathered(self, far, near, *opposite):
        behind, front = (far, near) if self.far_ahead else (near, far)
        return behind[: self.half] + front[1 : self.half] + list(opposite or [far[self.half]])


def scatter_hop(parts, count, came, step):
    _, ahead, back = ring_of(count)
    half = count // 2
    if step == 0:
        front, rear = parts[-2], parts[-1]
    else:
        front, rear = parts[count - 1 - step], parts[half - step]
        front, rear = call(
            hop_kernel, [struct(front.shape)] * 2, [in_vmem] * 4,
            (front, came[0], rear, came[1]), (0, 3 * nbytes([front, rear])),
        )
    return lax.ppermute(front, "expert", ahead), lax.ppermute(rear, "expert", back)


def double(gathered, step):
    size = lax.axis_size("expert")
    came = lax.ppermute(gathered, "expert", [(i, i ^ step) for i in range(size)])
    return jnp.concatenate([gathered, came], axis=0)


def swap_cores(value):
    return lax.ppermute(value, "dp", [(0, 1), (1, 0)])


def make_per_device(count):
    order, _, _ = ring_of(count)
    offsets = offsets_of(count)
    place = [order.index(chip) for chip in range(count)]
    table = np.array(
        [[order[(place[c] + off) % count] for off in offsets] for c in range(count)], np.int32
    )

    def per_device(
        tokens,
        cotangent,
        expert_choice_index,
        capacity,
        router_matrix,
        gate_matrix,
        up_matrix,
        down_matrix,
        up_adapter_first,
        up_adapter_second,
        down_adapter_first,
        down_adapter_second,
    ):
        tok_count, width = tokens.shape
        experts = router_matrix.shape[1]
        load = width + LANES
        half = count * MOST
        slots = 2 * half
        chip, core = lax.axis_index("expert"), lax.axis_index("dp")
        chips = jnp.sum(
            jnp.where(jnp.arange(count)[:, None] == chip, jnp.asarray(table), 0), axis=0
        )
        info = jnp.concatenate([jnp.stack([chip, core, capacity[0]]), chips[:1], chips])
        info = info.astype(jnp.int32)
        gate_w, up_w, down_w = gate_matrix[0], up_matrix[0], down_matrix[0]
        up_a, up_b = up_adapter_first[0], up_adapter_second[0]
        down_a, down_b = down_adapter_first[0], down_adapter_second[0]
        hidden, rank = gate_w.shape[1], up_a.shape[1]

        toks = count * tok_count
        tiles = 4
        up_a, down_a, router = up_a.T, down_a.T, router_matrix.T
        choice = expert_choice_index.T
        ring_token, ring_cot = Ring(count, True), Ring(count, False)
        hops = count // 2
        rows_of = [tok_count] * (count - 1) + [tok_count // 2] * 2

        stay = lambda *arrays: [pltpu.with_memory_space_constraint(a, pltpu.HBM) for a in arrays]

        def fetch(*arrays):
            return call(
                functools.partial(fetch_kernel, len(arrays)),
                [pltpu.VMEM(a.shape, bf16) for a in arrays],
                [in_hbm] * len(arrays),
                stay(*arrays),
                (0, nbytes(arrays)),
                scratch=[pltpu.SemaphoreType.DMA((len(arrays),))],
                mib=1,
            )

        (token_load,) = call(
            token_load_kernel, [struct((tok_count, load))], [in_hbm] * 3,
            stay(choice, tokens, router), (0, 2 * nbytes([tokens])),
            scratch=[
                pltpu.VMEM(choice.shape, jnp.int32), pltpu.VMEM(router.shape, bf16),
                pltpu.SemaphoreType.DMA((3,)),
            ],
        )

        tok_far, tok_near = [token_load], [token_load]
        ring_token.gather_hop(tok_far, tok_near)
        cot_far, cot_near = [cotangent], [cotangent]
        tok_near[-1], info = tie(tok_near[-1], info)
        ring_token.gather_hop(tok_far, tok_near)
        ring_cot.gather_hop(cot_far, cot_near)
        for hop in range(2, hops):
            ring_token.gather_hop(tok_far, tok_near)
            if hop == hops - 2:
                tok_far[-1], cot_near[1] = tie(tok_far[-1], cot_near[1])
                tok_near[-1], gate_late = tie(tok_near[-1], gate_w)
            if hop < hops - 1:
                ring_cot.gather_hop(cot_far, cot_near)
        gate_v, up_a_v, up_b_v = fetch(gate_late, up_a, up_b)
        token_blocks = ring_token.gathered(tok_far, tok_near)

        kept, sent, select, high, low, token_all = call(
            functools.partial(token_slots_kernel, experts),
            [struct((half, load))] * 2 + [struct((slots, toks))] * 3 + [struct((toks, load))],
            [in_smem] + [in_vmem] * (count + 1),
            (info, gate_v, *token_blocks),
            (2 * slots * toks * load, 2 * count * nbytes([token_load])),
        )
        sent, cot_far[-1], cot_near[-1] = tie(sent, cot_far[-1], cot_near[-1])
        came = swap_cores(sent)
        ring_cot.gather_hop(cot_far, cot_near)
        inner, slope, active, low_up = call(
            functools.partial(inner_kernel, count, tiles),
            [
                struct((slots, hidden)), struct((slots, hidden), f32), struct((slots, hidden), f32),
                struct((slots, rank)),
            ],
            [in_smem] + [in_vmem] * 5 + [in_hbm],
            (info, kept, came, gate_v, up_a_v, up_b_v, *stay(up_w)),
            (4 * slots * width * hidden, 2 * nbytes([gate_w])),
            scratch=[
                pltpu.VMEM((slots, LANES), f32), pltpu.VMEM((slots, width), bf16),
                pltpu.VMEM(up_w.shape, bf16),
                pltpu.SemaphoreType.DMA((1,)),
            ],
            mib=16,
        )
        inner, cot_far[-1], cot_near[-1] = tie(inner, cot_far[-1], cot_near[-1])
        cot_top, cot_low = ring_cot.last_hop(cot_far, cot_near)
        routed_kept, routed_sent, low_down = call(
            functools.partial(routed_kernel, width // (4 * LANES)),
            [struct((half, width))] * 2 + [struct((slots, rank))],
            [in_vmem] * 4,
            (inner, down_w, down_a, down_b),
            (2 * slots * width * hidden, nbytes([gate_w])),
        )
        routed_sent, high, cot_top, cot_low = tie(routed_sent, high, cot_top, cot_low)
        routed_came = swap_cores(routed_sent)
        cot_blocks = ring_cot.gathered(cot_far, cot_near, cot_top, cot_low)
        cot_kept, cot_sent, cot_all = call(
            cot_slots_kernel,
            [struct((half, width))] * 2 + [struct((toks, width))],
            [in_vmem] * (count + 3),
            (high, low, *cot_blocks),
            (4 * slots * toks * load, 2 * count * nbytes([token_load])),
        )
        cot_came = swap_cores(cot_sent)
        routed_came, cot_kept = tie(routed_came, cot_kept)

        mix_parts = call(
            mix_parts_kernel,
            [struct((rows, width)) for rows in rows_of],
            [in_vmem] * 4,
            (high, low, routed_kept, routed_came),
            (4 * slots * toks * load, 3 * count * nbytes([token_load])),
            scratch=[pltpu.VMEM((slots, width), bf16)],
        )
        mix_parts = list(mix_parts)
        cot_came, mix_parts[-1] = tie(cot_came, mix_parts[-1])
        mix_came = [scatter_hop(mix_parts, count, None, 0)]

        grad_routed, grad_gate, grad_up, back_low, back_up = call(
            functools.partial(inner_grad_kernel, tiles),
            [struct((slots, width))] + [struct((slots, hidden))] * 2 + [struct((slots, rank))] * 2,
            [in_vmem] * 8,
            (cot_kept, cot_came, down_w, down_b, down_a, slope, active, up_b_v),
            (2 * slots * width * hidden, nbytes([gate_w])),
        )
        grad_up, *mix_came[0] = tie(grad_up, *mix_came[0])
        mix_came.append(scatter_hop(mix_parts, count, mix_came[0], 1))
        back_kept, back_sent = call(
            functools.partial(row_grad_kernel, width // (4 * LANES)),
            [struct((half, width))] * 2,
            [in_vmem] * 6,
            (grad_gate, grad_up, back_up, gate_v, up_w, up_a_v),
            (4 * slots * width * hidden, 2 * nbytes([gate_w])),
        )
        routed_came, back_kept = tie(routed_came, back_kept)
        (dots,) = call(
            functools.partial(gate_grad_kernel, count),
            [struct((1, 2 * 8, toks))],
            [in_smem] + [in_vmem] * 4,
            (info, select, routed_kept, routed_came, cot_all),
            (2 * slots * toks * load, 2 * count * nbytes([token_load])),
            scratch=[pltpu.VMEM((slots, width), bf16)],
        )
        back_sent, dots, *mix_came[1] = tie(back_sent, dots, *mix_came[1])
        back_came = swap_cores(back_sent)
        mix_came.append(scatter_hop(mix_parts, count, mix_came[1], 2))
        back_parts = call(
            back_parts_kernel,
            [struct((rows, width)) for rows in rows_of],
            [in_vmem] * 3,
            (select, back_kept, back_came),
            (2 * slots * toks * load, 2 * count * nbytes([token_load])),
            scratch=[pltpu.VMEM((slots, width), bf16)],
        )
        back_parts = list(back_parts)
        back_came = [scatter_hop(back_parts, count, None, 0)]
        dots, step = double(dots, count // 2), count // 4
        back_up_late = back_up
        *back_came[0], mix2_far, mix2_near = tie(*back_came[0], *mix_came[2])
        mix_came[2] = (mix2_far, mix2_near)
        for hop in range(1, hops):
            if hop + 2 < hops:
                mix_came.append(scatter_hop(mix_parts, count, mix_came[-1], hop + 2))
            if hop == hops - 1:
                tied = tie(*back_came[-1], back_up_late, dots)
            else:
                tied = tie(*back_came[-1], back_up_late, dots)
            back_came[-1], back_up_late, dots = tied[:2], tied[2], tied[3]
            if hop == 1:
                adapters = call(
                    adapter_kernel,
                    [
                        struct((rank, width)), struct((rank, hidden)),
                        struct((rank, hidden)), struct((rank, width)),
                    ],
                    [in_vmem] * 9,
                    (kept, came, back_up_late, low_up, grad_up, inner, back_low, low_down,
                     grad_routed),
                    (8 * slots * width * rank, 4 * nbytes([grad_routed])),
                    out_specs=[pl.BlockSpec()] * 4,
                )
                adapters = list(adapters)
            if hop == 2:
                *back_came[-1], adapters[1] = tie(*back_came[-1], adapters[1])
            back_came.append(scatter_hop(back_parts, count, back_came[-1], hop))
            if step > 0:
                dots = double(dots, step)
                step //= 2
        while step > 0:
            dots = double(dots, step)
            step //= 2
        adapters = (adapters[0].T, adapters[1], adapters[2].T, adapters[3])

        (mixed,) = call(
            mixed_kernel,
            [struct((tok_count, width))],
            [in_vmem] * 3,
            (mix_parts[0], *mix_came[-1]),
            (0, 4 * nbytes([token_load])),
            out_specs=[pl.BlockSpec()],
        )
        router_half, router_term = call(
            functools.partial(router_grad_kernel, count),
            [struct((experts, width), f32), struct((tok_count, width), f32)],
            [in_smem] + [in_vmem] * 3,
            (info, dots, router, token_all),
            (0, count * nbytes([token_load])),
        )
        input_grad, router_grad = call(
            input_grad_kernel,
            [struct((tok_count, width)), struct((experts, width), f32)],
            [in_vmem] * 6,
            (back_parts[0], *back_came[-1], router_term, router_half, swap_cores(router_half)),
            (0, 4 * nbytes([token_load])),
            out_specs=[pl.BlockSpec()] * 2,
        )
        router_grad = router_grad.T
        return (mixed, input_grad, router_grad) + tuple(value[None] for value in adapters)

    return per_device


def solution(mesh):
    rows = P(("groups", "expert", "dp"), None)
    whole = P(("groups", "expert", "dp"), None, None)
    weight = P(("expert", "dp"), None, None)
    return jax.shard_map(
        make_per_device(mesh.shape["expert"]),
        mesh=mesh,
        in_specs=(rows, rows, rows, P(("groups", "expert", "dp")), P()) + (weight,) * 7,
        out_specs=(rows, rows, P("groups", None), whole, whole, whole, whole),
        check_vma=False,
    )
```
